32 devices in a mesh: rows: 8 (over z, x), vecs: 4 (over y, core).
Axes of the slice: x: 2, y: 2, z: 4, core: 2. Of those that a mesh axis runs over, the one named last changes fastest.
Arguments:
- hamiltonian: float32 [256, 6, 128, 128], P('rows'), may hold values from -0.10825317 to 0.10825317
- columns: int32 [256, 6], P('rows'), may hold values from 0 to 255, as said below
- vectors: float32 [32768, 1024], P('rows', 'vecs'), may hold values from -6 to 6
- coefficients: float32 [7], replicated, may hold values from -1 to 1
Outputs:
- filtered: float32 [32768, 1024], P('rows', 'vecs')
- gram: float32 [1024, 1024], P('vecs', 'rows')
The draws below stay inside these ranges and needn't reach their ends.
Inputs may be any that keep to these rules, and one draw needn't show every extreme that they name: The blocks of a block row have distinct columns; block row r has blocks in columns (r - 4) mod 256 and (r + 4) mod 256, and all its others within distance 4 - 1 of r, taken modulo 256.
All inputs are finite; a program needn't handle non-finite values.
Results may differ from the reference program's by a relative error of at most 0.0001.
Values sent between devices are 32-bit elements; how exact they have to be, the bound alone decides.
No kernel may reach another device: no remote copies, remote signals or barrier semaphores. Data moves between devices by JAX's collectives and lax.ppermute only.
A program may use at most 128 MiB of HBM per device.

```python
import jax
import jax.numpy as jnp
from jax import lax

BLOCK = 128
NV = 1024
PER_ROW = 6
REACH = 4
ORDER = 6
NBLK = 256
NROWS = 32768


def draw_columns(key, part):
    row_ids = jnp.arange(NBLK, dtype=jnp.int32)
    row_keys = jax.random.split(jax.random.fold_in(key, 7), NBLK)
    orders = jax.vmap(lambda sub: jax.random.permutation(sub, 2 * REACH - 1))(row_keys)
    inner = orders[:, :PER_ROW - 2].astype(jnp.int32) - (REACH - 1)
    ends = jnp.broadcast_to(jnp.array([-REACH, REACH], dtype=jnp.int32), (NBLK, 2))
    offsets = jnp.concatenate([ends, inner], axis=1)
    return ((row_ids[:, None] + offsets) % NBLK).astype(jnp.int32)


def shard_levels(key, dims, cuts, smallest, largest):
    factor_of, own = 1.0, jax.random.fold_in(key, 6)
    for dim, shards_of in cuts:
        heights = jnp.exp(jax.random.uniform(jax.random.fold_in(own, dim), (shards_of,), jnp.float32, smallest / len(cuts), largest / len(cuts)))
        factor_of = factor_of * jnp.repeat(heights, dims[dim] // shards_of).reshape([-1 if axis == dim else 1 for axis in range(len(dims))])
    return factor_of


def noise(stream_key, shape, spread, most, cuts=(), kind=jnp.bfloat16):
    values = spread * jax.random.normal(stream_key, shape, jnp.float32)
    if cuts:
        values = values * shard_levels(stream_key, shape, cuts, -0.22, 0.18)
    return jnp.clip(values, -most, most).astype(kind)


def setup_inputs(seed: int = 0) -> dict:
    seeds = jax.random.split(jax.random.key(seed), 5)
    return {
        "hamiltonian": noise(seeds[0], (NBLK, PER_ROW, BLOCK, BLOCK), (1.0 / (4 * PER_ROW * BLOCK) ** 0.5), 0.10825317, ((0, 8),), jnp.float32),
        "columns": draw_columns(jax.random.fold_in(seeds[4], 71), 0),
        "vectors": noise(seeds[2], (NROWS, NV), 1.0, 6.0, ((0, 8), (1, 4)), jnp.float32),
        "coefficients": jnp.clip(jax.random.uniform(seeds[3], (ORDER + 1,), jnp.float32, -1.0, 1.0), -1.0, 1.0),
    }


def product(vectors, hamiltonian, columns):
    blocks = vectors.reshape(NBLK, BLOCK, NV)

    def one_row(pair):
        h_rows, col_ids = pair
        return jnp.einsum("kab,kbv->av", h_rows, blocks[col_ids], precision=lax.Precision.HIGHEST)

    return lax.map(one_row, (hamiltonian, columns)).reshape(NROWS, NV)


def reference(hamiltonian, columns, vectors, coefficients):
    previous = vectors
    current = product(vectors, hamiltonian, columns)
    filtered = coefficients[0] * previous + coefficients[1] * current
    for order_step in range(2, ORDER + 1):
        following = 2.0 * product(current, hamiltonian, columns) - previous
        filtered = filtered + coefficients[order_step] * following
        previous, current = current, following
    gram = jnp.dot(filtered.T, filtered, precision=lax.Precision.HIGHEST, preferred_element_type=jnp.float32) / NROWS
    return filtered, gram
```

```python
import functools

import jax
import jax.numpy as jnp
from jax import lax
from jax.experimental import pallas as pl
from jax.experimental.pallas import tpu as pltpu
from jax.sharding import PartitionSpec as P

BLOCK = 128
REACH = 4
ORDER = 6
LANES = 128
VMEM_BYTES = 32 * 1024 * 1024
F32 = jnp.float32
BF16 = jnp.bfloat16


def params():
    return pltpu.CompilerParams(vmem_limit_bytes=VMEM_BYTES)


def two_parts(x):
    high = x.astype(BF16)
    low = (x - high.astype(F32)).astype(BF16)
    return high, low


def split_kernel(h_ref, out_ref):
    for k in range(h_ref.shape[1]):
        high, low = two_parts(h_ref[0, k])
        out_ref[0, :BLOCK, k * BLOCK : (k + 1) * BLOCK] = high
        out_ref[0, BLOCK:, k * BLOCK : (k + 1) * BLOCK] = low


def split_hamiltonian(hamiltonian):
    rows, per_row = hamiltonian.shape[:2]
    return pl.pallas_call(
        split_kernel,
        grid=(rows,),
        in_specs=[pl.BlockSpec((1, per_row, BLOCK, BLOCK), lambda g: (g, 0, 0, 0))],
        out_specs=pl.BlockSpec((1, 2 * BLOCK, per_row * BLOCK), lambda g: (g, 0, 0)),
        out_shape=jax.ShapeDtypeStruct((rows, 2 * BLOCK, per_row * BLOCK), BF16),
        compiler_params=params(),
        name="split_hamiltonian",
    )(hamiltonian)


def put_parts(parts_ref, start, value):
    high, low = two_parts(value)
    rows = value.shape[0]
    parts_ref[pl.ds(start, rows), :LANES] = high
    parts_ref[pl.ds(start, rows), LANES:] = low


def strip_product(slots_ref, h_ref, parts_ref, strip, base):
    per_row = h_ref.shape[2] // BLOCK
    out = []
    for r in range(REACH):
        picked = []
        for k in range(per_row):
            slot = slots_ref[(strip * REACH + r) * per_row + k] + base
            start = pl.multiple_of(slot * BLOCK, BLOCK)
            picked.append(parts_ref[pl.ds(start, BLOCK), :])
        both = jnp.dot(h_ref[r], jnp.concatenate(picked, axis=0), preferred_element_type=F32)
        top, bottom = both[:BLOCK], both[BLOCK:]
        small = (top[:, LANES:] + bottom[:, :LANES]) + bottom[:, LANES:]
        out.append(top[:, :LANES] + small)
    return out


def interior_kernel(pieces, has_q, slots_ref, scale_ref, h_ref, v_ref, *rest):
    piece_refs, rest = rest[:pieces], rest[pieces:]
    q_ref = rest[0] if has_q else None
    out_ref, parts_ref = rest[-2:]
    step = pl.program_id(0)

    @pl.when(step == 0)
    def _():
        start = 0
        for ref in piece_refs:
            for at in range(0, ref.shape[0], BLOCK):
                put_parts(parts_ref, start, ref[at : at + BLOCK])
                start += BLOCK

    sums = strip_product(slots_ref, h_ref, parts_ref, step + 1, step * REACH)
    for r, total in enumerate(sums):
        rows = slice(r * BLOCK, (r + 1) * BLOCK)
        value = scale_ref[0] * v_ref[rows] + scale_ref[1] * total
        if has_q:
            value = value - q_ref[rows]
        out_ref[rows] = value


def border_kernel(has_q, slots_ref, scale_ref, h_ref, v_ref, *rest):
    strips, rest = rest[:6], rest[6:]
    q_refs = rest[:2] if has_q else None
    outs, parts_ref = rest[-3:-1], rest[-1]
    step = pl.program_id(0)
    last = pl.num_programs(0) - 1
    size = REACH * BLOCK
    for side in range(2):

        @pl.when(step == side * last)
        def _(side=side):
            for n in range(3):
                ref = strips[3 * side + n]
                for at in range(0, size, BLOCK):
                    put_parts(parts_ref, n * size + at, ref[at : at + BLOCK])
            strip = 0 if side == 0 else slots_ref.shape[0] // (REACH * (h_ref.shape[2] // BLOCK)) - 1
            sums = strip_product(slots_ref, h_ref, parts_ref, strip, 0)
            for r, total in enumerate(sums):
                rows = slice(r * BLOCK, (r + 1) * BLOCK)
                value = scale_ref[0] * v_ref[rows] + scale_ref[1] * total
                if has_q:
                    value = value - q_refs[side][rows]
                outs[side][rows] = value


def fixed(shape, index):
    return pl.BlockSpec(shape, lambda g, *_: index)


def interior(slots, scale, parts_h, vectors, chunk, pieces, q):
    strips = parts_h.shape[0] // REACH
    size = REACH * BLOCK
    specs = [
        pl.BlockSpec(memory_space=pltpu.SMEM),
        pl.BlockSpec((REACH, *parts_h.shape[1:]), lambda g, *_: (g + 1, 0, 0)),
        pl.BlockSpec((size, LANES), lambda g, *_: (g + 1, chunk)),
    ]
    args = [scale, parts_h, vectors]
    for array, column in pieces:
        specs.append(fixed((array.shape[0], LANES), (0, column)))
        args.append(array)
    if q is not None:
        specs.append(pl.BlockSpec((size, LANES), lambda g, *_: (g, 0)))
        args.append(q)
    inner = strips - 2
    return pl.pallas_call(
        functools.partial(interior_kernel, len(pieces), q is not None),
        grid_spec=pltpu.PrefetchScalarGridSpec(
            num_scalar_prefetch=1,
            grid=(inner,),
            in_specs=specs,
            out_specs=pl.BlockSpec((size, LANES), lambda g, *_: (g, 0)),
            scratch_shapes=[pltpu.VMEM((strips * size, 2 * LANES), BF16)],
        ),
        out_shape=jax.ShapeDtypeStruct((inner * size, LANES), F32),
        compiler_params=params(),
        cost_estimate=pl.CostEstimate(
            flops=8 * inner * size * LANES * parts_h.shape[2],
            bytes_accessed=2 * parts_h.size + 4 * 5 * inner * size * LANES,
            transcendentals=0,
        ),
        name="interior",
    )(slots, *args)


def border(slots, scale, parts_h, vectors, chunk, strips_in, q):
    strips = parts_h.shape[0] // REACH
    size = REACH * BLOCK
    specs = [
        pl.BlockSpec(memory_space=pltpu.SMEM),
        pl.BlockSpec((REACH, *parts_h.shape[1:]), lambda g, *_: (g * (strips - 1), 0, 0)),
        pl.BlockSpec((size, LANES), lambda g, *_: (g * (strips - 1), chunk)),
    ]
    args = [scale, parts_h, vectors]
    for array, row, column in strips_in:
        specs.append(fixed((size, LANES), (row, column)))
        args.append(array)
    if q is not None:
        specs += [fixed((size, LANES), (0, 0))] * 2
        args += list(q)
    return pl.pallas_call(
        functools.partial(border_kernel, q is not None),
        grid_spec=pltpu.PrefetchScalarGridSpec(
            num_scalar_prefetch=1,
            grid=(2,),
            in_specs=specs,
            out_specs=[fixed((size, LANES), (0, 0))] * 2,
            scratch_shapes=[pltpu.VMEM((3 * size, 2 * LANES), BF16)],
        ),
        out_shape=[jax.ShapeDtypeStruct((size, LANES), F32)] * 2,
        compiler_params=params(),
        cost_estimate=pl.CostEstimate(
            flops=16 * size * LANES * parts_h.shape[2],
            bytes_accessed=2 * parts_h.size // strips * 2 + 4 * 12 * size * LANES,
            transcendentals=0,
        ),
        name="border",
    )(slots, *args)


def gram_kernel(chunks, own_parts, peers, half, has_before, bits_ref, *rest):
    own_refs, rest = rest[: chunks * own_parts], rest[chunks * own_parts :]
    got_refs, rest = rest[: chunks * (peers - 1)], rest[chunks * (peers - 1) :]
    before_ref = rest[0] if has_before else None
    out_ref = rest[-1]
    step = pl.program_id(0)

    @pl.when(step == 0)
    def _():
        out_ref[...] = before_ref[...] if has_before else jnp.zeros_like(out_ref)

    def joined(refs):
        return two_parts(jnp.concatenate([r[...] for r in refs], axis=1))

    own = []
    for c in range(chunks):
        mine = own_refs[c * own_parts : (c + 1) * own_parts]
        own.append(mine[0][...] if own_parts == 1 else jnp.where(step == 0, mine[0][...], mine[1][...]))
    own = jnp.concatenate(own, axis=1)
    high, low = two_parts(own.T)

    def products(other_high, other_low):
        total = jnp.dot(high, other_low, preferred_element_type=F32)
        total += jnp.dot(low, other_high, preferred_element_type=F32)
        return total + jnp.dot(high, other_high, preferred_element_type=F32)

    out_ref[0] += 0.5 * products(*two_parts(own))
    for d in range(1, peers):

        @pl.when(step // half == bits_ref[d.bit_length() - 1])
        def _(d=d):
            out_ref[d] += products(*joined(got_refs[chunks * (d - 1) : chunks * d]))


def gram_sums(bits, own, got, before):
    size = REACH * BLOCK
    chunks, own_parts, peers = len(own), len(own[0]), len(got) + 1
    half = got[0][0].shape[0] // size
    width = chunks * LANES
    specs, args = [], []
    for arrays in own:
        for array in arrays:
            specs.append(pl.BlockSpec((size, LANES), (lambda g, *_: (g, 0)) if own_parts == 1 else (lambda g, *_: (0, 0))))
            args.append(array)
    for arrays in got:
        for array in arrays:
            specs.append(pl.BlockSpec((size, LANES), lambda g, *_: (lax.rem(g, half), 0)))
            args.append(array)
    if before is not None:
        specs.append(fixed(before.shape, (0, 0, 0)))
        args.append(before)
    return pl.pallas_call(
        functools.partial(gram_kernel, chunks, own_parts, peers, half, before is not None),
        grid_spec=pltpu.PrefetchScalarGridSpec(
            num_scalar_prefetch=1,
            grid=(2 * half,),
            in_specs=specs,
            out_specs=fixed((peers, width, width), (0, 0, 0)),
        ),
        out_shape=jax.ShapeDtypeStruct((peers, width, width), F32),
        compiler_params=params(),
        cost_estimate=pl.CostEstimate(
            flops=6 * half * size * width * width * (peers + 1),
            bytes_accessed=4 * (peers + 1) * half * size * width,
            transcendentals=0,
        ),
        name="gram_sums",
    )(bits, *args)


def on_device(hamiltonian, columns, vectors, coefficients):
    block_rows, per_row = columns.shape
    peers = lax.axis_size("rows")
    groups = lax.axis_size("vecs")
    total_blocks = block_rows * peers
    width = vectors.shape[1]
    chunks = width // LANES
    size = REACH * BLOCK
    strips = block_rows // REACH
    rows_at, vecs_at = lax.axis_index("rows"), lax.axis_index("vecs")
    up = [(i, (i + 1) % peers) for i in range(peers)]
    down = [(j, i) for i, j in up]

    def exchange(first, last):
        return lax.ppermute(last, "rows", up), lax.ppermute(first, "rows", down)

    lanes = [slice(c * LANES, (c + 1) * LANES) for c in range(chunks)]
    halo = [exchange(vectors[:size, l], vectors[-size:, l]) for l in lanes]

    local = jnp.arange(block_rows, dtype=jnp.int32)
    offsets = (columns - (rows_at * block_rows + local)[:, None] + REACH) % total_blocks
    slots = (offsets + (local % REACH)[:, None]).reshape(-1)
    parts_h = split_hamiltonian(hamiltonian)

    scales = []
    for step in range(1, ORDER + 1):
        here = coefficients[ORDER - step]
        if step == 2:
            here = here - coefficients[ORDER]
        by = 2.0 * coefficients[ORDER] if step == 1 else (jnp.float32(1.0) if step == ORDER else jnp.float32(2.0))
        scales.append(jnp.stack([here, by]))

    older = [None] * chunks
    terms = [None] * chunks
    inner = [interior(slots, scales[0], parts_h, vectors, c, [(vectors, c)], None) for c in range(chunks)]
    for step in range(1, ORDER + 1):
        for c in range(chunks):
            before, after = halo[c]
            if step == 1:
                edge = [(vectors, 0, c), (vectors, 1, c), (vectors, strips - 2, c), (vectors, strips - 1, c)]
            else:
                low, mid, high = terms[c]
                edge = [(low, 0, 0), (mid, 0, 0), (mid, strips - 3, 0), (high, 0, 0)]
            q = older[c]
            pieces = [(before, 0, 0), *edge, (after, 0, 0)]
            low, high = border(slots, scales[step - 1], parts_h, vectors, c, pieces, q and (q[0], q[2]))
            previous, terms[c] = terms[c], (low, inner[c], high)
            if step < ORDER:
                halo[c] = exchange(low, high)
                next_q = previous and previous[1]
                inner[c] = interior(slots, scales[step], parts_h, vectors, c, [(a, 0) for a in terms[c]], next_q)
            older[c] = previous

    filtered = jnp.concatenate(
        [jnp.concatenate([t[n] for t in terms], axis=1) for n in range(3)], axis=0
    )

    bit_count = (groups - 1).bit_length()
    bits = jnp.stack([(vecs_at >> b) & 1 for b in range(bit_count)]).astype(jnp.int32)

    def swapped(x, distance):
        return lax.ppermute(x, "vecs", [(i, i ^ distance) for i in range(groups)])

    def received(halves_of):
        got = [None] * groups
        for d in range(1, groups):
            if d == 1 or d % 2 == 0:
                bit = bits[d.bit_length() - 1]
                got[d] = [swapped(halves_of(c, bit), d) for c in range(chunks)]
            else:
                got[d] = [swapped(x, 1) for x in got[d - 1]]
        return got[1:]

    half_inner = (strips - 2) * size // 2

    def inner_half(c, bit):
        return lax.dynamic_slice_in_dim(terms[c][1], (1 - bit) * half_inner, half_inner, axis=0)

    def outer_half(c, bit):
        return jnp.where(bit == 0, terms[c][2], terms[c][0])

    sums = gram_sums(bits, [[t[1]] for t in terms], received(inner_half), None)
    sums = gram_sums(bits, [[t[0], t[2]] for t in terms], received(outer_half), sums)

    per_group = peers // groups
    piece = width // per_group
    share = sums.reshape(groups, width, per_group, piece).transpose(0, 2, 1, 3).reshape(groups * per_group, width, piece)
    wanted = rows_at ^ (vecs_at * per_group)
    distance = 1
    while distance < peers:
        share = share.reshape(-1, 2, width, piece)
        mine = (wanted // distance) & 1
        keep = lax.dynamic_index_in_dim(share, mine, axis=1, keepdims=False)
        send = lax.dynamic_index_in_dim(share, 1 - mine, axis=1, keepdims=False)
        share = keep + lax.ppermute(send, "rows", [(i, i ^ distance) for i in range(peers)])
        distance *= 2
    share = share.reshape(per_group, piece, piece)
    turned = [None] * per_group
    for n in range(per_group):
        tile = (rows_at + n) % per_group
        pairs = []
        for i in range(peers):
            for g in range(groups):
                to = (g * per_group + (i + n) % per_group) * groups + i // per_group
                pairs.append((i * groups + g, to))
        sent = lax.dynamic_index_in_dim(share, tile, axis=0, keepdims=False)
        turned[n] = lax.ppermute(sent, ("rows", "vecs"), pairs).T
    gram = []
    for t in range(per_group):
        which = (rows_at - t) % per_group
        gram.append(share[t] + lax.dynamic_index_in_dim(jnp.stack(turned), which, axis=0, keepdims=False))
    gram = jnp.concatenate(gram, axis=0) / (total_blocks * BLOCK)
    return filtered, gram


def solution(mesh):
    return jax.shard_map(
        on_device,
        mesh=mesh,
        in_specs=(P("rows", None, None, None), P("rows", None), P("rows", "vecs"), P()),
        out_specs=(P("rows", "vecs"), P("vecs", "rows")),
        check_vma=False,
    )
```

```python
import functools

import jax
import jax.numpy as jnp
from jax import lax
from jax.experimental import pallas as pl
from jax.experimental.pallas import tpu as pltpu
from jax.sharding import PartitionSpec as P

BLOCK = 128
REACH = 4
ORDER = 6
LANES = 128
SIZE = REACH * BLOCK
F32 = jnp.float32
BF16 = jnp.bfloat16
WHOLE = pl.BlockSpec(memory_space=pltpu.VMEM)
ANYWHERE = pl.BlockSpec(memory_space=pl.ANY)
SCALARS = pl.BlockSpec(memory_space=pltpu.SMEM)


def params(mib):
    return pltpu.CompilerParams(vmem_limit_bytes=mib * 1024 * 1024)


def cost(flops, moved):
    return pl.CostEstimate(flops=flops, bytes_accessed=moved, transcendentals=0)


def two_parts(x):
    high = x.astype(BF16)
    low = (x - high.astype(F32)).astype(BF16)
    return high, low


def put_parts(ref, start, value):
    high, low = two_parts(value)
    ref[pl.ds(start, value.shape[0]), :LANES] = high
    ref[pl.ds(start, value.shape[0]), LANES:] = low


def split_kernel(h_ref, out_ref):
    for r in range(h_ref.shape[0]):
        for k in range(h_ref.shape[1]):
            high, low = two_parts(h_ref[r, k])
            out_ref[r, :BLOCK, k * BLOCK : (k + 1) * BLOCK] = high
            out_ref[r, BLOCK:, k * BLOCK : (k + 1) * BLOCK] = low


def split_hamiltonian(hamiltonian):
    rows, per_row = hamiltonian.shape[:2]
    return pl.pallas_call(
        split_kernel,
        grid=(rows // REACH,),
        in_specs=[pl.BlockSpec((REACH, per_row, BLOCK, BLOCK), lambda g: (g, 0, 0, 0))],
        out_specs=pl.BlockSpec((REACH, 2 * BLOCK, per_row * BLOCK), lambda g: (g, 0, 0)),
        out_shape=jax.ShapeDtypeStruct((rows, 2 * BLOCK, per_row * BLOCK), BF16),
        compiler_params=params(10),
        cost_estimate=cost(0, 8 * hamiltonian.size),
        name="split_hamiltonian",
    )(hamiltonian)


def first_kernel(chunk, v_ref, parts_ref):
    for at in range(0, v_ref.shape[0], SIZE):
        put_parts(parts_ref, SIZE + at, v_ref[at : at + SIZE, chunk * LANES : (chunk + 1) * LANES])


def split_vectors(vectors, chunk):
    rows = vectors.shape[0]
    return pl.pallas_call(
        functools.partial(first_kernel, chunk),
        in_specs=[WHOLE],
        out_specs=WHOLE,
        out_shape=jax.ShapeDtypeStruct((rows + 2 * SIZE, 2 * LANES), BF16),
        compiler_params=params(16),
        cost_estimate=cost(0, 8 * rows * LANES),
        name="split_vectors",
    )(vectors)


def scales(step, coef_ref):
    here, by = coef_ref[ORDER - step], 2.0
    if step == 1:
        by = 2.0 * coef_ref[ORDER]
    elif step == 2:
        here = here - coef_ref[ORDER]
    elif step == ORDER:
        by = 1.0
    return here, by


def product(slots_ref, h_ref, parts_ref, row):
    per_row = h_ref.shape[2] // BLOCK
    base = (row // REACH) * REACH
    picked = []
    for k in range(per_row):
        start = pl.multiple_of((slots_ref[row * per_row + k] + base) * BLOCK, BLOCK)
        picked.append(parts_ref[pl.ds(start, BLOCK), :])
    both = jnp.dot(h_ref[row], jnp.concatenate(picked, axis=0), preferred_element_type=F32)
    top, bottom = both[:BLOCK], both[BLOCK:]
    return top[:, :LANES] + ((top[:, LANES:] + bottom[:, :LANES]) + bottom[:, LANES:])


def interior_kernel(step, chunk, slots_ref, coef_ref, h_ref, v_ref, parts_ref, *rest):
    q_ref = rest[0] if step > 2 else None
    out_ref, next_ref = rest[-2:] if step < ORDER else rest[-3:-1]
    here, by = scales(step, coef_ref)
    lanes = slice(chunk * LANES, (chunk + 1) * LANES)
    count = h_ref.shape[0] - 2 * REACH
    unroll = max(n for n in range(1, 13) if count % n == 0)

    def some(i, carry):
        for u in range(unroll):
            at = i * unroll + u
            row = at + REACH
            total = product(slots_ref, h_ref, parts_ref, row)
            rows = pl.ds(pl.multiple_of(at * BLOCK, BLOCK), BLOCK)
            whole = pl.ds(pl.multiple_of(row * BLOCK, BLOCK), BLOCK)
            value = here * v_ref[whole, lanes] + by * total
            if q_ref is not None:
                value = value - q_ref[rows, :]
            out_ref[rows, :] = value
            if step < ORDER:
                put_parts(next_ref, pl.multiple_of((row + REACH) * BLOCK, BLOCK), value)
        return carry

    lax.fori_loop(0, count // unroll, some, 0)
    if step == ORDER:
        copy = pltpu.make_async_copy(out_ref, next_ref.at[pl.ds(SIZE, count * BLOCK), lanes], rest[-1])
        copy.start()
        copy.wait()


def interior(step, chunk, slots, coefficients, parts_h, vectors, parts, q, filtered):
    rows = vectors.shape[0]
    inner = rows - 2 * SIZE
    args = [slots, coefficients, parts_h, vectors, parts]
    if step > 2:
        args.append(q)
    aliases = {}
    if step < ORDER:
        second = jax.ShapeDtypeStruct(parts.shape, BF16)
    else:
        second = jax.ShapeDtypeStruct(vectors.shape, F32)
        if filtered is not None:
            aliases = {len(args): 1}
            args.append(filtered)
    specs = [SCALARS, SCALARS] + [WHOLE] * (len(args) - 2)
    if aliases:
        specs[-1] = ANYWHERE
    return pl.pallas_call(
        functools.partial(interior_kernel, step, chunk),
        in_specs=specs,
        out_specs=[WHOLE, WHOLE if step < ORDER else ANYWHERE],
        out_shape=[jax.ShapeDtypeStruct((inner, LANES), F32), second],
        scratch_shapes=[] if step < ORDER else [pltpu.SemaphoreType.DMA],
        input_output_aliases=aliases,
        compiler_params=params(16),
        cost_estimate=cost(8 * inner * LANES * parts_h.shape[2], 2 * parts_h.size),
        name="interior",
    )(*args)


def border_kernel(step, chunk, slots_ref, coef_ref, h_ref, v_ref, before_ref, after_ref, *rest):
    has_q = step > 2
    q_refs = rest[:2] if has_q else None
    low_ref, high_ref, parts_ref, next_ref = rest[-4:] if step < ORDER else rest[-5:-1]
    copies = []
    here, by = scales(step, coef_ref)
    lanes = slice(chunk * LANES, (chunk + 1) * LANES)
    count = h_ref.shape[0]
    put_parts(parts_ref, 0, before_ref[...])
    put_parts(parts_ref, (count + REACH) * BLOCK, after_ref[...])
    for side, (first, out_ref) in enumerate(((0, low_ref), (count - REACH, high_ref))):
        for r in range(REACH):
            row = first + r
            total = product(slots_ref, h_ref, parts_ref, row)
            rows = slice(r * BLOCK, (r + 1) * BLOCK)
            whole = slice(row * BLOCK, (row + 1) * BLOCK)
            value = here * v_ref[whole, lanes] + by * total
            if has_q:
                value = value - q_refs[side][rows]
            out_ref[rows] = value
            if step < ORDER:
                put_parts(next_ref, (row + REACH) * BLOCK, value)
        if step == ORDER:
            rows = pl.ds(first * BLOCK, SIZE)
            copies.append(pltpu.make_async_copy(out_ref, next_ref.at[rows, lanes], rest[-1].at[side]))
            copies[-1].start()
    for copy in copies:
        copy.wait()


def border(step, chunk, slots, coefficients, parts_h, vectors, halo, q, parts, following):
    args = [slots, coefficients, parts_h, vectors, *halo]
    if step > 2:
        args += list(q)
    aliases = {len(args): 2, len(args) + 1: 3}
    args += [parts, following]
    strip = jax.ShapeDtypeStruct((SIZE, LANES), F32)
    last = WHOLE if step < ORDER else ANYWHERE
    low, high, _, following = pl.pallas_call(
        functools.partial(border_kernel, step, chunk),
        in_specs=[SCALARS, SCALARS] + [WHOLE] * (len(args) - 3) + [last],
        out_specs=[WHOLE] * 3 + [last],
        scratch_shapes=[] if step < ORDER else [pltpu.SemaphoreType.DMA((2,))],
        out_shape=[strip, strip, jax.ShapeDtypeStruct(parts.shape, parts.dtype), jax.ShapeDtypeStruct(following.shape, following.dtype)],
        input_output_aliases=aliases,
        compiler_params=params(16),
        cost_estimate=cost(16 * SIZE * LANES * parts_h.shape[2], 4 * 12 * SIZE * LANES),
        name="border",
    )(*args)
    return low, high, following


def gram_kernel(chunks, halves, kinds, has_before, finish, bits_ref, *rest):
    own_refs, rest = rest[:chunks], rest[chunks:]
    got_refs = {}
    for d in kinds:
        if d:
            got_refs[d], rest = rest[:chunks], rest[chunks:]
    before_ref = rest[0] if has_before else None
    outs = rest[-2:] if finish else rest[-1:]
    width = chunks * LANES

    def joined(refs, strip):
        rows = pl.ds(pl.multiple_of(strip * SIZE, SIZE), SIZE)
        return jnp.concatenate([r[rows, :] for r in refs], axis=1)

    def products(left, right):
        total = jnp.dot(left[0], right[1], preferred_element_type=F32)
        total += jnp.dot(left[1], right[0], preferred_element_type=F32)
        return total + jnp.dot(left[0], right[0], preferred_element_type=F32)

    for n, d in enumerate(kinds):
        total = before_ref[n] if has_before else jnp.zeros((width, width), F32)
        if d == 0:
            for strip in range(2 * halves):
                own = joined(own_refs, strip)
                total += 0.5 * products(two_parts(own.T), two_parts(own))
        else:
            bit = bits_ref[d.bit_length() - 1]
            for strip in range(halves):
                own = joined(own_refs, strip + halves * bit)
                total += products(two_parts(own.T), two_parts(joined(got_refs[d], strip)))
        if not finish:
            outs[0][n] = total
        else:
            parts = width // finish
            for t in range(parts // 2):
                one = total[:, 2 * t * finish : (2 * t + 1) * finish]
                two = total[:, (2 * t + 1) * finish : (2 * t + 2) * finish]
                even = bits_ref[bits_ref.shape[0] - 1] == 0
                outs[0][n * (parts // 2) + t] = jnp.where(even, one, two)
                outs[1][n * (parts // 2) + t] = jnp.where(even, two, one)


def gram_sums(bits, kinds, own, got, before, finish):
    chunks = len(own)
    halves = own[0].shape[0] // (2 * SIZE)
    width = chunks * LANES
    args = [bits, *own]
    for d in kinds:
        if d:
            args += got[d]
    if before is not None:
        args.append(before)
    if finish:
        half = jax.ShapeDtypeStruct((len(kinds) * width // finish // 2, width, finish), F32)
        shape = [half, half]
    else:
        shape = [jax.ShapeDtypeStruct((len(kinds), width, width), F32)]
    out = pl.pallas_call(
        functools.partial(gram_kernel, chunks, halves, kinds, before is not None, finish),
        in_specs=[SCALARS] + [WHOLE] * (len(args) - 1),
        out_specs=[WHOLE] * len(shape),
        out_shape=shape,
        compiler_params=params(12),
        cost_estimate=cost(6 * halves * SIZE * width * width * (len(kinds) + 1), 4 * halves * SIZE * width * 4),
        name="gram_sums",
    )(*args)
    return out if finish else out[0]


def on_device(hamiltonian, columns, vectors, coefficients):
    block_rows, per_row = columns.shape
    peers = lax.axis_size("rows")
    groups = lax.axis_size("vecs")
    total_blocks = block_rows * peers
    width = vectors.shape[1]
    chunks = width // LANES
    rows_at, vecs_at = lax.axis_index("rows"), lax.axis_index("vecs")
    up = [(i, (i + 1) % peers) for i in range(peers)]
    down = [(j, i) for i, j in up]

    def exchange(first, last):
        return lax.ppermute(last, "rows", up), lax.ppermute(first, "rows", down)

    lanes = [slice(c * LANES, (c + 1) * LANES) for c in range(chunks)]
    halo = [exchange(vectors[:SIZE, l], vectors[-SIZE:, l]) for l in lanes]

    local = jnp.arange(block_rows, dtype=jnp.int32)
    offsets = (columns - (rows_at * block_rows + local)[:, None] + REACH) % total_blocks
    slots = (offsets + (local % REACH)[:, None]).reshape(-1)
    parts_h = split_hamiltonian(hamiltonian)

    parts = [split_vectors(vectors, c) for c in range(chunks)]
    terms, older, inner = ([None] * chunks for _ in range(3))
    filtered = None
    for c in range(chunks):
        inner[c] = interior(1, c, slots, coefficients, parts_h, vectors, parts[c], None, None)
    for step in range(1, ORDER + 1):
        for c in range(chunks):
            mid, following = inner[c]
            if step == ORDER:
                following = filtered
            q = older[c] and (older[c][0], older[c][2])
            low, high, following = border(
                step, c, slots, coefficients, parts_h, vectors, halo[c], q, parts[c], following
            )
            older[c], terms[c], parts[c] = terms[c], (low, mid, high), following
            if step == ORDER:
                filtered = following
                continue
            halo[c] = exchange(low, high)
            q = older[c] and older[c][1]
            inner[c] = interior(step + 1, c, slots, coefficients, parts_h, vectors, parts[c], q, filtered)
            if step + 1 == ORDER:
                filtered = inner[c][1]

    bit_count = (groups - 1).bit_length()
    vec_bits = [(vecs_at >> b) & 1 for b in range(bit_count)]
    per_group = peers // groups
    piece = width // per_group
    wanted = rows_at ^ (vecs_at * per_group)
    bits = jnp.stack([*vec_bits, wanted & 1]).astype(jnp.int32)

    def swapped(x, distance):
        return lax.ppermute(x, "vecs", [(i, i ^ distance) for i in range(groups)])

    def received(halves_of):
        got = {}
        for d in range(1, groups):
            if d == 1 or d % 2 == 0:
                bit = vec_bits[d.bit_length() - 1]
                got[d] = [swapped(halves_of(c, bit), d) for c in range(chunks)]
            else:
                got[d] = [swapped(x, 1) for x in got[d - 1]]
        return got

    half_inner = (vectors.shape[0] - 2 * SIZE) // 2

    def inner_half(c, bit):
        return lax.dynamic_slice_in_dim(terms[c][1], (1 - bit) * half_inner, half_inner, axis=0)

    def outer_half(c, bit):
        return jnp.where(bit == 0, terms[c][2], terms[c][0])

    early, late = received(inner_half), received(outer_half)
    near, far = tuple(range(min(2, groups))), tuple(range(2, groups))
    shares = []
    for kinds in (near, far):
        if not kinds:
            continue
        sums = gram_sums(bits, kinds, [t[1] for t in terms], early, None, 0)
        ends = [jnp.concatenate([t[0], t[2]], axis=0) for t in terms]
        keep, send = gram_sums(bits, kinds, ends, late, sums, piece)
        shares.append(keep + lax.ppermute(send, "rows", [(i, i ^ 1) for i in range(peers)]))

    distance = 2
    while distance < peers:
        if shares[0].shape[0] == 1 and len(shares) == 2:
            shares = [jnp.concatenate(shares, axis=0)]
        mine = (wanted // distance) & 1
        reduced = []
        for share in shares:
            share = share.reshape(-1, 2, width, piece)
            keep = lax.dynamic_index_in_dim(share, mine, axis=1, keepdims=False)
            send = lax.dynamic_index_in_dim(share, 1 - mine, axis=1, keepdims=False)
            reduced.append(keep + lax.ppermute(send, "rows", [(i, i ^ distance) for i in range(peers)]))
        shares = reduced
        if len(shares) == 2 and shares[1].shape[0] != shares[0].shape[0] and shares[0].shape[0] == 1:
            shares = [jnp.concatenate(shares, axis=0)]
        distance *= 2
    share = shares[0].reshape(per_group, piece, piece)

    turned = []
    for n in range(per_group):
        pairs = []
        for i in range(peers):
            for g in range(groups):
                to = (g * per_group + (i + n) % per_group) * groups + i // per_group
                pairs.append((i * groups + g, to))
        sent = lax.dynamic_index_in_dim(share, (rows_at + n) % per_group, axis=0, keepdims=False)
        turned.append(lax.ppermute(sent, ("rows", "vecs"), pairs).T)
    turned = jnp.stack(turned)
    gram = []
    for t in range(per_group):
        gram.append(share[t] + lax.dynamic_index_in_dim(turned, (rows_at - t) % per_group, axis=0, keepdims=False))
    gram = jnp.concatenate(gram, axis=0) / (total_blocks * BLOCK)
    return filtered, gram


def solution(mesh):
    return jax.shard_map(
        on_device,
        mesh=mesh,
        in_specs=(P("rows", None, None, None), P("rows", None), P("rows", "vecs"), P()),
        out_specs=(P("rows", "vecs"), P("vecs", "rows")),
        check_vma=False,
    )
```

```python
import functools

import jax
import jax.numpy as jnp
from jax import lax
from jax.experimental import pallas as pl
from jax.experimental.pallas import tpu as pltpu
from jax.sharding import PartitionSpec as P

BLOCK = 128
REACH = 4
ORDER = 6
LANES = 128
SIZE = REACH * BLOCK
F32 = jnp.float32
BF16 = jnp.bfloat16
WHOLE = pl.BlockSpec(memory_space=pltpu.VMEM)
ANYWHERE = pl.BlockSpec(memory_space=pl.ANY)
SCALARS = pl.BlockSpec(memory_space=pltpu.SMEM)


def shaped(shape, dtype=F32):
    return jax.ShapeDtypeStruct(shape, dtype)


def cost(flops, moved):
    return pl.CostEstimate(flops=flops, bytes_accessed=moved, transcendentals=0)


class Call:
    def __init__(self):
        self.args, self.specs, self.outs, self.out_specs, self.aliases = [], [], [], [], {}

    def scalars(self, *arrays):
        self.args += arrays
        self.specs += [SCALARS] * len(arrays)
        return self

    def reads(self, *arrays):
        self.args += arrays
        self.specs += [WHOLE] * len(arrays)
        return self

    def writes(self, shape, before=None, spec=WHOLE):
        if before is not None:
            self.aliases[len(self.args)] = len(self.outs)
            self.args.append(before)
            self.specs.append(spec)
        self.outs.append(shape)
        self.out_specs.append(spec)
        return self

    def __call__(self, body, name, estimate, scratch=(), mib=16):
        def kernel(*refs):
            ins, rest = refs[: len(self.args)], refs[len(self.args) :]
            body(ins, rest[: len(self.outs)], rest[len(self.outs) :])

        return pl.pallas_call(
            kernel,
            in_specs=self.specs,
            out_specs=self.out_specs,
            out_shape=self.outs,
            scratch_shapes=scratch,
            input_output_aliases=self.aliases,
            compiler_params=pltpu.CompilerParams(vmem_limit_bytes=mib * 1024 * 1024),
            cost_estimate=estimate,
            name=name,
        )(*self.args)


def two_parts(x):
    high = x.astype(BF16)
    low = (x - high.astype(F32)).astype(BF16)
    return high, low


def put_parts(ref, start, value):
    high, low = two_parts(value)
    ref[pl.ds(start, value.shape[0]), :LANES] = high
    ref[pl.ds(start, value.shape[0]), LANES:] = low


def split_kernel(table_ref, h_ref, out_ref):
    for r in range(h_ref.shape[0]):
        for k in range(h_ref.shape[1]):
            high, low = two_parts(h_ref[r, k])
            out_ref[r, :BLOCK, k * BLOCK : (k + 1) * BLOCK] = high
            out_ref[r, BLOCK:, k * BLOCK : (k + 1) * BLOCK] = low


def split_hamiltonian(table, hamiltonian):
    rows, per_row = hamiltonian.shape[:2]
    return pl.pallas_call(
        split_kernel,
        grid=(rows // REACH,),
        in_specs=[SCALARS, pl.BlockSpec((REACH, per_row, BLOCK, BLOCK), lambda g: (g, 0, 0, 0))],
        out_specs=pl.BlockSpec((REACH, 2 * BLOCK, per_row * BLOCK), lambda g: (g, 0, 0)),
        out_shape=shaped((rows, 2 * BLOCK, per_row * BLOCK), BF16),
        compiler_params=pltpu.CompilerParams(vmem_limit_bytes=16 * 1024 * 1024),
        cost_estimate=cost(0, 8 * hamiltonian.size),
        name="split_hamiltonian",
    )(table, pltpu.with_memory_space_constraint(hamiltonian, pltpu.HBM))


def split_vectors(vectors, chunk):
    rows = vectors.shape[0]

    def body(ins, outs, scratch):
        for at in range(0, rows, SIZE):
            put_parts(outs[0], SIZE + at, ins[0][at : at + SIZE, chunk * LANES : (chunk + 1) * LANES])

    call = Call().reads(vectors).writes(shaped((rows + 2 * SIZE, 2 * LANES), BF16))
    return call(body, "split_vectors", cost(0, 8 * rows * LANES))[0]


def scales(step, coef_ref):
    here, by = coef_ref[ORDER - step], 2.0
    if step == 1:
        by = 2.0 * coef_ref[ORDER]
    elif step == 2:
        here = here - coef_ref[ORDER]
    elif step == ORDER:
        by = 1.0
    return here, by


def new_rows(step, chunk, common, parts_ref, row, q):
    table_ref, coef_ref, h_ref, v_ref = common
    per_row = h_ref.shape[2] // BLOCK
    base = (row // REACH) * REACH
    picked = []
    for k in range(per_row):
        start = pl.multiple_of((table_ref[row * per_row + k] + base) * BLOCK, BLOCK)
        picked.append(parts_ref[pl.ds(start, BLOCK), :])
    both = jnp.dot(h_ref[row], jnp.concatenate(picked, axis=0), preferred_element_type=F32)
    top, bottom = both[:BLOCK], both[BLOCK:]
    total = top[:, :LANES] + ((top[:, LANES:] + bottom[:, :LANES]) + bottom[:, LANES:])
    here, by = scales(step, coef_ref)
    whole = pl.ds(pl.multiple_of(row * BLOCK, BLOCK), BLOCK)
    value = here * v_ref[whole, chunk * LANES : (chunk + 1) * LANES] + by * total
    return value if q is None else value - q


def unrolled(first, count, one):
    unroll = max(n for n in range(1, 13) if count % n == 0)

    def some(i, carry):
        for u in range(unroll):
            one(first + i * unroll + u)
        return carry

    lax.fori_loop(0, count // unroll, some, 0)


def at_rows(block, size=BLOCK):
    return pl.ds(pl.multiple_of(block * BLOCK, BLOCK), size)


class Shape:
    def __init__(self, block_rows, per_row, width, groups):
        self.rows = block_rows
        self.inner = block_rows - 2 * REACH
        self.core = block_rows - 4 * REACH
        self.chunks = width // LANES
        self.width = width
        self.vec_bits = (groups - 1).bit_length()
        self.bits_at = block_rows * per_row


def put_sends(shape, table_ref, source_ref, send_refs, lanes):
    half = source_ref.shape[0] // 2
    for b, ref in enumerate(send_refs):
        other = 1 - table_ref[shape.bits_at + b]
        rows = pl.ds(pl.multiple_of(other * half, BLOCK), half)
        ref[:, lanes if ref.shape[1] == source_ref.shape[1] else slice(None)] = source_ref[rows, lanes]


def interior(step, chunk, shape, common, parts, q, before):
    call = Call().scalars(*common[:2]).reads(*common[2:], parts)
    if q is not None:
        call.reads(q)
    call.writes(shaped((shape.inner * BLOCK, LANES))).writes(shaped(parts.shape, BF16), before)

    def body(ins, outs, scratch):
        def one(row):
            old = None if q is None else ins[5][at_rows(row - REACH), :]
            value = new_rows(step, chunk, ins[:4], ins[4], row, old)
            outs[0][at_rows(row - REACH), :] = value
            put_parts(outs[1], pl.multiple_of((row + REACH) * BLOCK, BLOCK), value)

        unrolled(REACH, shape.inner, one)

    flops = 8 * shape.inner * BLOCK * LANES * common[2].shape[2]
    return call(body, "interior", cost(flops, 8 * common[2].size))


def interior_and_core(step, chunk, shape, common, parts, q, mid, before, filtered):
    last = chunk == shape.chunks - 1
    call = Call().scalars(*common[:2]).reads(*common[2:], parts, q, mid)
    call.writes(shaped((shape.inner * BLOCK, LANES))).writes(shaped(parts.shape, BF16))
    core = shape.core * BLOCK
    before = before or [None] * (1 + shape.vec_bits)
    call.writes(shaped((core, shape.width)), before[0])
    for one_before in before[1:]:
        call.writes(shaped((core // 2, shape.width)), one_before)
    if last:
        call.writes(shaped((shape.rows * BLOCK, shape.width)), None, ANYWHERE)
    lanes = slice(chunk * LANES, (chunk + 1) * LANES)

    def body(ins, outs, scratch):
        def one(row):
            value = new_rows(step, chunk, ins[:4], ins[4], row, ins[5][at_rows(row - REACH), :])
            outs[0][at_rows(row - REACH), :] = value
            put_parts(outs[1], pl.multiple_of((row + REACH) * BLOCK, BLOCK), value)

        def two(row):
            old = ins[6][at_rows(row - REACH), :]
            outs[2][at_rows(row - 2 * REACH), lanes] = new_rows(step + 1, chunk, ins[:4], outs[1], row, old)

        unrolled(REACH, shape.inner, one)
        unrolled(2 * REACH, shape.core, two)
        if last:
            copy = pltpu.make_async_copy(outs[2], outs[-1].at[pl.ds(2 * SIZE, core)], scratch[0])
            copy.start()
        put_sends(shape, ins[0], outs[2], outs[3 : 3 + shape.vec_bits], lanes)
        if last:
            copy.wait()

    flops = 8 * (shape.inner + shape.core) * BLOCK * LANES * common[2].shape[2]
    out = call(body, "interior_and_core", cost(flops, 14 * common[2].size), [pltpu.SemaphoreType.DMA] if last else [])
    return out[:2], out[2 : 3 + shape.vec_bits], out[-1] if last else None


def ring(step, chunk, shape, common, parts, mid, before, filtered):
    last = chunk == shape.chunks - 1
    call = Call().scalars(*common[:2]).reads(*common[2:], parts, mid)
    before = before or [None] * (1 + shape.vec_bits)
    call.writes(shaped((2 * SIZE, shape.width)), before[0])
    for one_before in before[1:]:
        call.writes(shaped((SIZE, shape.width)), one_before)
    if last:
        call.writes(shaped(filtered.shape), filtered, ANYWHERE)
    lanes = slice(chunk * LANES, (chunk + 1) * LANES)

    def body(ins, outs, scratch):
        copies = []
        for side, first in enumerate((REACH, shape.rows - 2 * REACH)):
            for r in range(REACH):
                row = first + r
                old = ins[5][at_rows(row - REACH), :]
                rows = pl.ds((side * REACH + r) * BLOCK, BLOCK)
                outs[0][rows, lanes] = new_rows(step, chunk, ins[:4], ins[4], row, old)
            if last:
                source = outs[0].at[pl.ds(side * SIZE, SIZE)]
                copies.append(pltpu.make_async_copy(source, outs[-1].at[pl.ds(first * BLOCK, SIZE)], scratch[0].at[side]))
                copies[-1].start()
        put_sends(shape, ins[0], outs[0], outs[1 : 1 + shape.vec_bits], lanes)
        for copy in copies:
            copy.wait()

    flops = 16 * SIZE * LANES * common[2].shape[2]
    out = call(body, "ring", cost(flops, 4 * common[2].size), [pltpu.SemaphoreType.DMA((2,))] if last else [])
    return out[: 1 + shape.vec_bits], out[-1] if last else None


def border(step, chunk, shape, common, halo, q, parts, following):
    call = Call().scalars(*common[:2]).reads(*common[2:], *halo)
    if q is not None:
        call.reads(*q)
    strip = shaped((SIZE, LANES))
    call.writes(shaped(parts.shape, BF16), parts).writes(shaped(parts.shape, BF16), following)
    call.writes(strip).writes(strip)

    def body(ins, outs, scratch):
        put_parts(outs[0], 0, ins[4][...])
        put_parts(outs[0], (shape.rows + REACH) * BLOCK, ins[5][...])
        for side, first in enumerate((0, shape.rows - REACH)):
            for r in range(REACH):
                rows = slice(r * BLOCK, (r + 1) * BLOCK)
                old = None if q is None else ins[6 + side][rows]
                value = new_rows(step, chunk, ins[:4], outs[0], first + r, old)
                outs[2 + side][rows] = value
                put_parts(outs[1], (first + r + REACH) * BLOCK, value)

    flops = 16 * SIZE * LANES * common[2].shape[2]
    parts, following, low, high = call(body, "border", cost(flops, 4 * common[2].size))
    return low, high, parts, following


def last_border(step, chunk, shape, common, halo, q, parts, before, filtered):
    last = chunk == shape.chunks - 1
    call = Call().scalars(*common[:2]).reads(*common[2:], *halo, *q)
    call.writes(shaped(parts.shape, BF16), parts).writes(shaped((2 * SIZE, shape.width)), before)
    for _ in range(shape.vec_bits):
        call.writes(shaped((SIZE, LANES)))
    if last:
        call.writes(shaped(filtered.shape), filtered, ANYWHERE)
    lanes = slice(chunk * LANES, (chunk + 1) * LANES)

    def body(ins, outs, scratch):
        copies = []
        put_parts(outs[0], 0, ins[4][...])
        put_parts(outs[0], (shape.rows + REACH) * BLOCK, ins[5][...])
        for side, first in enumerate((0, shape.rows - REACH)):
            for r in range(REACH):
                old = ins[6 + side][r * BLOCK : (r + 1) * BLOCK]
                rows = pl.ds((side * REACH + r) * BLOCK, BLOCK)
                outs[1][rows, lanes] = new_rows(step, chunk, ins[:4], outs[0], first + r, old)
            if last:
                source = outs[1].at[pl.ds(side * SIZE, SIZE)]
                copies.append(pltpu.make_async_copy(source, outs[-1].at[pl.ds(first * BLOCK, SIZE)], scratch[0].at[side]))
                copies[-1].start()
        put_sends(shape, ins[0], outs[1], outs[2 : 2 + shape.vec_bits], lanes)
        for copy in copies:
            copy.wait()

    flops = 16 * SIZE * LANES * common[2].shape[2]
    out = call(body, "last_border", cost(flops, 4 * common[2].size), [pltpu.SemaphoreType.DMA((2,))] if last else [])
    return out[1], out[2 : 2 + shape.vec_bits], out[-1] if last else filtered


def gram_sums(shape, table, kinds, own, got, before, piece):
    width = shape.width
    call = Call().scalars(table).reads(*own)
    places = {}
    for d in kinds:
        if d:
            for n, arrays in enumerate(got[d]):
                places[d, n] = (len(call.args), len(arrays))
                call.reads(*arrays)
    before_at = len(call.args)
    if before is not None:
        call.reads(before)
    if piece:
        kept = shaped((len(kinds) * width // piece // 2, width, piece))
        call.writes(kept).writes(kept)
    else:
        call.writes(shaped((len(kinds), width, width)))

    def products(left, right):
        total = jnp.dot(left[0], right[1], preferred_element_type=F32)
        total += jnp.dot(left[1], right[0], preferred_element_type=F32)
        return total + jnp.dot(left[0], right[0], preferred_element_type=F32)

    def body(ins, outs, scratch):
        table_ref = ins[0]
        totals = [ins[before_at][n] if before is not None else jnp.zeros((width, width), F32) for n in range(len(kinds))]
        for n in range(len(own)):
            ref = ins[1 + n]
            half = ref.shape[0] // 2
            for at in range(0, half, SIZE):
                sides = [ref[at : at + SIZE], ref[half + at : half + at + SIZE]]
                chosen = {}
                for m, d in enumerate(kinds):
                    if d == 0:
                        for side in sides:
                            totals[m] += 0.5 * products(two_parts(side.T), two_parts(side))
                        continue
                    b = d.bit_length() - 1
                    if b not in chosen:
                        first = table_ref[shape.bits_at + b] == 0
                        chosen[b] = two_parts(jnp.where(first, sides[0], sides[1]).T)
                    where, count = places[d, n]
                    other = [ins[where + c][at : at + SIZE] for c in range(count)]
                    other = other[0] if count == 1 else jnp.concatenate(other, axis=1)
                    totals[m] += products(chosen[b], two_parts(other))
        for m, total in enumerate(totals):
            if not piece:
                outs[0][m] = total
                continue
            pairs = width // piece // 2
            even = table_ref[shape.bits_at + shape.vec_bits] == 0
            for t in range(pairs):
                one = total[:, 2 * t * piece : (2 * t + 1) * piece]
                two = total[:, (2 * t + 1) * piece : (2 * t + 2) * piece]
                outs[0][m * pairs + t] = jnp.where(even, one, two)
                outs[1][m * pairs + t] = jnp.where(even, two, one)

    rows = sum(a.shape[0] for a in own)
    flops = 3 * rows * width * width * (len(kinds) + 1)
    out = call(body, "gram_sums", cost(flops, 8 * rows * width))
    return out if piece else out[0]


def fold(shape, table, level, pairs):
    call = Call().scalars(table)
    count = 0
    for keep, got in pairs:
        call.reads(keep, got)
        count += keep.shape[0]
    half = shaped((count // 2, *pairs[0][0].shape[1:]))
    call.writes(half).writes(half)

    def body(ins, outs, scratch):
        even = ins[0][shape.bits_at + shape.vec_bits + level] == 0
        sums = []
        for n in range(len(pairs)):
            for m in range(ins[1 + 2 * n].shape[0]):
                sums.append(ins[1 + 2 * n][m] + ins[2 + 2 * n][m])
        for n in range(count // 2):
            outs[0][n] = jnp.where(even, sums[2 * n], sums[2 * n + 1])
            outs[1][n] = jnp.where(even, sums[2 * n + 1], sums[2 * n])

    return call(body, "fold", cost(0, 8 * count * pairs[0][0][0].size))


def on_device(hamiltonian, columns, vectors, coefficients):
    block_rows, per_row = columns.shape
    peers = lax.axis_size("rows")
    groups = lax.axis_size("vecs")
    total_blocks = block_rows * peers
    width = vectors.shape[1]
    shape = Shape(block_rows, per_row, width, groups)
    chunks = shape.chunks
    rows_at, vecs_at = lax.axis_index("rows"), lax.axis_index("vecs")
    up = [(i, (i + 1) % peers) for i in range(peers)]
    down = [(j, i) for i, j in up]

    def exchange(first, last):
        return lax.ppermute(last, "rows", up), lax.ppermute(first, "rows", down)

    lanes = [slice(c * LANES, (c + 1) * LANES) for c in range(chunks)]
    halo = [exchange(vectors[:SIZE, l], vectors[-SIZE:, l]) for l in lanes]

    local = jnp.arange(block_rows, dtype=jnp.int32)
    offsets = (columns - (rows_at * block_rows + local)[:, None] + REACH) % total_blocks
    slots = (offsets + (local % REACH)[:, None]).reshape(-1)
    per_group = peers // groups
    piece = width // per_group
    wanted = rows_at ^ (vecs_at * per_group)
    levels = (peers - 1).bit_length()
    bits = [(vecs_at >> b) & 1 for b in range(shape.vec_bits)] + [(wanted >> b) & 1 for b in range(levels)]
    table = jnp.concatenate([slots, jnp.stack(bits).astype(jnp.int32)])

    common = (table, coefficients, split_hamiltonian(table, hamiltonian), vectors)

    parts = [split_vectors(vectors, c) for c in range(chunks)]
    terms, older, inner = ([None] * chunks for _ in range(3))
    core = rims = ends = filtered = None
    late = [None] * chunks
    for step in range(1, ORDER + 1):
        for c in range(chunks):
            q = older[c] and (older[c][0], older[c][2])
            if step == ORDER:
                ends, late[c], filtered = last_border(step, c, shape, common, halo[c], q, parts[c], ends, filtered)
                continue
            low, high, padded, following = border(
                step, c, shape, common, halo[c], q, parts[c], inner[c] and inner[c][1]
            )
            halo[c] = exchange(low, high)
            if step == 1:
                inner[c] = interior(1, c, shape, common, padded, None, following)
                following = inner[c][1]
            older[c], terms[c], parts[c] = terms[c], (low, inner[c][0], high), following
            q = older[c] and older[c][1]
            if step + 1 < ORDER - 1:
                inner[c] = interior(step + 1, c, shape, common, parts[c], q, None)
            elif step + 1 == ORDER - 1:
                inner[c], core, whole = interior_and_core(
                    step + 1, c, shape, common, parts[c], q, terms[c][1], core, filtered
                )
                filtered = whole if whole is not None else filtered
            else:
                rims, whole = ring(step + 1, c, shape, common, parts[c], older[c][1], rims, filtered)
                filtered = whole if whole is not None else filtered

    def swapped(x, distance):
        return lax.ppermute(x, "vecs", [(i, i ^ distance) for i in range(groups)])

    def received(sends):
        got = {}
        for d in range(1, groups):
            if d == 1 or d % 2 == 0:
                got[d] = swapped(sends[d.bit_length() - 1], d)
            else:
                got[d] = swapped(got[d - 1], 1)
        return got

    got_core, got_rims = received(core[1:]), received(rims[1:])
    got_late = [received(sends) for sends in late]
    early = {d: [[got_core[d]], [got_rims[d]]] for d in range(1, groups)}
    late = {d: [[got[d] for got in got_late]] for d in range(1, groups)}
    shares = []
    swaps = [[(i, i ^ (1 << level)) for i in range(peers)] for level in range(levels)]
    for kinds in (tuple(range(min(2, groups))), tuple(range(2, groups))):
        if kinds:
            sums = gram_sums(shape, table, kinds, [core[0], rims[0]], early, None, 0)
            keep, send = gram_sums(shape, table, kinds, [ends], late, sums, piece)
            shares.append((keep, lax.ppermute(send, "rows", swaps[0])))
    for level in range(1, levels):
        if shares[0][0].shape[0] == 1:
            shares = [tuple(fold(shape, table, level, shares))]
        else:
            shares = [tuple(fold(shape, table, level, [pair])) for pair in shares]
        shares = [(keep, lax.ppermute(send, "rows", swaps[level])) for keep, send in shares]
    share = (shares[0][0] + shares[0][1]).reshape(per_group, piece, piece)

    turned = []
    for n in range(per_group):
        pairs = []
        for i in range(peers):
            for g in range(groups):
                to = (g * per_group + (i + n) % per_group) * groups + i // per_group
                pairs.append((i * groups + g, to))
        sent = lax.dynamic_index_in_dim(share, (rows_at + n) % per_group, axis=0, keepdims=False)
        turned.append(lax.ppermute(sent, ("rows", "vecs"), pairs).T)
    turned = jnp.stack(turned)
    gram = []
    for t in range(per_group):
        gram.append(share[t] + lax.dynamic_index_in_dim(turned, (rows_at - t) % per_group, axis=0, keepdims=False))
    gram = jnp.concatenate(gram, axis=0) / (total_blocks * BLOCK)
    return filtered, gram


def solution(mesh):
    return jax.shard_map(
        on_device,
        mesh=mesh,
        in_specs=(P("rows", None, None, None), P("rows", None), P("rows", "vecs"), P()),
        out_specs=(P("rows", "vecs"), P("vecs", "rows")),
        check_vma=False,
    )
```

```python
import functools

import jax
import jax.numpy as jnp
from jax import lax
from jax.experimental import pallas as pl
from jax.experimental.pallas import tpu as pltpu
from jax.sharding import PartitionSpec as P

BLOCK = 128
REACH = 4
ORDER = 6
LANES = 128
SIZE = REACH * BLOCK
F32 = jnp.float32
BF16 = jnp.bfloat16
WHOLE = pl.BlockSpec(memory_space=pltpu.VMEM)
ANYWHERE = pl.BlockSpec(memory_space=pl.ANY)
SCALARS = pl.BlockSpec(memory_space=pltpu.SMEM)


def shaped(shape, dtype=F32):
    return jax.ShapeDtypeStruct(shape, dtype)


def cost(flops, moved):
    return pl.CostEstimate(flops=flops, bytes_accessed=moved, transcendentals=0)


class Call:
    def __init__(self, chain):
        self.chain = chain
        self.args, self.specs, self.outs, self.out_specs, self.aliases = [], [], [], [], {}

    def anywhere(self, *arrays):
        self.args += arrays
        self.specs += [ANYWHERE] * len(arrays)
        return self

    def scalars(self, *arrays):
        self.args += arrays
        self.specs += [SCALARS] * len(arrays)
        return self

    def reads(self, *arrays):
        self.args += arrays
        self.specs += [WHOLE] * len(arrays)
        return self

    def writes(self, shape, before=None, spec=WHOLE):
        if before is not None:
            self.aliases[len(self.args)] = len(self.outs)
            self.args.append(before)
            self.specs.append(spec)
        self.outs.append(shape)
        self.out_specs.append(spec)
        return self

    def passes(self, *arrays):
        for array in arrays:
            self.writes(shaped(array.shape, array.dtype), array, ANYWHERE)
        return self

    def __call__(self, body, name, estimate, scratch=(), mib=16):
        if self.chain.token is not None:
            self.anywhere(self.chain.token)
        self.writes(shaped((8, LANES)))
        count = len(self.args)

        def kernel(*refs):
            ins, outs = refs[:count], refs[count : count + len(self.outs)]
            outs[-1][...] = jnp.zeros((8, LANES), F32)
            body(ins, outs[:-1], refs[count + len(self.outs) :])

        *results, self.chain.token = pl.pallas_call(
            kernel,
            in_specs=self.specs,
            out_specs=self.out_specs,
            out_shape=self.outs,
            scratch_shapes=scratch,
            input_output_aliases=self.aliases,
            compiler_params=pltpu.CompilerParams(vmem_limit_bytes=mib * 1024 * 1024),
            cost_estimate=estimate,
            name=name,
        )(*self.args)
        return results


class Chain:
    token = None


def two_parts(x):
    high = x.astype(BF16)
    low = (x - high.astype(F32)).astype(BF16)
    return high, low


def put_parts(ref, start, value):
    high, low = two_parts(value)
    ref[pl.ds(start, value.shape[0]), :LANES] = high
    ref[pl.ds(start, value.shape[0]), LANES:] = low


def prepare(shape, chain, table, hamiltonian, vectors):
    rows, per_row = hamiltonian.shape[:2]
    strips, slots = rows // REACH, 3
    strip = shaped((SIZE, LANES))
    far = [pltpu.with_memory_space_constraint(x, pltpu.HBM) for x in (hamiltonian, vectors)]
    call = Call(chain).scalars(table).anywhere(*far)
    call.writes(shaped((rows, 2 * BLOCK, per_row * BLOCK), BF16)).writes(shaped(vectors.shape))
    for _ in range(shape.chunks):
        call.writes(shaped((vectors.shape[0] + 2 * SIZE, 2 * LANES), BF16))
    for _ in range(1, shape.chunks):
        call.writes(strip).writes(strip)

    def body(ins, outs, scratch):
        h_ref, v_ref = ins[1], ins[2]
        parts_h, copy_v = outs[:2]
        held, sems, v_sem = scratch

        def fetch(g):
            slot = lax.rem(g, slots)
            return pltpu.make_async_copy(h_ref.at[pl.ds(g * REACH, REACH)], held.at[slot], sems.at[slot])

        def split(g, carry):
            slot = lax.rem(g, slots)
            fetch(g).wait()
            for r in range(REACH):
                for k in range(per_row):
                    high, low = two_parts(held[slot, r, k])
                    parts_h[g * REACH + r, :BLOCK, k * BLOCK : (k + 1) * BLOCK] = high
                    parts_h[g * REACH + r, BLOCK:, k * BLOCK : (k + 1) * BLOCK] = low

            @pl.when(g + slots < strips)
            def _():
                fetch(g + slots).start()

            return carry

        def split_v(g, carry):
            at = pl.multiple_of(g * SIZE, SIZE)
            for c in range(shape.chunks):
                put_parts(outs[2 + c], pl.multiple_of(at + SIZE, SIZE), copy_v[pl.ds(at, SIZE), c * LANES : (c + 1) * LANES])
            return carry

        copy = pltpu.make_async_copy(v_ref, copy_v, v_sem)
        for g in range(min(slots, strips)):
            fetch(jnp.int32(g)).start()
        copy.start()
        lax.fori_loop(0, strips // 2, split, 0)
        copy.wait()
        lax.fori_loop(0, strips, split_v, 0)
        for c in range(1, shape.chunks):
            lanes = slice(c * LANES, (c + 1) * LANES)
            outs[shape.chunks + 2 * c][...] = copy_v[:SIZE, lanes]
            outs[shape.chunks + 2 * c + 1][...] = copy_v[-SIZE:, lanes]
        lax.fori_loop(strips // 2, strips, split, 0)

    scratch = [pltpu.VMEM((slots, REACH, *hamiltonian.shape[1:]), F32), pltpu.SemaphoreType.DMA((slots,)), pltpu.SemaphoreType.DMA]
    out = call(body, "prepare", cost(0, 8 * hamiltonian.size), scratch)
    parts, sends = out[2 : 2 + shape.chunks], out[2 + shape.chunks :]
    return out[0], out[1], parts, [tuple(sends[2 * c : 2 * c + 2]) for c in range(shape.chunks - 1)]


def scales(step, coef_ref):
    here, by = coef_ref[ORDER - step], 2.0
    if step == 1:
        by = 2.0 * coef_ref[ORDER]
    elif step == 2:
        here = here - coef_ref[ORDER]
    elif step == ORDER:
        by = 1.0
    return here, by


def new_rows(step, chunk, common, parts_ref, row, q):
    table_ref, coef_ref, h_ref, v_ref = common
    per_row = h_ref.shape[2] // BLOCK
    base = (row // REACH) * REACH
    picked = []
    for k in range(per_row):
        start = pl.multiple_of((table_ref[row * per_row + k] + base) * BLOCK, BLOCK)
        picked.append(parts_ref[pl.ds(start, BLOCK), :])
    both = jnp.dot(h_ref[row], jnp.concatenate(picked, axis=0), preferred_element_type=F32)
    top, bottom = both[:BLOCK], both[BLOCK:]
    total = top[:, :LANES] + ((top[:, LANES:] + bottom[:, :LANES]) + bottom[:, LANES:])
    here, by = scales(step, coef_ref)
    whole = pl.ds(pl.multiple_of(row * BLOCK, BLOCK), BLOCK)
    value = here * v_ref[whole, chunk * LANES : (chunk + 1) * LANES] + by * total
    return value if q is None else value - q


def unrolled(first, count, one):
    unroll = max(n for n in range(1, 13) if count % n == 0)

    def some(i, carry):
        for u in range(unroll):
            one(first + i * unroll + u)
        return carry

    lax.fori_loop(0, count // unroll, some, 0)


def at_rows(block, size=BLOCK):
    return pl.ds(pl.multiple_of(block * BLOCK, BLOCK), size)


class Shape:
    def __init__(self, block_rows, per_row, width, groups):
        self.rows = block_rows
        self.inner = block_rows - 2 * REACH
        self.core = block_rows - 4 * REACH
        self.chunks = width // LANES
        self.width = width
        self.vec_bits = (groups - 1).bit_length()
        self.bits_at = block_rows * per_row


def put_sends(shape, table_ref, source_ref, sends, lanes):
    half = source_ref.shape[0] // 2
    for b, ref, at in sends:
        other = 1 - table_ref[shape.bits_at + b]
        rows = pl.ds(pl.multiple_of(other * half, BLOCK), half)
        ref[at : at + half, lanes if ref.shape[1] == source_ref.shape[1] else slice(None)] = source_ref[rows, lanes]


def interior(step, chunk, shape, chain, common, parts, q, before):
    call = Call(chain).scalars(*common[:2]).reads(*common[2:], parts)
    if q is not None:
        call.reads(q)
    call.writes(shaped((shape.inner * BLOCK, LANES))).writes(shaped(parts.shape, BF16), before)

    def body(ins, outs, scratch):
        def one(row):
            old = None if q is None else ins[5][at_rows(row - REACH), :]
            value = new_rows(step, chunk, ins[:4], ins[4], row, old)
            outs[0][at_rows(row - REACH), :] = value
            put_parts(outs[1], pl.multiple_of((row + REACH) * BLOCK, BLOCK), value)

        unrolled(REACH, shape.inner, one)

    flops = 8 * shape.inner * BLOCK * LANES * common[2].shape[2]
    return call(body, "interior", cost(flops, 8 * common[2].size))


def interior_and_core(step, chunk, shape, chain, common, parts, q, mid, before, filtered):
    last = chunk == shape.chunks - 1
    call = Call(chain).scalars(*common[:2]).reads(*common[2:], parts, q, mid)
    call.writes(shaped((shape.inner * BLOCK, LANES))).writes(shaped(parts.shape, BF16))
    core = shape.core * BLOCK
    before = before or [None, None]
    call.writes(shaped((core, shape.width)), before[0]).writes(shaped((core // 2, shape.width)), before[1])
    for _ in range(1, shape.vec_bits):
        call.writes(shaped((core // 2, LANES)))
    if last:
        call.writes(shaped((shape.rows * BLOCK, shape.width)), None, ANYWHERE)
    lanes = slice(chunk * LANES, (chunk + 1) * LANES)

    def body(ins, outs, scratch):
        def one(row):
            value = new_rows(step, chunk, ins[:4], ins[4], row, ins[5][at_rows(row - REACH), :])
            outs[0][at_rows(row - REACH), :] = value
            put_parts(outs[1], pl.multiple_of((row + REACH) * BLOCK, BLOCK), value)

        def two(row):
            old = ins[6][at_rows(row - REACH), :]
            outs[2][at_rows(row - 2 * REACH), lanes] = new_rows(step + 1, chunk, ins[:4], outs[1], row, old)

        unrolled(REACH, shape.inner, one)
        unrolled(2 * REACH, shape.core, two)
        if last:
            copy = pltpu.make_async_copy(outs[2], outs[-1].at[pl.ds(2 * SIZE, core)], scratch[0])
            copy.start()
        put_sends(shape, ins[0], outs[2], [(b, outs[3 + b], 0) for b in range(shape.vec_bits)], lanes)
        if last:
            copy.wait()

    flops = 8 * (shape.inner + shape.core) * BLOCK * LANES * common[2].shape[2]
    out = call(body, "interior_and_core", cost(flops, 14 * common[2].size), [pltpu.SemaphoreType.DMA] if last else [])
    return out[:2], out[2:4], out[4 : 3 + shape.vec_bits], out[-1] if last else None


def ring(step, chunk, shape, chain, common, parts, mid, before, filtered):
    last = chunk == shape.chunks - 1
    call = Call(chain).scalars(*common[:2]).reads(*common[2:], parts, mid)
    before = before or [None] * (1 + shape.vec_bits)
    for n, one_before in enumerate(before):
        call.writes(shaped((2 * SIZE if n < 2 else SIZE, shape.width)), one_before)
    if last:
        call.writes(shaped(filtered.shape), filtered, ANYWHERE)
    lanes = slice(chunk * LANES, (chunk + 1) * LANES)

    def body(ins, outs, scratch):
        copies = []
        for side, first in enumerate((REACH, shape.rows - 2 * REACH)):
            for r in range(REACH):
                row = first + r
                old = ins[5][at_rows(row - REACH), :]
                rows = pl.ds((side * REACH + r) * BLOCK, BLOCK)
                outs[0][rows, lanes] = new_rows(step, chunk, ins[:4], ins[4], row, old)
            if last:
                source = outs[0].at[pl.ds(side * SIZE, SIZE)]
                copies.append(pltpu.make_async_copy(source, outs[-1].at[pl.ds(first * BLOCK, SIZE)], scratch[0].at[side]))
                copies[-1].start()
        put_sends(shape, ins[0], outs[0], [(b, outs[1 + b], 0) for b in range(shape.vec_bits)], lanes)
        for copy in copies:
            copy.wait()

    flops = 16 * SIZE * LANES * common[2].shape[2]
    out = call(body, "ring", cost(flops, 4 * common[2].size), [pltpu.SemaphoreType.DMA((2,))] if last else [])
    return out[: 1 + shape.vec_bits], out[-1] if last else None


def border(step, chunk, shape, chain, common, halo, q, parts, following, passed=(), joined=None):
    call = Call(chain).scalars(*common[:2]).reads(*common[2:], *halo)
    if q is not None:
        call.reads(*q)
    strip = shaped((SIZE, LANES))
    call.writes(shaped(parts.shape, BF16), parts).writes(shaped(parts.shape, BF16), following)
    call.writes(strip).writes(strip).passes(*passed)
    wide_at = len(call.outs)
    for before in joined or ():
        call.writes(shaped((SIZE, shape.width)), before)
    lanes = slice(chunk * LANES, (chunk + 1) * LANES)

    def body(ins, outs, scratch):
        put_parts(outs[0], 0, ins[4][...])
        put_parts(outs[0], (shape.rows + REACH) * BLOCK, ins[5][...])
        for side, first in enumerate((0, shape.rows - REACH)):
            for r in range(REACH):
                rows = slice(r * BLOCK, (r + 1) * BLOCK)
                old = None if q is None else ins[6 + side][rows]
                value = new_rows(step, chunk, ins[:4], outs[0], first + r, old)
                outs[2 + side][rows] = value
                if joined:
                    outs[wide_at + side][rows, lanes] = value
                put_parts(outs[1], (first + r + REACH) * BLOCK, value)

    flops = 16 * SIZE * LANES * common[2].shape[2]
    parts, following, low, high, *rest = call(body, "border", cost(flops, 4 * common[2].size))
    return low, high, parts, following, rest[: len(passed)], rest[len(passed) :]


def last_border(step, chunk, shape, chain, common, halo, q, parts, near, before, filtered, got, passed):
    last = chunk == shape.chunks - 1
    call = Call(chain).scalars(*common[:2]).reads(*common[2:], *halo, *q)
    got_at = len(call.args)
    for arrays in got:
        call.reads(*arrays)
    call.writes(shaped(parts.shape, BF16), parts).writes(shaped(near.shape), near)
    before = before or [None] * shape.vec_bits
    for n, one_before in enumerate(before):
        call.writes(shaped((SIZE if n else 2 * SIZE, shape.width)), one_before)
    got_to = len(call.outs)
    for arrays in got:
        call.writes(shaped((arrays[0].shape[0], shape.width)))
    call.passes(*passed)
    if last:
        call.writes(shaped(filtered.shape), filtered, ANYWHERE)
    lanes = slice(chunk * LANES, (chunk + 1) * LANES)

    def body(ins, outs, scratch):
        copies = []
        put_parts(outs[0], 0, ins[4][:, lanes])
        put_parts(outs[0], (shape.rows + REACH) * BLOCK, ins[5][:, lanes])
        for side, first in enumerate((0, shape.rows - REACH)):
            for r in range(REACH):
                old = ins[6 + side][r * BLOCK : (r + 1) * BLOCK]
                rows = pl.ds((side * REACH + r) * BLOCK, BLOCK)
                outs[2][rows, lanes] = new_rows(step, chunk, ins[:4], outs[0], first + r, old)
            if last:
                source = outs[2].at[pl.ds(side * SIZE, SIZE)]
                copies.append(pltpu.make_async_copy(source, outs[-1].at[pl.ds(first * BLOCK, SIZE)], scratch[0].at[side]))
                copies[-1].start()
        sends = [(0, outs[1], SIZE)] + [(b, outs[2 + b], 0) for b in range(1, shape.vec_bits)]
        put_sends(shape, ins[0], outs[2], sends, lanes)
        for n, arrays in enumerate(got):
            for c in range(len(arrays)):
                outs[got_to + n][:, c * LANES : (c + 1) * LANES] = ins[got_at + n * len(arrays) + c][...]
        for copy in copies:
            copy.wait()

    flops = 16 * SIZE * LANES * common[2].shape[2]
    out = call(body, "last_border", cost(flops, 4 * common[2].size), [pltpu.SemaphoreType.DMA((2,))] if last else [])
    joined, passed = out[got_to : got_to + len(got)], out[got_to + len(got) :][: len(passed)]
    return out[1], out[2 : 2 + shape.vec_bits], joined, passed, out[-1] if last else filtered


def gram_sums(shape, chain, table, kinds, own, got, before, piece):
    width = shape.width
    call = Call(chain).scalars(table).reads(*own)
    places = {}
    for d in kinds:
        if d:
            for n, (arrays, offset) in enumerate(got[d]):
                places[d, n] = (len(call.args), len(arrays), offset)
                call.reads(*arrays)
    before_at = len(call.args)
    if before is not None:
        call.reads(before)
    if piece:
        kept = shaped((len(kinds) * width // piece // 2, width, piece))
        call.writes(kept).writes(kept)
    else:
        call.writes(shaped((len(kinds), width, width)))

    def products(left, right):
        total = jnp.dot(left[0], right[1], preferred_element_type=F32)
        total += jnp.dot(left[1], right[0], preferred_element_type=F32)
        return total + jnp.dot(left[0], right[0], preferred_element_type=F32)

    def body(ins, outs, scratch):
        table_ref = ins[0]
        totals = [ins[before_at][n] if before is not None else jnp.zeros((width, width), F32) for n in range(len(kinds))]
        for n in range(len(own)):
            ref = ins[1 + n]
            half = ref.shape[0] // 2
            for at in range(0, half, SIZE):
                sides = [ref[at : at + SIZE], ref[half + at : half + at + SIZE]]
                chosen = {}
                for m, d in enumerate(kinds):
                    if d == 0:
                        for side in sides:
                            totals[m] += 0.5 * products(two_parts(side.T), two_parts(side))
                        continue
                    b = d.bit_length() - 1
                    if b not in chosen:
                        first = table_ref[shape.bits_at + b] == 0
                        chosen[b] = two_parts(jnp.where(first, sides[0], sides[1]).T)
                    where, count, offset = places[d, n]
                    other = [ins[where + c][offset + at : offset + at + SIZE] for c in range(count)]
                    other = other[0] if count == 1 else jnp.concatenate(other, axis=1)
                    totals[m] += products(chosen[b], two_parts(other))
        for m, total in enumerate(totals):
            if not piece:
                outs[0][m] = total
                continue
            pairs = width // piece // 2
            even = table_ref[shape.bits_at + shape.vec_bits] == 0
            for t in range(pairs):
                one = total[:, 2 * t * piece : (2 * t + 1) * piece]
                two = total[:, (2 * t + 1) * piece : (2 * t + 2) * piece]
                outs[0][m * pairs + t] = jnp.where(even, one, two)
                outs[1][m * pairs + t] = jnp.where(even, two, one)

    rows = sum(a.shape[0] for a in own)
    flops = 3 * rows * width * width * (len(kinds) + 1)
    out = call(body, "gram_sums", cost(flops, 8 * rows * width))
    return out if piece else out[0]


def fold(shape, chain, table, level, pairs):
    call = Call(chain).scalars(table)
    count = 0
    for keep, got in pairs:
        call.reads(keep, got)
        count += keep.shape[0]
    half = shaped((count // 2, *pairs[0][0].shape[1:]))
    call.writes(half).writes(half)

    def body(ins, outs, scratch):
        even = ins[0][shape.bits_at + shape.vec_bits + level] == 0
        sums = []
        for n in range(len(pairs)):
            for m in range(ins[1 + 2 * n].shape[0]):
                sums.append(ins[1 + 2 * n][m] + ins[2 + 2 * n][m])
        for n in range(count // 2):
            outs[0][n] = jnp.where(even, sums[2 * n], sums[2 * n + 1])
            outs[1][n] = jnp.where(even, sums[2 * n + 1], sums[2 * n])

    return call(body, "fold", cost(0, 8 * count * pairs[0][0][0].size))


def on_device(hamiltonian, columns, vectors, coefficients):
    block_rows, per_row = columns.shape
    peers = lax.axis_size("rows")
    groups = lax.axis_size("vecs")
    total_blocks = block_rows * peers
    width = vectors.shape[1]
    shape = Shape(block_rows, per_row, width, groups)
    chunks = shape.chunks
    rows_at, vecs_at = lax.axis_index("rows"), lax.axis_index("vecs")
    up = [(i, (i + 1) % peers) for i in range(peers)]
    down = [(j, i) for i, j in up]

    def exchange(first, last):
        return lax.ppermute(last, "rows", up), lax.ppermute(first, "rows", down)

    chain = Chain()
    halo = [exchange(vectors[:SIZE, :LANES], vectors[-SIZE:, :LANES])]

    local = jnp.arange(block_rows, dtype=jnp.int32)
    offsets = (columns - (rows_at * block_rows + local)[:, None] + REACH) % total_blocks
    slots = (offsets + (local % REACH)[:, None]).reshape(-1)
    per_group = peers // groups
    piece = width // per_group
    wanted = rows_at ^ (vecs_at * per_group)
    levels = (peers - 1).bit_length()
    bits = [(vecs_at >> b) & 1 for b in range(shape.vec_bits)] + [(wanted >> b) & 1 for b in range(levels)]
    table = jnp.concatenate([slots, jnp.stack(bits).astype(jnp.int32)])

    parts_h, vectors, parts, strips = prepare(shape, chain, table, hamiltonian, vectors)
    halo += [exchange(*pair) for pair in strips]
    common = (table, coefficients, parts_h, vectors)

    terms, older, inner, core_sends, got_core = ([None] * chunks for _ in range(5))
    core = rims = ends = filtered = None
    wide = (None, None)

    def swapped(x, distance):
        return lax.ppermute(x, "vecs", [(i, i ^ distance) for i in range(groups)])

    def received(sends):
        return {d: swapped(sends[d.bit_length() - 2], d) for d in range(2, groups, 2)}

    def forwarded(got):
        out = {}
        for d, rows in got.items():
            out[d], out[d + 1] = rows, swapped(rows, 1)
        return out

    def inside(step, c, padded=None, following=None):
        nonlocal core, rims, filtered
        q = older[c] and older[c][1]
        whole = None
        if step == 1:
            inner[c] = interior(1, c, shape, chain, common, padded, None, following)
        elif step < ORDER - 1:
            inner[c] = interior(step, c, shape, chain, common, parts[c], q, None)
        elif step == ORDER - 1:
            inner[c], core, core_sends[c], whole = interior_and_core(
                step, c, shape, chain, common, parts[c], q, terms[c][1], core, filtered
            )
        else:
            rims, whole = ring(step, c, shape, chain, common, parts[c], q, rims, filtered)
        filtered = filtered if whole is None else whole

    for step in range(1, ORDER):
        for c in range(chunks):
            if step > 1 and (step > 2 or c > 0):
                inside(step, c)
            q = older[c] and (older[c][0], older[c][2])
            late = step == ORDER - 1
            low, high, padded, following, passed, both = border(
                step, c, shape, chain, common, halo[c], q, parts[c], inner[c] and inner[c][1],
                core_sends[c] if late else (), wide if late else (),
            )
            if late:
                got_core[c], wide = received(passed), both
            else:
                halo[c] = exchange(low, high)
            if step == 1:
                inside(1, c, padded, following)
                following = inner[c][1]
            older[c], terms[c], parts[c] = terms[c], (low, inner[c][0], high), following
        if step == 1:
            inside(2, 0)
    last_halo = exchange(*wide)
    for c in range(chunks):
        inside(ORDER, c)
    got_rims = received(rims[2:])
    near = rims[1]
    for c in range(chunks):
        q = (older[c][0], older[c][2])
        got = [[rows[d] for rows in got_core] for d in range(2, groups, 2)] if c == 0 else []
        passed = [core[1]] if c == chunks - 1 else []
        near, ends, joined, passed, filtered = last_border(
            ORDER, c, shape, chain, common, last_halo, q, parts[c], near, ends, filtered, got, passed
        )
        if c == 0:
            all_core = {2 * n + 2: rows for n, rows in enumerate(joined)}
    near_core = passed[0]
    got_core = forwarded(all_core)
    got_rims, got_ends = forwarded(got_rims), forwarded(received(ends[1:]))

    kinds, far = tuple(range(min(2, groups))), tuple(range(2, groups))
    swaps = [[(i, i ^ (1 << level)) for i in range(peers)] for level in range(levels)]
    shares = []
    sums = gram_sums(shape, chain, table, kinds, [core[0]], {1: [([swapped(near_core, 1)], 0)]}, None, 0)
    near = swapped(near, 1)
    keep, send = gram_sums(shape, chain, table, kinds, [rims[0], ends[0]], {1: [([near], 0), ([near], SIZE)]}, sums, piece)
    shares.append((keep, lax.ppermute(send, "rows", swaps[0])))
    if far:
        arrived = {d: [([got_core[d]], 0), ([got_rims[d]], 0)] for d in far}
        sums = gram_sums(shape, chain, table, far, [core[0], rims[0]], arrived, None, 0)
        keep, send = gram_sums(shape, chain, table, far, [ends[0]], {d: [([got_ends[d]], 0)] for d in far}, sums, piece)
        shares.append((keep, lax.ppermute(send, "rows", swaps[0])))
    for level in range(1, levels):
        if shares[0][0].shape[0] == 1:
            shares = [tuple(fold(shape, chain, table, level, shares))]
        else:
            shares = [tuple(fold(shape, chain, table, level, [pair])) for pair in shares]
        shares = [(keep, lax.ppermute(send, "rows", swaps[level])) for keep, send in shares]
    share = (shares[0][0] + shares[0][1]).reshape(per_group, piece, piece)

    turned = []
    for n in range(per_group):
        pairs = []
        for i in range(peers):
            for g in range(groups):
                to = (g * per_group + (i + n) % per_group) * groups + i // per_group
                pairs.append((i * groups + g, to))
        sent = lax.dynamic_index_in_dim(share, (rows_at + n) % per_group, axis=0, keepdims=False)
        turned.append(lax.ppermute(sent, ("rows", "vecs"), pairs).T)
    turned = jnp.stack(turned)
    gram = []
    for t in range(per_group):
        gram.append(share[t] + lax.dynamic_index_in_dim(turned, (rows_at - t) % per_group, axis=0, keepdims=False))
    gram = jnp.concatenate(gram, axis=0) / (total_blocks * BLOCK)
    return filtered, gram


def solution(mesh):
    return jax.shard_map(
        on_device,
        mesh=mesh,
        in_specs=(P("rows", None, None, None), P("rows", None), P("rows", "vecs"), P()),
        out_specs=(P("rows", "vecs"), P("vecs", "rows")),
        check_vma=False,
    )
```

```python
import functools

import jax
import jax.numpy as jnp
from jax import lax
from jax.experimental import pallas as pl
from jax.experimental.pallas import tpu as pltpu
from jax.sharding import PartitionSpec as P

BLOCK = 128
REACH = 4
ORDER = 6
LANES = 128
SIZE = REACH * BLOCK
F32 = jnp.float32
BF16 = jnp.bfloat16
WHOLE = pl.BlockSpec(memory_space=pltpu.VMEM)
ANYWHERE = pl.BlockSpec(memory_space=pl.ANY)
SCALARS = pl.BlockSpec(memory_space=pltpu.SMEM)


def shaped(shape, dtype=F32):
    return jax.ShapeDtypeStruct(shape, dtype)


def cost(flops, moved):
    return pl.CostEstimate(flops=flops, bytes_accessed=moved, transcendentals=0)


class Call:
    def __init__(self, chain):
        self.chain = chain
        self.args, self.specs, self.outs, self.out_specs, self.aliases = [], [], [], [], {}

    def anywhere(self, *arrays):
        self.args += arrays
        self.specs += [ANYWHERE] * len(arrays)
        return self

    def scalars(self, *arrays):
        self.args += arrays
        self.specs += [SCALARS] * len(arrays)
        return self

    def reads(self, *arrays):
        self.args += arrays
        self.specs += [WHOLE] * len(arrays)
        return self

    def writes(self, shape, before=None, spec=WHOLE):
        if before is not None:
            self.aliases[len(self.args)] = len(self.outs)
            self.args.append(before)
            self.specs.append(spec)
        self.outs.append(shape)
        self.out_specs.append(spec)
        return self

    def passes(self, *arrays):
        for array in arrays:
            self.writes(shaped(array.shape, array.dtype), array, ANYWHERE)
        return self

    def __call__(self, body, name, estimate, scratch=(), mib=16):
        if self.chain.token is not None:
            self.anywhere(self.chain.token)
        self.writes(shaped((8, LANES)))
        count = len(self.args)

        def kernel(*refs):
            ins, outs = refs[:count], refs[count : count + len(self.outs)]
            outs[-1][...] = jnp.zeros((8, LANES), F32)
            body(ins, outs[:-1], refs[count + len(self.outs) :])

        *results, self.chain.token = pl.pallas_call(
            kernel,
            in_specs=self.specs,
            out_specs=self.out_specs,
            out_shape=self.outs,
            scratch_shapes=scratch,
            input_output_aliases=self.aliases,
            compiler_params=pltpu.CompilerParams(vmem_limit_bytes=mib * 1024 * 1024),
            cost_estimate=estimate,
            name=name,
        )(*self.args)
        return results


class Chain:
    token = None


def two_parts(x):
    high = x.astype(BF16)
    low = (x - high.astype(F32)).astype(BF16)
    return high, low


def put_parts(ref, start, value):
    high, low = two_parts(value)
    ref[pl.ds(start, value.shape[0]), :LANES] = high
    ref[pl.ds(start, value.shape[0]), LANES:] = low


def prepare(shape, chain, table, hamiltonian, vectors):
    rows, per_row = hamiltonian.shape[:2]
    strips, slots = rows // REACH, 4
    far = [pltpu.with_memory_space_constraint(x, pltpu.HBM) for x in (hamiltonian, vectors)]
    call = Call(chain).scalars(table).anywhere(*far)
    call.writes(shaped((rows, 2 * BLOCK, per_row * BLOCK), BF16)).writes(shaped(vectors.shape))
    for _ in range(shape.chunks):
        call.writes(shaped((vectors.shape[0] + 2 * SIZE, 2 * LANES), BF16))

    def body(ins, outs, scratch):
        h_ref, v_ref = ins[1], ins[2]
        parts_h, copy_v = outs[:2]
        held, sems, v_sem = scratch

        def fetch(g):
            slot = lax.rem(g, slots)
            return pltpu.make_async_copy(h_ref.at[pl.ds(g * REACH, REACH)], held.at[slot], sems.at[slot])

        def split(g, carry):
            slot = lax.rem(g, slots)
            fetch(g).wait()
            for r in range(REACH):
                for k in range(per_row):
                    high, low = two_parts(held[slot, r, k])
                    parts_h[g * REACH + r, :BLOCK, k * BLOCK : (k + 1) * BLOCK] = high
                    parts_h[g * REACH + r, BLOCK:, k * BLOCK : (k + 1) * BLOCK] = low

            @pl.when(g + slots < strips)
            def _():
                fetch(g + slots).start()

            return carry

        def split_v(g, carry):
            at = pl.multiple_of(g * SIZE, SIZE)
            for c in range(shape.chunks):
                put_parts(outs[2 + c], pl.multiple_of(at + SIZE, SIZE), copy_v[pl.ds(at, SIZE), c * LANES : (c + 1) * LANES])
            return carry

        copy = pltpu.make_async_copy(v_ref, copy_v, v_sem)
        for g in range(min(slots, strips)):
            fetch(jnp.int32(g)).start()
        copy.start()
        lax.fori_loop(0, strips // 2, split, 0)
        copy.wait()
        lax.fori_loop(0, strips, split_v, 0)
        lax.fori_loop(strips // 2, strips, split, 0)

    scratch = [pltpu.VMEM((slots, REACH, *hamiltonian.shape[1:]), F32), pltpu.SemaphoreType.DMA((slots,)), pltpu.SemaphoreType.DMA]
    out = call(body, "prepare", cost(0, 8 * hamiltonian.size), scratch)
    return out[0], out[1], out[2:]


def scales(step, coef_ref):
    here, by = coef_ref[ORDER - step], 2.0
    if step == 1:
        by = 2.0 * coef_ref[ORDER]
    elif step == 2:
        here = here - coef_ref[ORDER]
    elif step == ORDER:
        by = 1.0
    return here, by


def new_rows(step, chunk, common, parts_ref, row, q):
    table_ref, coef_ref, h_ref, v_ref = common
    per_row = h_ref.shape[2] // BLOCK
    base = (row // REACH) * REACH
    picked = []
    for k in range(per_row):
        start = pl.multiple_of((table_ref[row * per_row + k] + base) * BLOCK, BLOCK)
        picked.append(parts_ref[pl.ds(start, BLOCK), :])
    both = jnp.dot(h_ref[row], jnp.concatenate(picked, axis=0), preferred_element_type=F32)
    top, bottom = both[:BLOCK], both[BLOCK:]
    total = top[:, :LANES] + ((top[:, LANES:] + bottom[:, :LANES]) + bottom[:, LANES:])
    here, by = scales(step, coef_ref)
    whole = pl.ds(pl.multiple_of(row * BLOCK, BLOCK), BLOCK)
    value = here * v_ref[whole, chunk * LANES : (chunk + 1) * LANES] + by * total
    return value if q is None else value - q


def unrolled(first, count, one):
    unroll = max(n for n in range(1, 13) if count % n == 0)

    def some(i, carry):
        for u in range(unroll):
            one(first + i * unroll + u)
        return carry

    lax.fori_loop(0, count // unroll, some, 0)


def at_rows(block, size=BLOCK):
    return pl.ds(pl.multiple_of(block * BLOCK, BLOCK), size)


class Shape:
    def __init__(self, block_rows, per_row, width, groups):
        self.rows = block_rows
        self.inner = block_rows - 2 * REACH
        self.core = block_rows - 4 * REACH
        self.chunks = width // LANES
        self.width = width
        self.vec_bits = (groups - 1).bit_length()
        self.bits_at = block_rows * per_row


def put_sends(shape, table_ref, source_ref, sends, lanes):
    half = source_ref.shape[0] // 2
    for b, ref, at in sends:
        other = 1 - table_ref[shape.bits_at + b]
        rows = pl.ds(pl.multiple_of(other * half, BLOCK), half)
        ref[at : at + half, lanes if ref.shape[1] == source_ref.shape[1] else slice(None)] = source_ref[rows, lanes]


def interior(step, chunk, shape, chain, common, parts, q, before):
    call = Call(chain).scalars(*common[:2]).reads(*common[2:], parts)
    if q is not None:
        call.reads(q)
    call.writes(shaped((shape.inner * BLOCK, LANES))).writes(shaped(parts.shape, BF16), before)

    def body(ins, outs, scratch):
        def one(row):
            old = None if q is None else ins[5][at_rows(row - REACH), :]
            value = new_rows(step, chunk, ins[:4], ins[4], row, old)
            outs[0][at_rows(row - REACH), :] = value
            put_parts(outs[1], pl.multiple_of((row + REACH) * BLOCK, BLOCK), value)

        unrolled(REACH, shape.inner, one)

    flops = 8 * shape.inner * BLOCK * LANES * common[2].shape[2]
    return call(body, "interior", cost(flops, 8 * common[2].size))


def interior_and_core(step, chunk, shape, chain, common, parts, q, mid, before, filtered):
    last = chunk == shape.chunks - 1
    call = Call(chain).scalars(*common[:2]).reads(*common[2:], parts, q, mid)
    call.writes(shaped((shape.inner * BLOCK, LANES))).writes(shaped(parts.shape, BF16))
    core = shape.core * BLOCK
    before = before or [None, None]
    call.writes(shaped((core, shape.width)), before[0]).writes(shaped((core // 2, shape.width)), before[1])
    spare = 0 if last else core // 8
    for _ in range(1, shape.vec_bits):
        call.writes(shaped((core // 2 + spare, LANES)))
    if last:
        call.writes(shaped((shape.rows * BLOCK, shape.width)), None, ANYWHERE)
    lanes = slice(chunk * LANES, (chunk + 1) * LANES)

    def body(ins, outs, scratch):
        def one(row):
            value = new_rows(step, chunk, ins[:4], ins[4], row, ins[5][at_rows(row - REACH), :])
            outs[0][at_rows(row - REACH), :] = value
            put_parts(outs[1], pl.multiple_of((row + REACH) * BLOCK, BLOCK), value)

        def two(row):
            old = ins[6][at_rows(row - REACH), :]
            outs[2][at_rows(row - 2 * REACH), lanes] = new_rows(step + 1, chunk, ins[:4], outs[1], row, old)

        unrolled(REACH, shape.inner, one)
        unrolled(2 * REACH, shape.core, two)
        if last:
            copy = pltpu.make_async_copy(outs[2], outs[-1].at[pl.ds(2 * SIZE, core)], scratch[0])
            copy.start()
        put_sends(shape, ins[0], outs[2], [(b, outs[3 + b], 0) for b in range(shape.vec_bits)], lanes)
        if last:
            copy.wait()

    flops = 8 * (shape.inner + shape.core) * BLOCK * LANES * common[2].shape[2]
    out = call(body, "interior_and_core", cost(flops, 14 * common[2].size), [pltpu.SemaphoreType.DMA] if last else [])
    return out[:2], out[2:4], out[4 : 3 + shape.vec_bits], out[-1] if last else None


def ring(step, chunk, shape, chain, common, parts, mid, before, filtered):
    last = chunk == shape.chunks - 1
    call = Call(chain).scalars(*common[:2]).reads(*common[2:], parts, mid)
    before = before or [None] * (1 + shape.vec_bits)
    for n, one_before in enumerate(before):
        call.writes(shaped((2 * SIZE if n < 2 else SIZE, shape.width)), one_before)
    if last:
        call.writes(shaped(filtered.shape), filtered, ANYWHERE)
    lanes = slice(chunk * LANES, (chunk + 1) * LANES)

    def body(ins, outs, scratch):
        copies = []
        for side, first in enumerate((REACH, shape.rows - 2 * REACH)):
            for r in range(REACH):
                row = first + r
                old = ins[5][at_rows(row - REACH), :]
                rows = pl.ds((side * REACH + r) * BLOCK, BLOCK)
                outs[0][rows, lanes] = new_rows(step, chunk, ins[:4], ins[4], row, old)
            if last:
                source = outs[0].at[pl.ds(side * SIZE, SIZE)]
                copies.append(pltpu.make_async_copy(source, outs[-1].at[pl.ds(first * BLOCK, SIZE)], scratch[0].at[side]))
                copies[-1].start()
        put_sends(shape, ins[0], outs[0], [(b, outs[1 + b], 0) for b in range(shape.vec_bits)], lanes)
        for copy in copies:
            copy.wait()

    flops = 16 * SIZE * LANES * common[2].shape[2]
    out = call(body, "ring", cost(flops, 4 * common[2].size), [pltpu.SemaphoreType.DMA((2,))] if last else [])
    return out[: 1 + shape.vec_bits], out[-1] if last else None


def border(step, chunk, shape, chain, common, halo, q, parts, following, joined=None):
    call = Call(chain).scalars(*common[:2]).reads(*common[2:], *halo)
    if q is not None:
        call.reads(*q)
    strip = shaped((SIZE, LANES))
    call.writes(shaped(parts.shape, BF16), parts).writes(shaped(parts.shape, BF16), following)
    call.writes(strip).writes(strip)
    wide_at = len(call.outs)
    for before in joined or ():
        call.writes(shaped((SIZE, shape.width)), before)
    lanes = slice(chunk * LANES, (chunk + 1) * LANES)

    def body(ins, outs, scratch):
        put_parts(outs[0], 0, ins[4][...])
        put_parts(outs[0], (shape.rows + REACH) * BLOCK, ins[5][...])
        for side, first in enumerate((0, shape.rows - REACH)):
            for r in range(REACH):
                rows = slice(r * BLOCK, (r + 1) * BLOCK)
                old = None if q is None else ins[6 + side][rows]
                value = new_rows(step, chunk, ins[:4], outs[0], first + r, old)
                outs[2 + side][rows] = value
                if joined:
                    outs[wide_at + side][rows, lanes] = value
                put_parts(outs[1], (first + r + REACH) * BLOCK, value)

    flops = 16 * SIZE * LANES * common[2].shape[2]
    parts, following, low, high, *both = call(body, "border", cost(flops, 4 * common[2].size))
    return low, high, parts, following, both


def last_border(step, chunk, shape, chain, common, halo, q, parts, near, before, filtered, got, passed):
    last = chunk == shape.chunks - 1
    call = Call(chain).scalars(*common[:2]).reads(*common[2:], *halo, *q)
    got_at = len(call.args)
    for arrays in got:
        call.reads(*arrays)
    call.writes(shaped(parts.shape, BF16), parts).writes(shaped(near.shape), near)
    before = before or [None] * shape.vec_bits
    for n, one_before in enumerate(before):
        call.writes(shaped((SIZE if n else 2 * SIZE, shape.width)), one_before)
    got_to = len(call.outs)
    for arrays in got:
        call.writes(shaped((arrays[-1].shape[0], shape.width)))
    call.passes(*passed)
    if last:
        call.writes(shaped(filtered.shape), filtered, ANYWHERE)
    lanes = slice(chunk * LANES, (chunk + 1) * LANES)

    def body(ins, outs, scratch):
        copies = []
        put_parts(outs[0], 0, ins[4][:, lanes])
        put_parts(outs[0], (shape.rows + REACH) * BLOCK, ins[5][:, lanes])
        for side, first in enumerate((0, shape.rows - REACH)):
            for r in range(REACH):
                old = ins[6 + side][r * BLOCK : (r + 1) * BLOCK]
                rows = pl.ds((side * REACH + r) * BLOCK, BLOCK)
                outs[2][rows, lanes] = new_rows(step, chunk, ins[:4], outs[0], first + r, old)
            if last:
                source = outs[2].at[pl.ds(side * SIZE, SIZE)]
                copies.append(pltpu.make_async_copy(source, outs[-1].at[pl.ds(first * BLOCK, SIZE)], scratch[0].at[side]))
                copies[-1].start()
        sends = [(0, outs[1], SIZE)] + [(b, outs[2 + b], 0) for b in range(1, shape.vec_bits)]
        put_sends(shape, ins[0], outs[2], sends, lanes)
        for n, arrays in enumerate(got):
            for c in range(len(arrays)):
                rows = slice(0, arrays[-1].shape[0])
                outs[got_to + n][:, c * LANES : (c + 1) * LANES] = ins[got_at + n * len(arrays) + c][rows]
        for copy in copies:
            copy.wait()

    flops = 16 * SIZE * LANES * common[2].shape[2]
    out = call(body, "last_border", cost(flops, 4 * common[2].size), [pltpu.SemaphoreType.DMA((2,))] if last else [])
    joined, passed = out[got_to : got_to + len(got)], out[got_to + len(got) :][: len(passed)]
    return out[1], out[2 : 2 + shape.vec_bits], joined, passed, out[-1] if last else filtered


def gram_sums(shape, chain, table, kinds, own, got, before, piece):
    width = shape.width
    call = Call(chain).scalars(table).reads(*own)
    places = {}
    for d in kinds:
        if d:
            for n, (arrays, offset) in enumerate(got[d]):
                places[d, n] = (len(call.args), len(arrays), offset)
                call.reads(*arrays)
    before_at = len(call.args)
    if before is not None:
        call.reads(before)
    if piece:
        kept = shaped((len(kinds) * width // piece // 2, width, piece))
        call.writes(kept).writes(kept)
    else:
        call.writes(shaped((len(kinds), width, width)))

    def products(left, right):
        total = jnp.dot(left[0], right[1], preferred_element_type=F32)
        total += jnp.dot(left[1], right[0], preferred_element_type=F32)
        return total + jnp.dot(left[0], right[0], preferred_element_type=F32)

    def body(ins, outs, scratch):
        table_ref = ins[0]
        totals = [ins[before_at][n] if before is not None else jnp.zeros((width, width), F32) for n in range(len(kinds))]
        for n in range(len(own)):
            ref = ins[1 + n]
            half = ref.shape[0] // 2
            for at in range(0, half, SIZE):
                sides = [ref[at : at + SIZE], ref[half + at : half + at + SIZE]]
                chosen = {}
                for m, d in enumerate(kinds):
                    if d == 0:
                        for side in sides:
                            totals[m] += 0.5 * products(two_parts(side.T), two_parts(side))
                        continue
                    b = d.bit_length() - 1
                    if b not in chosen:
                        first = table_ref[shape.bits_at + b] == 0
                        chosen[b] = two_parts(jnp.where(first, sides[0], sides[1]).T)
                    where, count, offset = places[d, n]
                    other = [ins[where + c][offset + at : offset + at + SIZE] for c in range(count)]
                    other = other[0] if count == 1 else jnp.concatenate(other, axis=1)
                    totals[m] += products(chosen[b], two_parts(other))
        for m, total in enumerate(totals):
            if not piece:
                outs[0][m] = total
                continue
            pairs = width // piece // 2
            even = table_ref[shape.bits_at + shape.vec_bits] == 0
            for t in range(pairs):
                one = total[:, 2 * t * piece : (2 * t + 1) * piece]
                two = total[:, (2 * t + 1) * piece : (2 * t + 2) * piece]
                outs[0][m * pairs + t] = jnp.where(even, one, two)
                outs[1][m * pairs + t] = jnp.where(even, two, one)

    rows = sum(a.shape[0] for a in own)
    flops = 3 * rows * width * width * (len(kinds) + 1)
    out = call(body, "gram_sums", cost(flops, 8 * rows * width))
    return out if piece else out[0]


def fold(shape, chain, table, level, pairs, passed=()):
    call = Call(chain).scalars(table)
    count = 0
    for keep, got in pairs:
        call.reads(keep, got)
        count += keep.shape[0]
    half = shaped((count // 2, *pairs[0][0].shape[1:]))
    call.writes(half).writes(half).passes(*passed)

    def body(ins, outs, scratch):
        even = ins[0][shape.bits_at + shape.vec_bits + level] == 0
        sums = []
        for n in range(len(pairs)):
            for m in range(ins[1 + 2 * n].shape[0]):
                sums.append(ins[1 + 2 * n][m] + ins[2 + 2 * n][m])
        for n in range(count // 2):
            outs[0][n] = jnp.where(even, sums[2 * n], sums[2 * n + 1])
            outs[1][n] = jnp.where(even, sums[2 * n + 1], sums[2 * n])

    keep, send, *passed = call(body, "fold", cost(0, 8 * count * pairs[0][0][0].size))
    return keep, send, passed


def on_device(hamiltonian, columns, vectors, coefficients):
    block_rows, per_row = columns.shape
    peers = lax.axis_size("rows")
    groups = lax.axis_size("vecs")
    total_blocks = block_rows * peers
    width = vectors.shape[1]
    shape = Shape(block_rows, per_row, width, groups)
    chunks = shape.chunks
    rows_at, vecs_at = lax.axis_index("rows"), lax.axis_index("vecs")
    up = [(i, (i + 1) % peers) for i in range(peers)]
    down = [(j, i) for i, j in up]

    def exchange(first, last):
        return lax.ppermute(last, "rows", up), lax.ppermute(first, "rows", down)

    chain = Chain()
    lanes = [slice(c * LANES, (c + 1) * LANES) for c in range(chunks)]
    halo = [exchange(vectors[:SIZE, l], vectors[-SIZE:, l]) for l in lanes]

    local = jnp.arange(block_rows, dtype=jnp.int32)
    offsets = (columns - (rows_at * block_rows + local)[:, None] + REACH) % total_blocks
    slots = (offsets + (local % REACH)[:, None]).reshape(-1)
    per_group = peers // groups
    piece = width // per_group
    wanted = rows_at ^ (vecs_at * per_group)
    levels = (peers - 1).bit_length()
    bits = [(vecs_at >> b) & 1 for b in range(shape.vec_bits)] + [(wanted >> b) & 1 for b in range(levels)]
    table = jnp.concatenate([slots, jnp.stack(bits).astype(jnp.int32)])

    parts_h, vectors, parts = prepare(shape, chain, table, hamiltonian, vectors)
    common = (table, coefficients, parts_h, vectors)

    terms, older, inner, core_sends, got_core = ([None] * chunks for _ in range(5))
    core = rims = ends = filtered = None
    wide = (None, None)

    def swapped(x, distance):
        return lax.ppermute(x, "vecs", [(i, i ^ distance) for i in range(groups)])

    def received(sends):
        return {d: swapped(sends[d.bit_length() - 2], d) for d in range(2, groups, 2)}

    def forwarded(got):
        out = {}
        for d, rows in got.items():
            out[d], out[d + 1] = rows, swapped(rows, 1)
        return out

    def inside(step, c, padded=None, following=None):
        nonlocal core, rims, filtered
        q = older[c] and older[c][1]
        whole = None
        if step == 1:
            inner[c] = interior(1, c, shape, chain, common, padded, None, following)
        elif step < ORDER - 1:
            inner[c] = interior(step, c, shape, chain, common, parts[c], q, None)
        elif step == ORDER - 1:
            inner[c], core, core_sends[c], whole = interior_and_core(
                step, c, shape, chain, common, parts[c], q, terms[c][1], core, filtered
            )
        else:
            rims, whole = ring(step, c, shape, chain, common, parts[c], q, rims, filtered)
        filtered = filtered if whole is None else whole

    for step in range(1, ORDER):
        for c in range(chunks):
            if step > 1 and (step > 2 or c > 0):
                inside(step, c)
            q = older[c] and (older[c][0], older[c][2])
            late = step == ORDER - 1
            low, high, padded, following, both = border(
                step, c, shape, chain, common, halo[c], q, parts[c], inner[c] and inner[c][1], wide if late else ()
            )
            if late:
                got_core[c], wide = received(core_sends[c]), both
            else:
                halo[c] = exchange(low, high)
            if step == 1:
                inside(1, c, padded, following)
                following = inner[c][1]
            older[c], terms[c], parts[c] = terms[c], (low, inner[c][0], high), following
        if step == 1:
            inside(2, 0)
    last_halo = exchange(*wide)
    for c in range(chunks):
        inside(ORDER, c)
    got_rims = received(rims[2:])
    near = rims[1]
    for c in range(chunks):
        q = (older[c][0], older[c][2])
        got = [[rows[d] for rows in got_core] for d in range(2, groups, 2)] if c == 0 else []
        passed = [core[1], *got_rims.values()] if c == chunks - 1 else []
        near, ends, joined, passed, filtered = last_border(
            ORDER, c, shape, chain, common, last_halo, q, parts[c], near, ends, filtered, got, passed
        )
        if c == 0:
            all_core = {2 * n + 2: rows for n, rows in enumerate(joined)}
    near_core = passed[0]
    got_core = forwarded(all_core)
    got_rims = forwarded(dict(zip(got_rims, passed[1:])))
    got_ends = received(ends[1:])

    kinds, far = tuple(range(min(2, groups))), tuple(range(2, groups))
    swaps = [[(i, i ^ (1 << level)) for i in range(peers)] for level in range(levels)]
    sums = gram_sums(shape, chain, table, kinds, [core[0]], {1: [([swapped(near_core, 1)], 0)]}, None, 0)
    near = swapped(near, 1)
    near_pair = gram_sums(shape, chain, table, kinds, [rims[0], ends[0]], {1: [([near], 0), ([near], SIZE)]}, sums, piece)
    shares = [(near_pair[0], lax.ppermute(near_pair[1], "rows", swaps[0]))]
    if far:
        arrived = {d: [([got_core[d]], 0), ([got_rims[d]], 0)] for d in far}
        sums = gram_sums(shape, chain, table, far, [core[0], rims[0]], arrived, None, 0)
        keep, send, rows = fold(shape, chain, table, 1, shares, got_ends.values())
        shares = [(keep, lax.ppermute(send, "rows", swaps[1]))]
        got_ends = forwarded(dict(zip(got_ends, rows)))
        far_pair = gram_sums(shape, chain, table, far, [ends[0]], {d: [([got_ends[d]], 0)] for d in far}, sums, piece)
        shares.append((far_pair[0], lax.ppermute(far_pair[1], "rows", swaps[0])))
    for level in range(1, levels):
        ahead = level == 1 and len(shares) > 1
        if shares[0][0].shape[0] == 1 and not ahead:
            keep, send, _ = fold(shape, chain, table, level, shares)
            shares = [(keep, lax.ppermute(send, "rows", swaps[level]))]
            continue
        for n in range(int(ahead), len(shares)):
            keep, send, _ = fold(shape, chain, table, level, [shares[n]])
            shares[n] = (keep, lax.ppermute(send, "rows", swaps[level]))
    share = (shares[0][0] + shares[0][1]).reshape(per_group, piece, piece)

    turned = []
    for n in range(per_group):
        pairs = []
        for i in range(peers):
            for g in range(groups):
                to = (g * per_group + (i + n) % per_group) * groups + i // per_group
                pairs.append((i * groups + g, to))
        sent = lax.dynamic_index_in_dim(share, (rows_at + n) % per_group, axis=0, keepdims=False)
        turned.append(lax.ppermute(sent, ("rows", "vecs"), pairs).T)
    turned = jnp.stack(turned)
    gram = []
    for t in range(per_group):
        gram.append(share[t] + lax.dynamic_index_in_dim(turned, (rows_at - t) % per_group, axis=0, keepdims=False))
    gram = jnp.concatenate(gram, axis=0) / (total_blocks * BLOCK)
    return filtered, gram


def solution(mesh):
    return jax.shard_map(
        on_device,
        mesh=mesh,
        in_specs=(P("rows", None, None, None), P("rows", None), P("rows", "vecs"), P()),
        out_specs=(P("rows", "vecs"), P("vecs", "rows")),
        check_vma=False,
    )
```

```python
import functools

import jax
import jax.numpy as jnp
from jax import lax
from jax.experimental import pallas as pl
from jax.experimental.pallas import tpu as pltpu
from jax.sharding import PartitionSpec as P

BLOCK = 128
REACH = 4
ORDER = 6
LANES = 128
SIZE = REACH * BLOCK
SPARE = 16
F32 = jnp.float32
BF16 = jnp.bfloat16
WHOLE = pl.BlockSpec(memory_space=pltpu.VMEM)
ANYWHERE = pl.BlockSpec(memory_space=pl.ANY)
SCALARS = pl.BlockSpec(memory_space=pltpu.SMEM)


def shaped(shape, dtype=F32):
    return jax.ShapeDtypeStruct(shape, dtype)


def cost(flops, moved):
    return pl.CostEstimate(flops=flops, bytes_accessed=moved, transcendentals=0)


class Call:
    def __init__(self, chain):
        self.chain = chain
        self.args, self.specs, self.outs, self.out_specs, self.aliases = [], [], [], [], {}

    def anywhere(self, *arrays):
        self.args += arrays
        self.specs += [ANYWHERE] * len(arrays)
        return self

    def scalars(self, *arrays):
        self.args += arrays
        self.specs += [SCALARS] * len(arrays)
        return self

    def reads(self, *arrays):
        self.args += arrays
        self.specs += [WHOLE] * len(arrays)
        return self

    def writes(self, shape, before=None, spec=WHOLE):
        if before is not None:
            self.aliases[len(self.args)] = len(self.outs)
            self.args.append(before)
            self.specs.append(spec)
        self.outs.append(shape)
        self.out_specs.append(spec)
        return self

    def passes(self, *arrays):
        for array in arrays:
            self.writes(shaped(array.shape, array.dtype), array, ANYWHERE)
        return self

    def __call__(self, body, name, estimate, scratch=(), mib=16):
        if self.chain.token is not None:
            self.anywhere(self.chain.token)
        self.writes(shaped((8, LANES)))
        count = len(self.args)

        def kernel(*refs):
            ins, outs = refs[:count], refs[count : count + len(self.outs)]
            outs[-1][...] = jnp.zeros((8, LANES), F32)
            body(ins, outs[:-1], refs[count + len(self.outs) :])

        *results, self.chain.token = pl.pallas_call(
            kernel,
            in_specs=self.specs,
            out_specs=self.out_specs,
            out_shape=self.outs,
            scratch_shapes=scratch,
            input_output_aliases=self.aliases,
            compiler_params=pltpu.CompilerParams(vmem_limit_bytes=mib * 1024 * 1024),
            cost_estimate=estimate,
            name=name,
        )(*self.args)
        return results


class Chain:
    token = None


def two_parts(x):
    high = x.astype(BF16)
    low = (x - high.astype(F32)).astype(BF16)
    return high, low


def put_parts(ref, start, value):
    high, low = two_parts(value)
    ref[pl.ds(start, value.shape[0]), :LANES] = high
    ref[pl.ds(start, value.shape[0]), LANES:] = low


def prepare(shape, chain, table, hamiltonian, vectors):
    rows, per_row = hamiltonian.shape[:2]
    strips, slots = rows // REACH, 4
    far = [pltpu.with_memory_space_constraint(x, pltpu.HBM) for x in (hamiltonian, vectors)]
    call = Call(chain).scalars(table).anywhere(*far)
    call.writes(shaped((rows, 2 * BLOCK, per_row * BLOCK), BF16)).writes(shaped(vectors.shape))
    for _ in range(shape.chunks):
        call.writes(shaped((vectors.shape[0] + 2 * SIZE, 2 * LANES), BF16))

    def body(ins, outs, scratch):
        h_ref, v_ref = ins[1], ins[2]
        parts_h, copy_v = outs[:2]
        held, sems, v_sem = scratch

        def fetch(g):
            slot = lax.rem(g, slots)
            return pltpu.make_async_copy(h_ref.at[pl.ds(g * REACH, REACH)], held.at[slot], sems.at[slot])

        def split(g, carry):
            slot = lax.rem(g, slots)
            fetch(g).wait()
            for r in range(REACH):
                for k in range(per_row):
                    high, low = two_parts(held[slot, r, k])
                    parts_h[g * REACH + r, :BLOCK, k * BLOCK : (k + 1) * BLOCK] = high
                    parts_h[g * REACH + r, BLOCK:, k * BLOCK : (k + 1) * BLOCK] = low

            @pl.when(g + slots < strips)
            def _():
                fetch(g + slots).start()

            return carry

        def split_v(g, carry):
            at = pl.multiple_of(g * SIZE, SIZE)
            for c in range(shape.chunks):
                put_parts(outs[2 + c], pl.multiple_of(at + SIZE, SIZE), copy_v[pl.ds(at, SIZE), c * LANES : (c + 1) * LANES])
            return carry

        copy = pltpu.make_async_copy(v_ref, copy_v, v_sem)
        for g in range(min(slots, strips)):
            fetch(jnp.int32(g)).start()
        copy.start()
        lax.fori_loop(0, strips // 2, split, 0)
        copy.wait()
        lax.fori_loop(0, strips, split_v, 0)
        lax.fori_loop(strips // 2, strips, split, 0)

    scratch = [pltpu.VMEM((slots, REACH, *hamiltonian.shape[1:]), F32), pltpu.SemaphoreType.DMA((slots,)), pltpu.SemaphoreType.DMA]
    out = call(body, "prepare", cost(0, 8 * hamiltonian.size), scratch)
    return out[0], out[1], out[2:]


def scales(step, coef_ref):
    here, by = coef_ref[ORDER - step], 2.0
    if step == 1:
        by = 2.0 * coef_ref[ORDER]
    elif step == 2:
        here = here - coef_ref[ORDER]
    elif step == ORDER:
        by = 1.0
    return here, by


def new_rows(step, chunk, common, parts_ref, row, q):
    table_ref, coef_ref, h_ref, v_ref = common
    per_row = h_ref.shape[2] // BLOCK
    base = (row // REACH) * REACH
    picked = []
    for k in range(per_row):
        start = pl.multiple_of((table_ref[row * per_row + k] + base) * BLOCK, BLOCK)
        picked.append(parts_ref[pl.ds(start, BLOCK), :])
    both = jnp.dot(h_ref[row], jnp.concatenate(picked, axis=0), preferred_element_type=F32)
    top, bottom = both[:BLOCK], both[BLOCK:]
    total = top[:, :LANES] + ((top[:, LANES:] + bottom[:, :LANES]) + bottom[:, LANES:])
    here, by = scales(step, coef_ref)
    whole = pl.ds(pl.multiple_of(row * BLOCK, BLOCK), BLOCK)
    value = here * v_ref[whole, chunk * LANES : (chunk + 1) * LANES] + by * total
    return value if q is None else value - q


def unrolled(first, count, one):
    unroll = max(n for n in range(1, 13) if count % n == 0)

    def some(i, carry):
        for u in range(unroll):
            one(first + i * unroll + u)
        return carry

    lax.fori_loop(0, count // unroll, some, 0)


def at_rows(block, size=BLOCK):
    return pl.ds(pl.multiple_of(block * BLOCK, BLOCK), size)


class Shape:
    def __init__(self, block_rows, per_row, width, groups):
        self.rows = block_rows
        self.inner = block_rows - 2 * REACH
        self.core = block_rows - 4 * REACH
        self.chunks = width // LANES
        self.width = width
        self.vec_bits = (groups - 1).bit_length()
        self.bits_at = block_rows * per_row


def put_sends(shape, table_ref, source_ref, sends, lanes):
    half = source_ref.shape[0] // 2
    for b, ref, at in sends:
        other = 1 - table_ref[shape.bits_at + b]
        rows = pl.ds(pl.multiple_of(other * half, BLOCK), half)
        ref[at : at + half, lanes if ref.shape[1] == source_ref.shape[1] else slice(None)] = source_ref[rows, lanes]


def interior(step, chunk, shape, chain, common, parts, q):
    call = Call(chain).scalars(*common[:2]).reads(*common[2:], parts)
    if q is not None:
        call.reads(q)
    call.writes(shaped((shape.inner * BLOCK, LANES))).writes(shaped(parts.shape, BF16))

    def body(ins, outs, scratch):
        def one(row):
            old = None if q is None else ins[5][at_rows(row - REACH), :]
            value = new_rows(step, chunk, ins[:4], ins[4], row, old)
            outs[0][at_rows(row - REACH), :] = value
            put_parts(outs[1], pl.multiple_of((row + REACH) * BLOCK, BLOCK), value)

        unrolled(REACH, shape.inner, one)

    flops = 8 * shape.inner * BLOCK * LANES * common[2].shape[2]
    return call(body, "interior", cost(flops, 8 * common[2].size))


def core_rows(step, chunk, shape, chain, common, parts, inner, q, mid, before):
    last = chunk == shape.chunks - 1
    call = Call(chain).scalars(*common[:2]).reads(*common[2:], parts, mid)
    if inner:
        call.reads(q).writes(shaped((shape.inner * BLOCK, LANES))).writes(shaped(parts.shape, BF16))
    core, out_at = shape.core * BLOCK, len(call.outs)
    before = before or [None, None]
    call.writes(shaped((core, shape.width)), before[0]).writes(shaped((core // 2, shape.width)), before[1])
    spare = SPARE if last else core // 8
    for _ in range(1, shape.vec_bits):
        call.writes(shaped((core // 2 + spare, LANES)))
    if last:
        call.writes(shaped((shape.rows * BLOCK, shape.width)), None, ANYWHERE)
    lanes = slice(chunk * LANES, (chunk + 1) * LANES)

    def body(ins, outs, scratch):
        term = outs[1] if inner else ins[4]
        result = outs[out_at]

        def one(row):
            value = new_rows(step - 1, chunk, ins[:4], ins[4], row, ins[6][at_rows(row - REACH), :])
            outs[0][at_rows(row - REACH), :] = value
            put_parts(term, pl.multiple_of((row + REACH) * BLOCK, BLOCK), value)

        def two(row):
            old = ins[5][at_rows(row - REACH), :]
            result[at_rows(row - 2 * REACH), lanes] = new_rows(step, chunk, ins[:4], term, row, old)

        if inner:
            unrolled(REACH, shape.inner, one)
        unrolled(2 * REACH, shape.core, two)
        if last:
            copy = pltpu.make_async_copy(result, outs[-1].at[pl.ds(2 * SIZE, core)], scratch[0])
            copy.start()
        put_sends(shape, ins[0], result, [(b, outs[out_at + 1 + b], 0) for b in range(shape.vec_bits)], lanes)
        if last:
            copy.wait()

    out = call(body, "core_rows", cost(0, 0), [pltpu.SemaphoreType.DMA] if last else [])
    rest = out[out_at:]
    return out[:out_at], rest[:2], rest[2 : 1 + shape.vec_bits], rest[-1] if last else None


def ring(step, chunk, shape, chain, common, parts, mid, before, filtered):
    last = chunk == shape.chunks - 1
    call = Call(chain).scalars(*common[:2]).reads(*common[2:], parts, mid)
    before = before or [None] * (1 + shape.vec_bits)
    for n, one_before in enumerate(before):
        call.writes(shaped((2 * SIZE if n < 2 else SIZE, shape.width)), one_before)
    if last:
        call.writes(shaped(filtered.shape), filtered, ANYWHERE)
    lanes = slice(chunk * LANES, (chunk + 1) * LANES)

    def body(ins, outs, scratch):
        copies = []
        for side, first in enumerate((REACH, shape.rows - 2 * REACH)):
            for r in range(REACH):
                row = first + r
                old = ins[5][at_rows(row - REACH), :]
                rows = pl.ds((side * REACH + r) * BLOCK, BLOCK)
                outs[0][rows, lanes] = new_rows(step, chunk, ins[:4], ins[4], row, old)
            if last:
                source = outs[0].at[pl.ds(side * SIZE, SIZE)]
                copies.append(pltpu.make_async_copy(source, outs[-1].at[pl.ds(first * BLOCK, SIZE)], scratch[0].at[side]))
                copies[-1].start()
        put_sends(shape, ins[0], outs[0], [(b, outs[1 + b], 0) for b in range(shape.vec_bits)], lanes)
        for copy in copies:
            copy.wait()

    out = call(body, "ring", cost(0, 0), [pltpu.SemaphoreType.DMA((2,))] if last else [])
    return out[: 1 + shape.vec_bits], out[-1] if last else None


def border(step, chunk, shape, chain, common, halo, q, parts, following, joined=None):
    call = Call(chain).scalars(*common[:2]).reads(*common[2:], *halo)
    if q is not None:
        call.reads(*q)
    strip = shaped((SIZE, LANES))
    call.writes(shaped(parts.shape, BF16), parts).writes(shaped(parts.shape, BF16), following)
    call.writes(strip).writes(strip)
    wide_at = len(call.outs)
    for before in joined or ():
        call.writes(shaped((SIZE + SPARE, shape.width)), before)
    lanes = slice(chunk * LANES, (chunk + 1) * LANES)

    def body(ins, outs, scratch):
        put_parts(outs[0], 0, ins[4][...])
        put_parts(outs[0], (shape.rows + REACH) * BLOCK, ins[5][...])
        for side, first in enumerate((0, shape.rows - REACH)):
            for r in range(REACH):
                rows = slice(r * BLOCK, (r + 1) * BLOCK)
                old = None if q is None else ins[6 + side][rows]
                value = new_rows(step, chunk, ins[:4], outs[0], first + r, old)
                outs[2 + side][rows] = value
                if joined:
                    outs[wide_at + side][rows, lanes] = value
                put_parts(outs[1], (first + r + REACH) * BLOCK, value)

    flops = 16 * SIZE * LANES * common[2].shape[2]
    _, following, low, high, *both = call(body, "border", cost(flops, 4 * common[2].size))
    return low, high, following, both


def last_border(step, chunk, shape, chain, common, halo, q, parts, near, before, filtered, got, passed):
    last = chunk == shape.chunks - 1
    call = Call(chain).scalars(*common[:2]).reads(*common[2:], *halo, *q)
    got_at = len(call.args)
    for arrays in got:
        call.reads(*arrays)
    call.writes(shaped(parts.shape, BF16), parts).writes(shaped(near.shape), near)
    before = before or [None] * shape.vec_bits
    for n, one_before in enumerate(before):
        call.writes(shaped((SIZE if n else 2 * SIZE, shape.width)), one_before)
    got_to = len(call.outs)
    for arrays in got:
        call.writes(shaped((shape.core * BLOCK // 2, shape.width)))
    call.passes(*passed)
    if last:
        call.writes(shaped(filtered.shape), filtered, ANYWHERE)
    lanes = slice(chunk * LANES, (chunk + 1) * LANES)

    def body(ins, outs, scratch):
        copies = []
        put_parts(outs[0], 0, ins[4][:SIZE, lanes])
        put_parts(outs[0], (shape.rows + REACH) * BLOCK, ins[5][:SIZE, lanes])
        for side, first in enumerate((0, shape.rows - REACH)):
            for r in range(REACH):
                old = ins[6 + side][r * BLOCK : (r + 1) * BLOCK]
                rows = pl.ds((side * REACH + r) * BLOCK, BLOCK)
                outs[2][rows, lanes] = new_rows(step, chunk, ins[:4], outs[0], first + r, old)
            if last:
                source = outs[2].at[pl.ds(side * SIZE, SIZE)]
                copies.append(pltpu.make_async_copy(source, outs[-1].at[pl.ds(first * BLOCK, SIZE)], scratch[0].at[side]))
                copies[-1].start()
        sends = [(0, outs[1], SIZE)] + [(b, outs[2 + b], 0) for b in range(1, shape.vec_bits)]
        put_sends(shape, ins[0], outs[2], sends, lanes)
        for n, arrays in enumerate(got):
            for c in range(len(arrays)):
                rows = slice(0, shape.core * BLOCK // 2)
                outs[got_to + n][:, c * LANES : (c + 1) * LANES] = ins[got_at + n * len(arrays) + c][rows]
        for copy in copies:
            copy.wait()

    out = call(body, "last_border", cost(0, 0), [pltpu.SemaphoreType.DMA((2,))] if last else [])
    joined, passed = out[got_to : got_to + len(got)], out[got_to + len(got) :][: len(passed)]
    return out[1], out[2 : 2 + shape.vec_bits], joined, passed, out[-1] if last else filtered


def gram_sums(shape, chain, table, kinds, own, got, before, piece):
    width = shape.width
    call = Call(chain).scalars(table).reads(*own)
    places = {}
    for d in kinds:
        if d:
            for n, (arrays, offset) in enumerate(got[d]):
                places[d, n] = (len(call.args), len(arrays), offset)
                call.reads(*arrays)
    before_at = len(call.args)
    if before is not None:
        call.reads(before)
    if piece:
        kept = shaped((len(kinds) * width // piece // 2, width, piece))
        call.writes(kept).writes(kept)
    else:
        call.writes(shaped((len(kinds), width, width)))

    def products(left, right):
        total = jnp.dot(left[0], right[1], preferred_element_type=F32)
        total += jnp.dot(left[1], right[0], preferred_element_type=F32)
        return total + jnp.dot(left[0], right[0], preferred_element_type=F32)

    def body(ins, outs, scratch):
        table_ref = ins[0]
        totals = [ins[before_at][n] if before is not None else jnp.zeros((width, width), F32) for n in range(len(kinds))]
        for n in range(len(own)):
            ref = ins[1 + n]
            half = ref.shape[0] // 2
            for at in range(0, half, SIZE):
                sides = [ref[at : at + SIZE], ref[half + at : half + at + SIZE]]
                chosen = {}
                for m, d in enumerate(kinds):
                    if d == 0:
                        for side in sides:
                            totals[m] += 0.5 * products(two_parts(side.T), two_parts(side))
                        continue
                    b = d.bit_length() - 1
                    if b not in chosen:
                        first = table_ref[shape.bits_at + b] == 0
                        chosen[b] = two_parts(jnp.where(first, sides[0], sides[1]).T)
                    where, count, offset = places[d, n]
                    other = [ins[where + c][offset + at : offset + at + SIZE] for c in range(count)]
                    other = other[0] if count == 1 else jnp.concatenate(other, axis=1)
                    totals[m] += products(chosen[b], two_parts(other))
        for m, total in enumerate(totals):
            if not piece:
                outs[0][m] = total
                continue
            pairs = width // piece // 2
            even = table_ref[shape.bits_at + shape.vec_bits] == 0
            for t in range(pairs):
                one = total[:, 2 * t * piece : (2 * t + 1) * piece]
                two = total[:, (2 * t + 1) * piece : (2 * t + 2) * piece]
                outs[0][m * pairs + t] = jnp.where(even, one, two)
                outs[1][m * pairs + t] = jnp.where(even, two, one)

    rows = sum(a.shape[0] for a in own)
    flops = 3 * rows * width * width * (len(kinds) + 1)
    out = call(body, "gram_sums", cost(flops, 8 * rows * width))
    return out if piece else out[0]


def fold(shape, chain, table, level, pairs, passed=()):
    call = Call(chain).scalars(table)
    count = 0
    for keep, got in pairs:
        call.reads(keep, got)
        count += keep.shape[0]
    half = shaped((count // 2, *pairs[0][0].shape[1:]))
    call.writes(half).writes(half).passes(*passed)

    def body(ins, outs, scratch):
        even = ins[0][shape.bits_at + shape.vec_bits + level] == 0
        sums = []
        for n in range(len(pairs)):
            for m in range(ins[1 + 2 * n].shape[0]):
                sums.append(ins[1 + 2 * n][m] + ins[2 + 2 * n][m])
        for n in range(count // 2):
            outs[0][n] = jnp.where(even, sums[2 * n], sums[2 * n + 1])
            outs[1][n] = jnp.where(even, sums[2 * n + 1], sums[2 * n])

    keep, send, *passed = call(body, "fold", cost(0, 8 * count * pairs[0][0][0].size))
    return keep, send, passed


def on_device(hamiltonian, columns, vectors, coefficients):
    block_rows, per_row = columns.shape
    peers = lax.axis_size("rows")
    groups = lax.axis_size("vecs")
    total_blocks = block_rows * peers
    width = vectors.shape[1]
    shape = Shape(block_rows, per_row, width, groups)
    chunks = shape.chunks
    rows_at, vecs_at = lax.axis_index("rows"), lax.axis_index("vecs")
    up = [(i, (i + 1) % peers) for i in range(peers)]
    down = [(j, i) for i, j in up]

    def exchange(first, last):
        return lax.ppermute(last, "rows", up), lax.ppermute(first, "rows", down)

    chain = Chain()
    lanes = [slice(c * LANES, (c + 1) * LANES) for c in range(chunks)]
    halo = [exchange(vectors[:SIZE, l], vectors[-SIZE:, l]) for l in lanes]

    local = jnp.arange(block_rows, dtype=jnp.int32)
    offsets = (columns - (rows_at * block_rows + local)[:, None] + REACH) % total_blocks
    slots = (offsets + (local % REACH)[:, None]).reshape(-1)
    per_group = peers // groups
    piece = width // per_group
    wanted = rows_at ^ (vecs_at * per_group)
    levels = (peers - 1).bit_length()
    bits = [(vecs_at >> b) & 1 for b in range(shape.vec_bits)] + [(wanted >> b) & 1 for b in range(levels)]
    table = jnp.concatenate([slots, jnp.stack(bits).astype(jnp.int32)])

    parts_h, vectors, parts = prepare(shape, chain, table, hamiltonian, vectors)
    common = (table, coefficients, parts_h, vectors)

    terms, older, inner, core_sends = ([None] * chunks for _ in range(4))
    core = rims = ends = filtered = None
    wide = (None, None)

    def swapped(x, distance):
        return lax.ppermute(x, "vecs", [(i, i ^ distance) for i in range(groups)])

    def received(sends):
        return {d: swapped(sends[d.bit_length() - 2], d) for d in range(2, groups, 2)}

    def forwarded(got):
        out = {}
        for d, rows in got.items():
            out[d], out[d + 1] = rows, swapped(rows, 1)
        return out

    def inside(step, c):
        nonlocal core, rims, filtered
        q = older[c] and older[c][1]
        whole = None
        if step < ORDER - 1 or (step == ORDER - 1 and c == chunks - 1):
            inner[c] = interior(step, c, shape, chain, common, parts[c], q)
        elif step == ORDER - 1:
            inner[c], core, core_sends[c], _ = core_rows(
                ORDER, c, shape, chain, common, parts[c], True, q, terms[c][1], core
            )
        else:
            rims, whole = ring(step, c, shape, chain, common, parts[c], q, rims, filtered)
        filtered = filtered if whole is None else whole

    for step in range(1, ORDER):
        for c in range(chunks):
            inside(step, c)
            q = older[c] and (older[c][0], older[c][2])
            late = step == ORDER - 1
            low, high, following, both = border(
                step, c, shape, chain, common, halo[c], q, parts[c], inner[c][1], wide if late else ()
            )
            if late:
                wide = both
            else:
                halo[c] = exchange(low, high)
            older[c], terms[c], parts[c] = terms[c], (low, inner[c][0], high), following
    last_halo = exchange(*wide)
    _, core, core_sends[-1], filtered = core_rows(
        ORDER, chunks - 1, shape, chain, common, parts[-1], False, None, older[-1][1], core
    )
    got_core = [received(sends) for sends in core_sends]
    for c in range(chunks):
        inside(ORDER, c)
    got_rims = received(rims[2:])
    near = rims[1]
    for c in range(chunks):
        q = (older[c][0], older[c][2])
        got = [[rows[d] for rows in got_core] for d in range(2, groups, 2)] if c == 0 else []
        passed = [core[1], *got_rims.values()] if c == chunks - 1 else []
        near, ends, joined, passed, filtered = last_border(
            ORDER, c, shape, chain, common, last_halo, q, parts[c], near, ends, filtered, got, passed
        )
        if c == 0:
            all_core = {2 * n + 2: rows for n, rows in enumerate(joined)}
    near_core = passed[0]
    got_core = forwarded(all_core)
    got_rims = forwarded(dict(zip(got_rims, passed[1:])))
    got_ends = received(ends[1:])

    kinds, far = tuple(range(min(2, groups))), tuple(range(2, groups))
    swaps = [[(i, i ^ (1 << level)) for i in range(peers)] for level in range(levels)]
    sums = gram_sums(shape, chain, table, kinds, [core[0]], {1: [([swapped(near_core, 1)], 0)]}, None, 0)
    near = swapped(near, 1)
    near_pair = gram_sums(shape, chain, table, kinds, [rims[0], ends[0]], {1: [([near], 0), ([near], SIZE)]}, sums, piece)
    shares = [(near_pair[0], lax.ppermute(near_pair[1], "rows", swaps[0]))]
    if far:
        arrived = {d: [([got_core[d]], 0), ([got_rims[d]], 0)] for d in far}
        sums = gram_sums(shape, chain, table, far, [core[0], rims[0]], arrived, None, 0)
        keep, send, rows = fold(shape, chain, table, 1, shares, got_ends.values())
        shares = [(keep, lax.ppermute(send, "rows", swaps[1]))]
        got_ends = forwarded(dict(zip(got_ends, rows)))
        far_pair = gram_sums(shape, chain, table, far, [ends[0]], {d: [([got_ends[d]], 0)] for d in far}, sums, piece)
        shares.append((far_pair[0], lax.ppermute(far_pair[1], "rows", swaps[0])))
    for level in range(1, levels):
        ahead = level == 1 and len(shares) > 1
        if shares[0][0].shape[0] == 1 and not ahead:
            keep, send, _ = fold(shape, chain, table, level, shares)
            shares = [(keep, lax.ppermute(send, "rows", swaps[level]))]
            continue
        for n in range(int(ahead), len(shares)):
            keep, send, _ = fold(shape, chain, table, level, [shares[n]])
            shares[n] = (keep, lax.ppermute(send, "rows", swaps[level]))
    share = (shares[0][0] + shares[0][1]).reshape(per_group, piece, piece)

    turned = []
    for n in range(per_group):
        pairs = []
        for i in range(peers):
            for g in range(groups):
                to = (g * per_group + (i + n) % per_group) * groups + i // per_group
                pairs.append((i * groups + g, to))
        sent = lax.dynamic_index_in_dim(share, (rows_at + n) % per_group, axis=0, keepdims=False)
        turned.append(lax.ppermute(sent, ("rows", "vecs"), pairs).T)
    turned = jnp.stack(turned)
    gram = []
    for t in range(per_group):
        gram.append(share[t] + lax.dynamic_index_in_dim(turned, (rows_at - t) % per_group, axis=0, keepdims=False))
    gram = jnp.concatenate(gram, axis=0) / (total_blocks * BLOCK)
    return filtered, gram


def solution(mesh):
    return jax.shard_map(
        on_device,
        mesh=mesh,
        in_specs=(P("rows", None, None, None), P("rows", None), P("rows", "vecs"), P()),
        out_specs=(P("rows", "vecs"), P("vecs", "rows")),
        check_vma=False,
    )
```

```python
import functools

import jax
import jax.numpy as jnp
from jax import lax
from jax.experimental import pallas as pl
from jax.experimental.pallas import tpu as pltpu
from jax.sharding import PartitionSpec as P

BLOCK = 128
REACH = 4
ORDER = 6
LANES = 128
SIZE = REACH * BLOCK
SPARE = 32
F32 = jnp.float32
BF16 = jnp.bfloat16
WHOLE = pl.BlockSpec(memory_space=pltpu.VMEM)
ANYWHERE = pl.BlockSpec(memory_space=pl.ANY)
SCALARS = pl.BlockSpec(memory_space=pltpu.SMEM)


def shaped(shape, dtype=F32):
    return jax.ShapeDtypeStruct(shape, dtype)


def cost(flops, moved):
    return pl.CostEstimate(flops=flops, bytes_accessed=moved, transcendentals=0)


class Call:
    def __init__(self, chain):
        self.chain = chain
        self.args, self.specs, self.outs, self.out_specs, self.aliases = [], [], [], [], {}

    def anywhere(self, *arrays):
        self.args += arrays
        self.specs += [ANYWHERE] * len(arrays)
        return self

    def scalars(self, *arrays):
        self.args += arrays
        self.specs += [SCALARS] * len(arrays)
        return self

    def reads(self, *arrays):
        self.args += arrays
        self.specs += [WHOLE] * len(arrays)
        return self

    def writes(self, shape, before=None, spec=WHOLE):
        if before is not None:
            self.aliases[len(self.args)] = len(self.outs)
            self.args.append(before)
            self.specs.append(spec)
        self.outs.append(shape)
        self.out_specs.append(spec)
        return self

    def passes(self, *arrays):
        for array in arrays:
            self.writes(shaped(array.shape, array.dtype), array, ANYWHERE)
        return self

    def __call__(self, body, name, estimate, scratch=(), mib=16):
        if self.chain.token is not None:
            self.anywhere(self.chain.token)
        self.writes(shaped((8, LANES)))
        count = len(self.args)

        def kernel(*refs):
            ins, outs = refs[:count], refs[count : count + len(self.outs)]
            outs[-1][...] = jnp.zeros((8, LANES), F32)
            body(ins, outs[:-1], refs[count + len(self.outs) :])

        *results, self.chain.token = pl.pallas_call(
            kernel,
            in_specs=self.specs,
            out_specs=self.out_specs,
            out_shape=self.outs,
            scratch_shapes=scratch,
            input_output_aliases=self.aliases,
            compiler_params=pltpu.CompilerParams(vmem_limit_bytes=mib * 1024 * 1024),
            cost_estimate=estimate,
            name=name,
        )(*self.args)
        return results


class Chain:
    token = None


def two_parts(x):
    high = x.astype(BF16)
    low = (x - high.astype(F32)).astype(BF16)
    return high, low


def put_parts(ref, start, value):
    high, low = two_parts(value)
    ref[pl.ds(start, value.shape[0]), :LANES] = high
    ref[pl.ds(start, value.shape[0]), LANES:] = low


def prepare(shape, chain, table, hamiltonian, vectors):
    rows, per_row = hamiltonian.shape[:2]
    strips, slots = rows // REACH, 4
    far = [pltpu.with_memory_space_constraint(x, pltpu.HBM) for x in (hamiltonian, vectors)]
    call = Call(chain).scalars(table).anywhere(*far)
    call.writes(shaped((rows, 2 * BLOCK, per_row * BLOCK), BF16)).writes(shaped(vectors.shape))
    for _ in range(shape.chunks):
        call.writes(shaped((vectors.shape[0] + 2 * SIZE, 2 * LANES), BF16))

    def body(ins, outs, scratch):
        h_ref, v_ref = ins[1], ins[2]
        parts_h, copy_v = outs[:2]
        held, sems, v_sem = scratch

        def fetch(g):
            slot = lax.rem(g, slots)
            return pltpu.make_async_copy(h_ref.at[pl.ds(g * REACH, REACH)], held.at[slot], sems.at[slot])

        def split(g, carry):
            slot = lax.rem(g, slots)
            fetch(g).wait()
            for r in range(REACH):
                for k in range(per_row):
                    high, low = two_parts(held[slot, r, k])
                    parts_h[g * REACH + r, :BLOCK, k * BLOCK : (k + 1) * BLOCK] = high
                    parts_h[g * REACH + r, BLOCK:, k * BLOCK : (k + 1) * BLOCK] = low

            @pl.when(g + slots < strips)
            def _():
                fetch(g + slots).start()

            return carry

        def split_v(g, carry):
            at = pl.multiple_of(g * SIZE, SIZE)
            for c in range(shape.chunks):
                put_parts(outs[2 + c], pl.multiple_of(at + SIZE, SIZE), copy_v[pl.ds(at, SIZE), c * LANES : (c + 1) * LANES])
            return carry

        copy = pltpu.make_async_copy(v_ref, copy_v, v_sem)
        for g in range(min(slots, strips)):
            fetch(jnp.int32(g)).start()
        copy.start()
        lax.fori_loop(0, strips // 2, split, 0)
        copy.wait()
        lax.fori_loop(0, strips, split_v, 0)
        lax.fori_loop(strips // 2, strips, split, 0)

    scratch = [pltpu.VMEM((slots, REACH, *hamiltonian.shape[1:]), F32), pltpu.SemaphoreType.DMA((slots,)), pltpu.SemaphoreType.DMA]
    out = call(body, "prepare", cost(0, 8 * hamiltonian.size), scratch)
    return out[0], out[1], out[2:]


def scales(step, coef_ref):
    here, by = coef_ref[ORDER - step], 2.0
    if step == 1:
        by = 2.0 * coef_ref[ORDER]
    elif step == 2:
        here = here - coef_ref[ORDER]
    elif step == ORDER:
        by = 1.0
    return here, by


def new_rows(step, chunk, common, parts_ref, row, q):
    table_ref, coef_ref, h_ref, v_ref = common
    per_row = h_ref.shape[2] // BLOCK
    base = (row // REACH) * REACH
    picked = []
    for k in range(per_row):
        start = pl.multiple_of((table_ref[row * per_row + k] + base) * BLOCK, BLOCK)
        picked.append(parts_ref[pl.ds(start, BLOCK), :])
    both = jnp.dot(h_ref[row], jnp.concatenate(picked, axis=0), preferred_element_type=F32)
    top, bottom = both[:BLOCK], both[BLOCK:]
    total = top[:, :LANES] + ((top[:, LANES:] + bottom[:, :LANES]) + bottom[:, LANES:])
    here, by = scales(step, coef_ref)
    whole = pl.ds(pl.multiple_of(row * BLOCK, BLOCK), BLOCK)
    value = here * v_ref[whole, chunk * LANES : (chunk + 1) * LANES] + by * total
    return value if q is None else value - q


def unrolled(first, count, one):
    unroll = max(n for n in range(1, 13) if count % n == 0)

    def some(i, carry):
        for u in range(unroll):
            one(first + i * unroll + u)
        return carry

    lax.fori_loop(0, count // unroll, some, 0)


def at_rows(block, size=BLOCK):
    return pl.ds(pl.multiple_of(block * BLOCK, BLOCK), size)


class Shape:
    def __init__(self, block_rows, per_row, width, groups):
        self.rows = block_rows
        self.inner = block_rows - 2 * REACH
        self.core = block_rows - 4 * REACH
        self.chunks = width // LANES
        self.width = width
        self.vec_bits = (groups - 1).bit_length()
        self.bits_at = block_rows * per_row


def put_sends(shape, table_ref, source_ref, sends, lanes):
    half = source_ref.shape[0] // 2
    for b, ref, at in sends:
        other = 1 - table_ref[shape.bits_at + b]
        rows = pl.ds(pl.multiple_of(other * half, BLOCK), half)
        ref[at : at + half, lanes if ref.shape[1] == source_ref.shape[1] else slice(None)] = source_ref[rows, lanes]


def interior(step, chunk, shape, chain, common, parts, q):
    call = Call(chain).scalars(*common[:2]).reads(*common[2:], parts)
    if q is not None:
        call.reads(q)
    call.writes(shaped((shape.inner * BLOCK, LANES))).writes(shaped(parts.shape, BF16))

    def body(ins, outs, scratch):
        def one(row):
            old = None if q is None else ins[5][at_rows(row - REACH), :]
            value = new_rows(step, chunk, ins[:4], ins[4], row, old)
            outs[0][at_rows(row - REACH), :] = value
            put_parts(outs[1], pl.multiple_of((row + REACH) * BLOCK, BLOCK), value)

        unrolled(REACH, shape.inner, one)

    flops = 8 * shape.inner * BLOCK * LANES * common[2].shape[2]
    return call(body, "interior", cost(flops, 8 * common[2].size))


def core_rows(step, chunk, shape, chain, common, parts, q, mid, before):
    call = Call(chain).scalars(*common[:2]).reads(*common[2:], parts, q, mid).writes(shaped(parts.shape, BF16))
    core = shape.core * BLOCK
    before = before or [None, None]
    call.writes(shaped((core, shape.width)), before[0]).writes(shaped((core // 2, shape.width)), before[1])
    for _ in range(1, shape.vec_bits):
        call.writes(shaped((core // 2 + (shape.chunks - chunk) * SPARE, LANES)))
    lanes = slice(chunk * LANES, (chunk + 1) * LANES)

    def body(ins, outs, scratch):
        def one(row):
            value = new_rows(step - 1, chunk, ins[:4], ins[4], row, ins[5][at_rows(row - REACH), :])
            put_parts(outs[0], pl.multiple_of((row + REACH) * BLOCK, BLOCK), value)

        def two(row):
            old = ins[6][at_rows(row - REACH), :]
            outs[1][at_rows(row - 2 * REACH), lanes] = new_rows(step, chunk, ins[:4], outs[0], row, old)

        unrolled(REACH, shape.inner, one)
        unrolled(2 * REACH, shape.core, two)
        put_sends(shape, ins[0], outs[1], [(b, outs[2 + b], 0) for b in range(shape.vec_bits)], lanes)

    out = call(body, "core_rows", cost(0, 0))
    return (None, out[0]), out[1:3], out[3:]


def ring(step, chunk, shape, chain, common, parts, mid, before):
    call = Call(chain).scalars(*common[:2]).reads(*common[2:], parts, mid)
    before = before or [None] * (1 + shape.vec_bits)
    for n, one_before in enumerate(before):
        call.writes(shaped((2 * SIZE if n < 2 else SIZE, shape.width)), one_before)
    lanes = slice(chunk * LANES, (chunk + 1) * LANES)

    def body(ins, outs, scratch):
        for side, first in enumerate((REACH, shape.rows - 2 * REACH)):
            for r in range(REACH):
                row = first + r
                old = ins[5][at_rows(row - REACH), :]
                rows = pl.ds((side * REACH + r) * BLOCK, BLOCK)
                outs[0][rows, lanes] = new_rows(step, chunk, ins[:4], ins[4], row, old)
        put_sends(shape, ins[0], outs[0], [(b, outs[1 + b], 0) for b in range(shape.vec_bits)], lanes)

    return call(body, "ring", cost(0, 0))


def border(step, chunk, shape, chain, common, halo, q, parts, following, joined=None):
    call = Call(chain).scalars(*common[:2]).reads(*common[2:], *halo)
    if q is not None:
        call.reads(*q)
    call.writes(shaped(parts.shape, BF16), parts).writes(shaped(parts.shape, BF16), following)
    for before in joined or (None, None):
        call.writes(shaped((SIZE, shape.width if joined else LANES)), before)
    lanes = slice(chunk * LANES, (chunk + 1) * LANES) if joined else slice(None)

    def body(ins, outs, scratch):
        put_parts(outs[0], 0, ins[4][...])
        put_parts(outs[0], (shape.rows + REACH) * BLOCK, ins[5][...])
        for side, first in enumerate((0, shape.rows - REACH)):
            for r in range(REACH):
                rows = slice(r * BLOCK, (r + 1) * BLOCK)
                old = None if q is None else ins[6 + side][rows]
                value = new_rows(step, chunk, ins[:4], outs[0], first + r, old)
                outs[2 + side][rows, lanes] = value
                put_parts(outs[1], (first + r + REACH) * BLOCK, value)

    flops = 16 * SIZE * LANES * common[2].shape[2]
    _, following, low, high = call(body, "border", cost(flops, 4 * common[2].size))
    return low, high, following


def last_border(step, chunk, shape, chain, common, halo, q, parts, near, before, got, passed):
    call = Call(chain).scalars(*common[:2]).reads(*common[2:], *halo, *q)
    got_at = len(call.args)
    for arrays in got:
        call.reads(*arrays)
    call.writes(shaped(parts.shape, BF16), parts).writes(shaped(near.shape), near)
    before = before or [None] * shape.vec_bits
    for n, one_before in enumerate(before):
        call.writes(shaped((SIZE if n else 2 * SIZE, shape.width)), one_before)
    got_to = len(call.outs)
    for arrays in got:
        call.writes(shaped((shape.core * BLOCK // 2, shape.width)))
    call.passes(*passed)
    lanes = slice(chunk * LANES, (chunk + 1) * LANES)

    def body(ins, outs, scratch):
        put_parts(outs[0], 0, ins[4][:SIZE, lanes])
        put_parts(outs[0], (shape.rows + REACH) * BLOCK, ins[5][:SIZE, lanes])
        for side, first in enumerate((0, shape.rows - REACH)):
            for r in range(REACH):
                old = ins[6 + side][r * BLOCK : (r + 1) * BLOCK]
                rows = pl.ds((side * REACH + r) * BLOCK, BLOCK)
                outs[2][rows, lanes] = new_rows(step, chunk, ins[:4], outs[0], first + r, old)
        sends = [(0, outs[1], SIZE)] + [(b, outs[2 + b], 0) for b in range(1, shape.vec_bits)]
        put_sends(shape, ins[0], outs[2], sends, lanes)
        for n, arrays in enumerate(got):
            for c in range(len(arrays)):
                rows = slice(0, shape.core * BLOCK // 2)
                outs[got_to + n][:, c * LANES : (c + 1) * LANES] = ins[got_at + n * len(arrays) + c][rows]

    out = call(body, "last_border", cost(0, 0))
    joined, passed = out[got_to : got_to + len(got)], out[got_to + len(got) :][: len(passed)]
    return out[1], out[2 : 2 + shape.vec_bits], joined, passed


def gram_sums(shape, chain, table, kinds, own, got, before, piece, result=()):
    width = shape.width
    call = Call(chain).scalars(table).reads(*own)
    places = {}
    for d in kinds:
        if d:
            for n, (arrays, offset) in enumerate(got[d]):
                places[d, n] = (len(call.args), len(arrays), offset)
                call.reads(*arrays)
    before_at = len(call.args)
    if before is not None:
        call.reads(before)
    if piece:
        kept = shaped((len(kinds) * width // piece // 2, width, piece))
        call.writes(kept).writes(kept)
    else:
        call.writes(shaped((len(kinds), width, width)))
    result_at = len(call.args)
    for array, *_ in result:
        call.reads(array)
    if result:
        call.writes(shaped((shape.rows * BLOCK, width)), None, ANYWHERE)

    def products(left, right):
        total = jnp.dot(left[0], right[1], preferred_element_type=F32)
        total += jnp.dot(left[1], right[0], preferred_element_type=F32)
        return total + jnp.dot(left[0], right[0], preferred_element_type=F32)

    def body(ins, outs, scratch):
        table_ref = ins[0]
        copies = []
        for n, (_, start, rows, to) in enumerate(result):
            source = ins[result_at + n].at[pl.ds(start, rows)]
            copies.append(pltpu.make_async_copy(source, outs[-1].at[pl.ds(to, rows)], scratch[0].at[n]))
            copies[-1].start()
        totals = [ins[before_at][n] if before is not None else jnp.zeros((width, width), F32) for n in range(len(kinds))]
        for n in range(len(own)):
            ref = ins[1 + n]
            half = ref.shape[0] // 2
            for at in range(0, half, SIZE):
                sides = [ref[at : at + SIZE], ref[half + at : half + at + SIZE]]
                chosen = {}
                for m, d in enumerate(kinds):
                    if d == 0:
                        for side in sides:
                            totals[m] += 0.5 * products(two_parts(side.T), two_parts(side))
                        continue
                    b = d.bit_length() - 1
                    if b not in chosen:
                        first = table_ref[shape.bits_at + b] == 0
                        chosen[b] = two_parts(jnp.where(first, sides[0], sides[1]).T)
                    where, count, offset = places[d, n]
                    other = [ins[where + c][offset + at : offset + at + SIZE] for c in range(count)]
                    other = other[0] if count == 1 else jnp.concatenate(other, axis=1)
                    totals[m] += products(chosen[b], two_parts(other))
        for m, total in enumerate(totals):
            if not piece:
                outs[0][m] = total
                continue
            pairs = width // piece // 2
            even = table_ref[shape.bits_at + shape.vec_bits] == 0
            for t in range(pairs):
                one = total[:, 2 * t * piece : (2 * t + 1) * piece]
                two = total[:, (2 * t + 1) * piece : (2 * t + 2) * piece]
                outs[0][m * pairs + t] = jnp.where(even, one, two)
                outs[1][m * pairs + t] = jnp.where(even, two, one)
        for copy in copies:
            copy.wait()

    rows = sum(a.shape[0] for a in own)
    flops = 3 * rows * width * width * (len(kinds) + 1)
    scratch = [pltpu.SemaphoreType.DMA((len(result),))] if result else []
    out = call(body, "gram_sums", cost(flops, 8 * rows * width), scratch)
    return out if piece else out[0]


def fold(shape, chain, table, level, pairs, passed=()):
    call = Call(chain).scalars(table)
    count = 0
    for keep, got in pairs:
        call.reads(keep, got)
        count += keep.shape[0]
    half = shaped((count // 2, *pairs[0][0].shape[1:]))
    call.writes(half).writes(half).passes(*passed)

    def body(ins, outs, scratch):
        even = ins[0][shape.bits_at + shape.vec_bits + level] == 0
        sums = []
        for n in range(len(pairs)):
            for m in range(ins[1 + 2 * n].shape[0]):
                sums.append(ins[1 + 2 * n][m] + ins[2 + 2 * n][m])
        for n in range(count // 2):
            outs[0][n] = jnp.where(even, sums[2 * n], sums[2 * n + 1])
            outs[1][n] = jnp.where(even, sums[2 * n + 1], sums[2 * n])

    keep, send, *passed = call(body, "fold", cost(0, 8 * count * pairs[0][0][0].size))
    return keep, send, passed


def on_device(hamiltonian, columns, vectors, coefficients):
    block_rows, per_row = columns.shape
    peers = lax.axis_size("rows")
    groups = lax.axis_size("vecs")
    total_blocks = block_rows * peers
    width = vectors.shape[1]
    shape = Shape(block_rows, per_row, width, groups)
    chunks = shape.chunks
    rows_at, vecs_at = lax.axis_index("rows"), lax.axis_index("vecs")
    up = [(i, (i + 1) % peers) for i in range(peers)]
    down = [(j, i) for i, j in up]

    def exchange(first, last):
        return lax.ppermute(last, "rows", up), lax.ppermute(first, "rows", down)

    chain = Chain()
    lanes = [slice(c * LANES, (c + 1) * LANES) for c in range(chunks)]
    halo = [exchange(vectors[:SIZE, l], vectors[-SIZE:, l]) for l in lanes]

    local = jnp.arange(block_rows, dtype=jnp.int32)
    offsets = (columns - (rows_at * block_rows + local)[:, None] + REACH) % total_blocks
    slots = (offsets + (local % REACH)[:, None]).reshape(-1)
    per_group = peers // groups
    piece = width // per_group
    wanted = rows_at ^ (vecs_at * per_group)
    levels = (peers - 1).bit_length()
    bits = [(vecs_at >> b) & 1 for b in range(shape.vec_bits)] + [(wanted >> b) & 1 for b in range(levels)]
    table = jnp.concatenate([slots, jnp.stack(bits).astype(jnp.int32)])

    parts_h, vectors, parts = prepare(shape, chain, table, hamiltonian, vectors)
    common = (table, coefficients, parts_h, vectors)

    terms, older, inner, core_sends = ([None] * chunks for _ in range(4))
    core = rims = ends = None
    wide = (None, None)

    def swapped(x, distance):
        return lax.ppermute(x, "vecs", [(i, i ^ distance) for i in range(groups)])

    def received(sends):
        return {d: swapped(sends[d.bit_length() - 2], d) for d in range(2, groups, 2)}

    def forwarded(got):
        out = {}
        for d, rows in got.items():
            out[d], out[d + 1] = rows, swapped(rows, 1)
        return out

    def inside(step, c):
        nonlocal core, rims
        q = older[c] and older[c][1]
        if step < ORDER - 1:
            inner[c] = interior(step, c, shape, chain, common, parts[c], q)
        elif step == ORDER - 1:
            inner[c], core, core_sends[c] = core_rows(ORDER, c, shape, chain, common, parts[c], q, terms[c][1], core)
        else:
            rims = ring(step, c, shape, chain, common, parts[c], q, rims)

    for step in range(1, ORDER):
        for c in range(chunks):
            inside(step, c)
            q = older[c] and (older[c][0], older[c][2])
            late = step == ORDER - 1
            low, high, following = border(
                step, c, shape, chain, common, halo[c], q, parts[c], inner[c][1], wide if late else ()
            )
            if late:
                wide = (low, high)
            else:
                halo[c] = exchange(low, high)
            older[c], terms[c], parts[c] = terms[c], (low, inner[c][0], high), following
    last_halo = exchange(*wide)
    got_core = [received(sends) for sends in core_sends]
    for c in range(chunks):
        inside(ORDER, c)
    got_rims = received(rims[2:])
    near = rims[1]
    for c in range(chunks):
        q = (older[c][0], older[c][2])
        got = [[rows[d] for rows in got_core] for d in range(2, groups, 2)] if c == 0 else []
        passed = [core[1], *got_rims.values()] if c == chunks - 1 else []
        near, ends, joined, passed = last_border(
            ORDER, c, shape, chain, common, last_halo, q, parts[c], near, ends, got, passed
        )
        if c == 0:
            all_core = {2 * n + 2: rows for n, rows in enumerate(joined)}
    near_core = passed[0]
    got_core = forwarded(all_core)
    got_rims = forwarded(dict(zip(got_rims, passed[1:])))
    got_ends = received(ends[1:])

    kinds, far = tuple(range(min(2, groups))), tuple(range(2, groups))
    swaps = [[(i, i ^ (1 << level)) for i in range(peers)] for level in range(levels)]
    sums = gram_sums(shape, chain, table, kinds, [core[0]], {1: [([swapped(near_core, 1)], 0)]}, None, 0)
    near = swapped(near, 1)
    last = block_rows * BLOCK - SIZE
    result = [(core[0], 0, core[0].shape[0], 2 * SIZE), (rims[0], 0, SIZE, SIZE), (rims[0], SIZE, SIZE, last - SIZE)]
    result += [(ends[0], 0, SIZE, 0), (ends[0], SIZE, SIZE, last)]
    arrived = {1: [([near], 0), ([near], SIZE)]}
    keep, send, filtered = gram_sums(shape, chain, table, kinds, [rims[0], ends[0]], arrived, sums, piece, result)
    shares = [(keep, lax.ppermute(send, "rows", swaps[0]))]
    if far:
        arrived = {d: [([got_core[d]], 0), ([got_rims[d]], 0)] for d in far}
        sums = gram_sums(shape, chain, table, far, [core[0], rims[0]], arrived, None, 0)
        keep, send, rows = fold(shape, chain, table, 1, shares, got_ends.values())
        shares = [(keep, lax.ppermute(send, "rows", swaps[1]))]
        got_ends = forwarded(dict(zip(got_ends, rows)))
        far_pair = gram_sums(shape, chain, table, far, [ends[0]], {d: [([got_ends[d]], 0)] for d in far}, sums, piece)
        shares.append((far_pair[0], lax.ppermute(far_pair[1], "rows", swaps[0])))
    for level in range(1, levels):
        ahead = level == 1 and len(shares) > 1
        if shares[0][0].shape[0] == 1 and not ahead:
            keep, send, _ = fold(shape, chain, table, level, shares)
            shares = [(keep, lax.ppermute(send, "rows", swaps[level]))]
            continue
        for n in range(int(ahead), len(shares)):
            keep, send, _ = fold(shape, chain, table, level, [shares[n]])
            shares[n] = (keep, lax.ppermute(send, "rows", swaps[level]))
    share = (shares[0][0] + shares[0][1]).reshape(per_group, piece, piece)

    turned = []
    for n in range(per_group):
        pairs = []
        for i in range(peers):
            for g in range(groups):
                to = (g * per_group + (i + n) % per_group) * groups + i // per_group
                pairs.append((i * groups + g, to))
        sent = lax.dynamic_index_in_dim(share, (rows_at + n) % per_group, axis=0, keepdims=False)
        turned.append(lax.ppermute(sent, ("rows", "vecs"), pairs).T)
    turned = jnp.stack(turned)
    gram = []
    for t in range(per_group):
        gram.append(share[t] + lax.dynamic_index_in_dim(turned, (rows_at - t) % per_group, axis=0, keepdims=False))
    gram = jnp.concatenate(gram, axis=0) / (total_blocks * BLOCK)
    return filtered, gram


def solution(mesh):
    return jax.shard_map(
        on_device,
        mesh=mesh,
        in_specs=(P("rows", None, None, None), P("rows", None), P("rows", "vecs"), P()),
        out_specs=(P("rows", "vecs"), P("vecs", "rows")),
        check_vma=False,
    )
```

```python
import functools

import jax
import jax.numpy as jnp
from jax import lax
from jax.experimental import pallas as pl
from jax.experimental.pallas import tpu as pltpu
from jax.sharding import PartitionSpec as P

BLOCK = 128
REACH = 4
ORDER = 6
LANES = 128
SIZE = REACH * BLOCK
SPARE = 32
F32 = jnp.float32
BF16 = jnp.bfloat16
WHOLE = pl.BlockSpec(memory_space=pltpu.VMEM)
ANYWHERE = pl.BlockSpec(memory_space=pl.ANY)
SCALARS = pl.BlockSpec(memory_space=pltpu.SMEM)


def shaped(shape, dtype=F32):
    return jax.ShapeDtypeStruct(shape, dtype)


def cost(flops, moved):
    return pl.CostEstimate(flops=flops, bytes_accessed=moved, transcendentals=0)


class Call:
    def __init__(self, chain):
        self.chain = chain
        self.args, self.specs, self.outs, self.out_specs, self.aliases = [], [], [], [], {}

    def anywhere(self, *arrays):
        self.args += arrays
        self.specs += [ANYWHERE] * len(arrays)
        return self

    def scalars(self, *arrays):
        self.args += arrays
        self.specs += [SCALARS] * len(arrays)
        return self

    def reads(self, *arrays):
        self.args += arrays
        self.specs += [WHOLE] * len(arrays)
        return self

    def writes(self, shape, before=None, spec=WHOLE):
        if before is not None:
            self.aliases[len(self.args)] = len(self.outs)
            self.args.append(before)
            self.specs.append(spec)
        self.outs.append(shape)
        self.out_specs.append(spec)
        return self

    def passes(self, *arrays):
        for array in arrays:
            self.writes(shaped(array.shape, array.dtype), array, ANYWHERE)
        return self

    def __call__(self, body, name, estimate, scratch=(), mib=16):
        if self.chain.token is not None:
            self.anywhere(self.chain.token)
        self.writes(shaped((8, LANES)))
        count = len(self.args)

        def kernel(*refs):
            ins, outs = refs[:count], refs[count : count + len(self.outs)]
            outs[-1][...] = jnp.zeros((8, LANES), F32)
            body(ins, outs[:-1], refs[count + len(self.outs) :])

        *results, self.chain.token = pl.pallas_call(
            kernel,
            in_specs=self.specs,
            out_specs=self.out_specs,
            out_shape=self.outs,
            scratch_shapes=scratch,
            input_output_aliases=self.aliases,
            compiler_params=pltpu.CompilerParams(vmem_limit_bytes=mib * 1024 * 1024),
            cost_estimate=estimate,
            name=name,
        )(*self.args)
        return results


class Chain:
    token = None


def two_parts(x):
    high = x.astype(BF16)
    low = (x - high.astype(F32)).astype(BF16)
    return high, low


def put_parts(ref, start, value):
    high, low = two_parts(value)
    ref[pl.ds(start, value.shape[0]), :LANES] = high
    ref[pl.ds(start, value.shape[0]), LANES:] = low


def prepare(shape, chain, table, hamiltonian, vectors):
    rows, per_row = hamiltonian.shape[:2]
    strips, slots = rows // REACH, 4
    far = [pltpu.with_memory_space_constraint(x, pltpu.HBM) for x in (hamiltonian, vectors)]
    call = Call(chain).scalars(table).anywhere(*far)
    call.writes(shaped((rows, 2 * BLOCK, per_row * BLOCK), BF16)).writes(shaped(vectors.shape))
    for _ in range(shape.chunks):
        call.writes(shaped((vectors.shape[0] + 2 * SIZE, 2 * LANES), BF16))

    def body(ins, outs, scratch):
        h_ref, v_ref = ins[1], ins[2]
        parts_h, copy_v = outs[:2]
        held, sems, v_sem = scratch

        def fetch(g):
            slot = lax.rem(g, slots)
            return pltpu.make_async_copy(h_ref.at[pl.ds(g * REACH, REACH)], held.at[slot], sems.at[slot])

        def split(g, carry):
            slot = lax.rem(g, slots)
            fetch(g).wait()
            for r in range(REACH):
                for k in range(per_row):
                    high, low = two_parts(held[slot, r, k])
                    parts_h[g * REACH + r, :BLOCK, k * BLOCK : (k + 1) * BLOCK] = high
                    parts_h[g * REACH + r, BLOCK:, k * BLOCK : (k + 1) * BLOCK] = low

            @pl.when(g + slots < strips)
            def _():
                fetch(g + slots).start()

            return carry

        def split_v(g, carry):
            at = pl.multiple_of(g * SIZE, SIZE)
            for c in range(shape.chunks):
                put_parts(outs[2 + c], pl.multiple_of(at + SIZE, SIZE), copy_v[pl.ds(at, SIZE), c * LANES : (c + 1) * LANES])
            return carry

        copy = pltpu.make_async_copy(v_ref, copy_v, v_sem)
        for g in range(min(slots, strips)):
            fetch(jnp.int32(g)).start()
        copy.start()
        lax.fori_loop(0, strips // 2, split, 0)
        copy.wait()
        lax.fori_loop(0, strips, split_v, 0)
        lax.fori_loop(strips // 2, strips, split, 0)

    scratch = [pltpu.VMEM((slots, REACH, *hamiltonian.shape[1:]), F32), pltpu.SemaphoreType.DMA((slots,)), pltpu.SemaphoreType.DMA]
    out = call(body, "prepare", cost(0, 8 * hamiltonian.size), scratch)
    return out[0], out[1], out[2:]


def scales(step, coef_ref):
    here, by = coef_ref[ORDER - step], 2.0
    if step == 1:
        by = 2.0 * coef_ref[ORDER]
    elif step == 2:
        here = here - coef_ref[ORDER]
    elif step == ORDER:
        by = 1.0
    return here, by


def new_rows(step, chunk, common, parts_ref, row, q):
    table_ref, coef_ref, h_ref, v_ref = common
    per_row = h_ref.shape[2] // BLOCK
    base = (row // REACH) * REACH
    picked = []
    for k in range(per_row):
        start = pl.multiple_of((table_ref[row * per_row + k] + base) * BLOCK, BLOCK)
        picked.append(parts_ref[pl.ds(start, BLOCK), :])
    both = jnp.dot(h_ref[row], jnp.concatenate(picked, axis=0), preferred_element_type=F32)
    top, bottom = both[:BLOCK], both[BLOCK:]
    total = top[:, :LANES] + ((top[:, LANES:] + bottom[:, :LANES]) + bottom[:, LANES:])
    here, by = scales(step, coef_ref)
    whole = pl.ds(pl.multiple_of(row * BLOCK, BLOCK), BLOCK)
    value = here * v_ref[whole, chunk * LANES : (chunk + 1) * LANES] + by * total
    return value if q is None else value - q


def unrolled(first, count, one):
    unroll = max(n for n in range(1, 13) if count % n == 0)

    def some(i, carry):
        for u in range(unroll):
            one(first + i * unroll + u)
        return carry

    lax.fori_loop(0, count // unroll, some, 0)


def at_rows(block, size=BLOCK):
    return pl.ds(pl.multiple_of(block * BLOCK, BLOCK), size)


class Shape:
    def __init__(self, block_rows, per_row, width, groups):
        self.rows = block_rows
        self.inner = block_rows - 2 * REACH
        self.core = block_rows - 4 * REACH
        self.chunks = width // LANES
        self.width = width
        self.vec_bits = (groups - 1).bit_length()
        self.bits_at = block_rows * per_row


def put_sends(shape, table_ref, source_ref, sends, lanes):
    half = source_ref.shape[0] // 2
    for b, ref, at in sends:
        other = 1 - table_ref[shape.bits_at + b]
        rows = pl.ds(pl.multiple_of(other * half, BLOCK), half)
        ref[at : at + half, lanes if ref.shape[1] == source_ref.shape[1] else slice(None)] = source_ref[rows, lanes]


def interior(step, chunk, shape, chain, common, parts, q):
    call = Call(chain).scalars(*common[:2]).reads(*common[2:], parts)
    if q is not None:
        call.reads(q)
    call.writes(shaped((shape.inner * BLOCK, LANES))).writes(shaped(parts.shape, BF16))

    def body(ins, outs, scratch):
        def one(row):
            old = None if q is None else ins[5][at_rows(row - REACH), :]
            value = new_rows(step, chunk, ins[:4], ins[4], row, old)
            outs[0][at_rows(row - REACH), :] = value
            put_parts(outs[1], pl.multiple_of((row + REACH) * BLOCK, BLOCK), value)

        unrolled(REACH, shape.inner, one)

    flops = 8 * shape.inner * BLOCK * LANES * common[2].shape[2]
    return call(body, "interior", cost(flops, 8 * common[2].size))


def core_rows(step, chunk, shape, chain, common, parts, q, mid, before):
    call = Call(chain).scalars(*common[:2]).reads(*common[2:], parts, q, mid).writes(shaped(parts.shape, BF16))
    core = shape.core * BLOCK
    before = before or [None, None]
    call.writes(shaped((core, shape.width)), before[0]).writes(shaped((core // 2, shape.width)), before[1])
    for _ in range(1, shape.vec_bits):
        call.writes(shaped((core // 2 + (shape.chunks - chunk) * SPARE, LANES)))
    lanes = slice(chunk * LANES, (chunk + 1) * LANES)

    def body(ins, outs, scratch):
        def one(row):
            value = new_rows(step - 1, chunk, ins[:4], ins[4], row, ins[5][at_rows(row - REACH), :])
            put_parts(outs[0], pl.multiple_of((row + REACH) * BLOCK, BLOCK), value)

        def two(row):
            old = ins[6][at_rows(row - REACH), :]
            outs[1][at_rows(row - 2 * REACH), lanes] = new_rows(step, chunk, ins[:4], outs[0], row, old)

        unrolled(REACH, shape.inner, one)
        unrolled(2 * REACH, shape.core, two)
        put_sends(shape, ins[0], outs[1], [(b, outs[2 + b], 0) for b in range(shape.vec_bits)], lanes)

    out = call(body, "core_rows", cost(0, 0))
    return (None, out[0]), out[1:3], out[3:]


def ring(step, chunk, shape, chain, common, parts, mid, before):
    call = Call(chain).scalars(*common[:2]).reads(*common[2:], parts, mid)
    before = before or [None] * (1 + shape.vec_bits)
    for n, one_before in enumerate(before):
        call.writes(shaped((2 * SIZE if n < 2 else SIZE, shape.width)), one_before)
    lanes = slice(chunk * LANES, (chunk + 1) * LANES)

    def body(ins, outs, scratch):
        for side, first in enumerate((REACH, shape.rows - 2 * REACH)):
            for r in range(REACH):
                row = first + r
                old = ins[5][at_rows(row - REACH), :]
                rows = pl.ds((side * REACH + r) * BLOCK, BLOCK)
                outs[0][rows, lanes] = new_rows(step, chunk, ins[:4], ins[4], row, old)
        put_sends(shape, ins[0], outs[0], [(b, outs[1 + b], 0) for b in range(shape.vec_bits)], lanes)

    return call(body, "ring", cost(0, 0))


def border(step, chunk, shape, chain, common, halo, q, parts, following, joined=None):
    call = Call(chain).scalars(*common[:2]).reads(*common[2:], *halo)
    if q is not None:
        call.reads(*q)
    call.writes(shaped(parts.shape, BF16), parts).writes(shaped(parts.shape, BF16), following)
    for before in joined or (None, None):
        call.writes(shaped((SIZE, shape.width if joined else LANES)), before)
    lanes = slice(chunk * LANES, (chunk + 1) * LANES) if joined else slice(None)

    def body(ins, outs, scratch):
        put_parts(outs[0], 0, ins[4][...])
        put_parts(outs[0], (shape.rows + REACH) * BLOCK, ins[5][...])
        for side, first in enumerate((0, shape.rows - REACH)):
            for r in range(REACH):
                rows = slice(r * BLOCK, (r + 1) * BLOCK)
                old = None if q is None else ins[6 + side][rows]
                value = new_rows(step, chunk, ins[:4], outs[0], first + r, old)
                outs[2 + side][rows, lanes] = value
                put_parts(outs[1], (first + r + REACH) * BLOCK, value)

    flops = 16 * SIZE * LANES * common[2].shape[2]
    _, following, low, high = call(body, "border", cost(flops, 4 * common[2].size))
    return low, high, following


def last_border(step, chunk, shape, chain, common, halo, q, parts, near, before, got, passed):
    call = Call(chain).scalars(*common[:2]).reads(*common[2:], *halo, *q)
    got_at = len(call.args)
    for arrays in got:
        call.reads(*arrays)
    call.writes(shaped(parts.shape, BF16), parts).writes(shaped(near.shape), near)
    before = before or [None] * shape.vec_bits
    for n, one_before in enumerate(before):
        call.writes(shaped((SIZE if n else 2 * SIZE, shape.width)), one_before)
    got_to = len(call.outs)
    for arrays in got:
        call.writes(shaped((shape.core * BLOCK // 2, shape.width)))
    call.passes(*passed)
    lanes = slice(chunk * LANES, (chunk + 1) * LANES)

    def body(ins, outs, scratch):
        put_parts(outs[0], 0, ins[4][:SIZE, lanes])
        put_parts(outs[0], (shape.rows + REACH) * BLOCK, ins[5][:SIZE, lanes])
        for side, first in enumerate((0, shape.rows - REACH)):
            for r in range(REACH):
                old = ins[6 + side][r * BLOCK : (r + 1) * BLOCK]
                rows = pl.ds((side * REACH + r) * BLOCK, BLOCK)
                outs[2][rows, lanes] = new_rows(step, chunk, ins[:4], outs[0], first + r, old)
        sends = [(0, outs[1], SIZE)] + [(b, outs[2 + b], 0) for b in range(1, shape.vec_bits)]
        put_sends(shape, ins[0], outs[2], sends, lanes)
        for n, arrays in enumerate(got):
            for c in range(len(arrays)):
                rows = slice(0, shape.core * BLOCK // 2)
                outs[got_to + n][:, c * LANES : (c + 1) * LANES] = ins[got_at + n * len(arrays) + c][rows]

    out = call(body, "last_border", cost(0, 0))
    joined, passed = out[got_to : got_to + len(got)], out[got_to + len(got) :][: len(passed)]
    return out[1], out[2 : 2 + shape.vec_bits], joined, passed


def gram_sums(shape, chain, table, kinds, own, got, before, piece, result=()):
    width = shape.width
    call = Call(chain).scalars(table).reads(*own)
    places = {}
    for d in kinds:
        if d:
            for n, (arrays, offset) in enumerate(got[d]):
                places[d, n] = (len(call.args), len(arrays), offset)
                call.reads(*arrays)
    before_at = len(call.args)
    if before is not None:
        call.reads(before)
    if piece:
        kept = shaped((len(kinds) * width // piece // 2, width, piece))
        call.writes(kept).writes(kept)
    else:
        call.writes(shaped((len(kinds), width, width)))
    result_at = len(call.args)
    for array, *_ in result:
        call.reads(array)
    if result:
        call.writes(shaped((shape.rows * BLOCK, width)), None, ANYWHERE)

    def products(left, right):
        total = jnp.dot(left[0], right[1], preferred_element_type=F32)
        total += jnp.dot(left[1], right[0], preferred_element_type=F32)
        return total + jnp.dot(left[0], right[0], preferred_element_type=F32)

    def body(ins, outs, scratch):
        table_ref = ins[0]
        copies = []
        for n, (_, start, rows, to) in enumerate(result):
            source = ins[result_at + n].at[pl.ds(start, rows)]
            copies.append(pltpu.make_async_copy(source, outs[-1].at[pl.ds(to, rows)], scratch[0].at[n]))
            copies[-1].start()
        totals = [ins[before_at][n] if before is not None else jnp.zeros((width, width), F32) for n in range(len(kinds))]
        for n in range(len(own)):
            ref = ins[1 + n]
            half = ref.shape[0] // 2
            for at in range(0, half, SIZE):
                sides = [ref[at : at + SIZE], ref[half + at : half + at + SIZE]]
                chosen = {}
                for m, d in enumerate(kinds):
                    if d == 0:
                        for side in sides:
                            totals[m] += 0.5 * products(two_parts(side.T), two_parts(side))
                        continue
                    b = d.bit_length() - 1
                    if b not in chosen:
                        first = table_ref[shape.bits_at + b] == 0
                        chosen[b] = two_parts(jnp.where(first, sides[0], sides[1]).T)
                    where, count, offset = places[d, n]
                    other = [ins[where + c][offset + at : offset + at + SIZE] for c in range(count)]
                    other = other[0] if count == 1 else jnp.concatenate(other, axis=1)
                    totals[m] += products(chosen[b], two_parts(other))
        for m, total in enumerate(totals):
            if not piece:
                outs[0][m] = total
                continue
            pairs = width // piece // 2
            even = table_ref[shape.bits_at + shape.vec_bits] == 0
            for t in range(pairs):
                one = total[:, 2 * t * piece : (2 * t + 1) * piece]
                two = total[:, (2 * t + 1) * piece : (2 * t + 2) * piece]
                outs[0][m * pairs + t] = jnp.where(even, one, two)
                outs[1][m * pairs + t] = jnp.where(even, two, one)
        for copy in copies:
            copy.wait()

    rows = sum(a.shape[0] for a in own)
    flops = 3 * rows * width * width * (len(kinds) + 1)
    scratch = [pltpu.SemaphoreType.DMA((len(result),))] if result else []
    out = call(body, "gram_sums", cost(flops, 8 * rows * width), scratch)
    return out if piece or result else out[0]


def fold(shape, chain, table, level, pairs, tiles=0, passed=()):
    call = Call(chain).scalars(table)
    count = 0
    for keep, got in pairs:
        call.reads(keep, got)
        count += keep.shape[0]
    half = shaped((count // 2, *pairs[0][0].shape[1:]))
    call.writes(half).writes(half)
    rows, columns = half.shape[1], half.shape[2]
    for _ in range(2 * tiles):
        call.writes(shaped((rows // tiles, columns)))
    call.passes(*passed)

    def body(ins, outs, scratch):
        bit_at = shape.bits_at + shape.vec_bits
        even = ins[0][bit_at + level] == 0
        sums = []
        for n in range(len(pairs)):
            for m in range(ins[1 + 2 * n].shape[0]):
                sums.append(ins[1 + 2 * n][m] + ins[2 + 2 * n][m])
        for n in range(count // 2):
            outs[0][n] = jnp.where(even, sums[2 * n], sums[2 * n + 1])
            outs[1][n] = jnp.where(even, sums[2 * n + 1], sums[2 * n])
        for n in range(tiles):
            number = lax.rem(ins[0][ins[0].shape[0] - 1] + n, tiles)
            at = pl.ds(pl.multiple_of(number * (rows // tiles), rows // tiles), rows // tiles)
            outs[2 + 2 * n][...] = outs[0][0, at, :]
            outs[3 + 2 * n][...] = outs[1][0, at, :]

    return call(body, "fold", cost(0, 8 * count * pairs[0][0][0].size))


def assemble(shape, chain, table, keep, direct, turned, scale):
    tiles = len(turned) // 2
    rows, columns = keep.shape[1:]
    size = rows // tiles
    call = Call(chain).scalars(table).reads(keep, direct, *turned).writes(shaped((rows, columns)))

    def body(ins, outs, scratch):
        number = ins[0][ins[0].shape[0] - 1]
        sums = [(ins[3 + 2 * n][...] + ins[4 + 2 * n][...]).T for n in range(tiles)]
        for t in range(tiles):
            which = lax.rem(number - t + tiles, tiles)
            tile = sums[0]
            for n in range(1, tiles):
                tile = jnp.where(which == n, sums[n], tile)
            at = slice(t * size, (t + 1) * size)
            outs[0][at] = (ins[1][0, at] + ins[2][0, at] + tile) * scale

    return call(body, "assemble", cost(0, 0))[0]


def on_device(hamiltonian, columns, vectors, coefficients):
    block_rows, per_row = columns.shape
    peers = lax.axis_size("rows")
    groups = lax.axis_size("vecs")
    total_blocks = block_rows * peers
    width = vectors.shape[1]
    shape = Shape(block_rows, per_row, width, groups)
    chunks = shape.chunks
    rows_at, vecs_at = lax.axis_index("rows"), lax.axis_index("vecs")
    up = [(i, (i + 1) % peers) for i in range(peers)]
    down = [(j, i) for i, j in up]

    def exchange(first, last):
        return lax.ppermute(last, "rows", up), lax.ppermute(first, "rows", down)

    chain = Chain()
    lanes = [slice(c * LANES, (c + 1) * LANES) for c in range(chunks)]
    halo = [exchange(vectors[:SIZE, l], vectors[-SIZE:, l]) for l in lanes]

    local = jnp.arange(block_rows, dtype=jnp.int32)
    offsets = (columns - (rows_at * block_rows + local)[:, None] + REACH) % total_blocks
    slots = (offsets + (local % REACH)[:, None]).reshape(-1)
    per_group = peers // groups
    piece = width // per_group
    wanted = rows_at ^ (vecs_at * per_group)
    levels = (peers - 1).bit_length()
    bits = [(vecs_at >> b) & 1 for b in range(shape.vec_bits)] + [(wanted >> b) & 1 for b in range(levels)]
    bits.append(rows_at % per_group)
    table = jnp.concatenate([slots, jnp.stack(bits).astype(jnp.int32)])

    parts_h, vectors, parts = prepare(shape, chain, table, hamiltonian, vectors)
    common = (table, coefficients, parts_h, vectors)

    terms, older, inner, core_sends = ([None] * chunks for _ in range(4))
    core = rims = ends = None
    wide = (None, None)

    def swapped(x, distance):
        return lax.ppermute(x, "vecs", [(i, i ^ distance) for i in range(groups)])

    def received(sends):
        return {d: swapped(sends[d.bit_length() - 2], d) for d in range(2, groups, 2)}

    def forwarded(got):
        out = {}
        for d, rows in got.items():
            out[d], out[d + 1] = rows, swapped(rows, 1)
        return out

    def inside(step, c):
        nonlocal core, rims
        q = older[c] and older[c][1]
        if step < ORDER - 1:
            inner[c] = interior(step, c, shape, chain, common, parts[c], q)
        elif step == ORDER - 1:
            inner[c], core, core_sends[c] = core_rows(ORDER, c, shape, chain, common, parts[c], q, terms[c][1], core)
        else:
            rims = ring(step, c, shape, chain, common, parts[c], q, rims)

    for step in range(1, ORDER):
        for c in range(chunks):
            inside(step, c)
            q = older[c] and (older[c][0], older[c][2])
            late = step == ORDER - 1
            low, high, following = border(
                step, c, shape, chain, common, halo[c], q, parts[c], inner[c][1], wide if late else ()
            )
            if late:
                wide = (low, high)
            else:
                halo[c] = exchange(low, high)
            older[c], terms[c], parts[c] = terms[c], (low, inner[c][0], high), following
    last_halo = exchange(*wide)
    got_core = [received(sends) for sends in core_sends]
    for c in range(chunks):
        inside(ORDER, c)
    got_rims = received(rims[2:])
    near = rims[1]
    for c in range(chunks):
        q = (older[c][0], older[c][2])
        got = [[rows[d] for rows in got_core] for d in range(2, groups, 2)] if c == 0 else []
        passed = [core[1], *got_rims.values()] if c == chunks - 1 else []
        near, ends, joined, passed = last_border(
            ORDER, c, shape, chain, common, last_halo, q, parts[c], near, ends, got, passed
        )
        if c == 0:
            all_core = {2 * n + 2: rows for n, rows in enumerate(joined)}
    near_core = passed[0]
    got_core = forwarded(all_core)
    got_rims = forwarded(dict(zip(got_rims, passed[1:])))
    got_ends = received(ends[1:])

    kinds, far = tuple(range(min(2, groups))), tuple(range(2, groups))
    swaps = [[(i, i ^ (1 << level)) for i in range(peers)] for level in range(levels)]
    sums = gram_sums(shape, chain, table, kinds, [core[0]], {1: [([swapped(near_core, 1)], 0)]}, None, 0)
    near = swapped(near, 1)
    last = block_rows * BLOCK - SIZE
    result = [(core[0], 0, core[0].shape[0], 2 * SIZE), (rims[0], 0, SIZE, SIZE), (rims[0], SIZE, SIZE, last - SIZE)]
    result += [(ends[0], 0, SIZE, 0), (ends[0], SIZE, SIZE, last)]
    arrived = {1: [([near], 0), ([near], SIZE)]}
    whole = [] if far else result
    keep, send, *rest = gram_sums(shape, chain, table, kinds, [rims[0], ends[0]], arrived, sums, piece, whole)
    shares = [(keep, lax.ppermute(send, "rows", swaps[0]))]
    if far:
        arrived = {d: [([got_core[d]], 0), ([got_rims[d]], 0)] for d in far}
        sums, *rest = gram_sums(shape, chain, table, far, [core[0], rims[0]], arrived, None, 0, result)
        keep, send, *rows = fold(shape, chain, table, 1, shares, 0, got_ends.values())
        shares = [(keep, lax.ppermute(send, "rows", swaps[1]))]
        got_ends = forwarded(dict(zip(got_ends, rows)))
        arrived = {d: [([got_ends[d]], 0)] for d in far}
        keep, send = gram_sums(shape, chain, table, far, [ends[0]], arrived, sums, piece)
        shares.append((keep, lax.ppermute(send, "rows", swaps[0])))
    filtered = rest[0]

    for level in range(1, levels - 1):
        ahead = shares[:1] if level == 1 and len(shares) > 1 else []
        joined = [shares] if shares[0][0].shape[0] == 1 and not ahead else [[pair] for pair in shares[len(ahead) :]]
        folded = [fold(shape, chain, table, level, pairs) for pairs in joined]
        shares = ahead + [(keep, lax.ppermute(send, "rows", swaps[level])) for keep, send in folded]

    keep, send, *tiles = fold(shape, chain, table, levels - 1, shares, per_group)
    direct = lax.ppermute(send, "rows", swaps[-1])
    turned = []
    for n in range(per_group):
        for part, tile in enumerate(tiles[2 * n : 2 * n + 2]):
            pairs = []
            for i in range(peers):
                owner = i ^ (part * peers // 2)
                for g in range(groups):
                    to = (g * per_group + (owner + n) % per_group) * groups + owner // per_group
                    pairs.append((i * groups + g, to))
            turned.append(lax.ppermute(tile, ("rows", "vecs"), pairs))
    gram = assemble(shape, chain, table, keep, direct, turned, 1.0 / (total_blocks * BLOCK))
    return filtered, gram


def solution(mesh):
    return jax.shard_map(
        on_device,
        mesh=mesh,
        in_specs=(P("rows", None, None, None), P("rows", None), P("rows", "vecs"), P()),
        out_specs=(P("rows", "vecs"), P("vecs", "rows")),
        check_vma=False,
    )
```

```python
import functools

import jax
import jax.numpy as jnp
from jax import lax
from jax.experimental import pallas as pl
from jax.experimental.pallas import tpu as pltpu
from jax.sharding import PartitionSpec as P

BLOCK = 128
REACH = 4
ORDER = 6
LANES = 128
SIZE = REACH * BLOCK
SPARE = 32
F32 = jnp.float32
BF16 = jnp.bfloat16
WHOLE = pl.BlockSpec(memory_space=pltpu.VMEM)
ANYWHERE = pl.BlockSpec(memory_space=pl.ANY)
SCALARS = pl.BlockSpec(memory_space=pltpu.SMEM)


def shaped(shape, dtype=F32):
    return jax.ShapeDtypeStruct(shape, dtype)


def cost(flops, moved):
    return pl.CostEstimate(flops=flops, bytes_accessed=moved, transcendentals=0)


class Call:
    def __init__(self, chain):
        self.chain = chain
        self.args, self.specs, self.outs, self.out_specs, self.aliases = [], [], [], [], {}

    def anywhere(self, *arrays):
        self.args += arrays
        self.specs += [ANYWHERE] * len(arrays)
        return self

    def scalars(self, *arrays):
        self.args += arrays
        self.specs += [SCALARS] * len(arrays)
        return self

    def reads(self, *arrays):
        self.args += arrays
        self.specs += [WHOLE] * len(arrays)
        return self

    def writes(self, shape, before=None, spec=WHOLE):
        if before is not None:
            self.aliases[len(self.args)] = len(self.outs)
            self.args.append(before)
            self.specs.append(spec)
        self.outs.append(shape)
        self.out_specs.append(spec)
        return self

    def passes(self, *arrays):
        for array in arrays:
            self.writes(shaped(array.shape, array.dtype), array, ANYWHERE)
        return self

    def __call__(self, body, name, estimate, scratch=(), mib=16):
        if self.chain.token is not None:
            self.anywhere(self.chain.token)
        self.writes(shaped((8, LANES)))
        count = len(self.args)

        def kernel(*refs):
            ins, outs = refs[:count], refs[count : count + len(self.outs)]
            outs[-1][...] = jnp.zeros((8, LANES), F32)
            body(ins, outs[:-1], refs[count + len(self.outs) :])

        *results, self.chain.token = pl.pallas_call(
            kernel,
            in_specs=self.specs,
            out_specs=self.out_specs,
            out_shape=self.outs,
            scratch_shapes=scratch,
            input_output_aliases=self.aliases,
            compiler_params=pltpu.CompilerParams(vmem_limit_bytes=mib * 1024 * 1024),
            cost_estimate=estimate,
            name=name,
        )(*self.args)
        return results


class Chain:
    token = None


def two_parts(x):
    high = x.astype(BF16)
    low = (x - high.astype(F32)).astype(BF16)
    return high, low


def put_parts(ref, start, value):
    high, low = two_parts(value)
    ref[pl.ds(start, value.shape[0]), :LANES] = high
    ref[pl.ds(start, value.shape[0]), LANES:] = low


def prepare(shape, chain, table, hamiltonian, vectors):
    rows, per_row = hamiltonian.shape[:2]
    strips, slots = rows // REACH, 4
    far = [pltpu.with_memory_space_constraint(x, pltpu.HBM) for x in (hamiltonian, vectors)]
    call = Call(chain).scalars(table).anywhere(*far)
    call.writes(shaped((rows, 2 * BLOCK, per_row * BLOCK), BF16)).writes(shaped(vectors.shape))
    for _ in range(shape.chunks):
        call.writes(shaped((vectors.shape[0] + 2 * SIZE, 2 * LANES), BF16))

    def body(ins, outs, scratch):
        h_ref, v_ref = ins[1], ins[2]
        parts_h, copy_v = outs[:2]
        held, sems, v_sem = scratch

        def fetch(g):
            slot = lax.rem(g, slots)
            return pltpu.make_async_copy(h_ref.at[pl.ds(g * REACH, REACH)], held.at[slot], sems.at[slot])

        def split(g, carry):
            slot = lax.rem(g, slots)
            fetch(g).wait()
            for r in range(REACH):
                for k in range(per_row):
                    high, low = two_parts(held[slot, r, k])
                    parts_h[g * REACH + r, :BLOCK, k * BLOCK : (k + 1) * BLOCK] = high
                    parts_h[g * REACH + r, BLOCK:, k * BLOCK : (k + 1) * BLOCK] = low

            @pl.when(g + slots < strips)
            def _():
                fetch(g + slots).start()

            return carry

        def split_v(g, carry):
            at = pl.multiple_of(g * SIZE, SIZE)
            for c in range(shape.chunks):
                put_parts(outs[2 + c], pl.multiple_of(at + SIZE, SIZE), copy_v[pl.ds(at, SIZE), c * LANES : (c + 1) * LANES])
            return carry

        copy = pltpu.make_async_copy(v_ref, copy_v, v_sem)
        for g in range(min(slots, strips)):
            fetch(jnp.int32(g)).start()
        copy.start()
        lax.fori_loop(0, strips // 2, split, 0)
        copy.wait()
        lax.fori_loop(0, strips, split_v, 0)
        lax.fori_loop(strips // 2, strips, split, 0)

    scratch = [pltpu.VMEM((slots, REACH, *hamiltonian.shape[1:]), F32), pltpu.SemaphoreType.DMA((slots,)), pltpu.SemaphoreType.DMA]
    out = call(body, "prepare", cost(0, 8 * hamiltonian.size), scratch)
    return out[0], out[1], out[2:]


def scales(step, coef_ref):
    here, by = coef_ref[ORDER - step], 2.0
    if step == 1:
        by = 2.0 * coef_ref[ORDER]
    elif step == 2:
        here = here - coef_ref[ORDER]
    elif step == ORDER:
        by = 1.0
    return here, by


def new_rows(step, chunk, common, parts_ref, row, q):
    table_ref, coef_ref, h_ref, v_ref = common
    per_row = h_ref.shape[2] // BLOCK
    base = (row // REACH) * REACH
    picked = []
    for k in range(per_row):
        start = pl.multiple_of((table_ref[row * per_row + k] + base) * BLOCK, BLOCK)
        picked.append(parts_ref[pl.ds(start, BLOCK), :])
    both = jnp.dot(h_ref[row], jnp.concatenate(picked, axis=0), preferred_element_type=F32)
    top, bottom = both[:BLOCK], both[BLOCK:]
    total = top[:, :LANES] + ((top[:, LANES:] + bottom[:, :LANES]) + bottom[:, LANES:])
    here, by = scales(step, coef_ref)
    whole = pl.ds(pl.multiple_of(row * BLOCK, BLOCK), BLOCK)
    value = here * v_ref[whole, chunk * LANES : (chunk + 1) * LANES] + by * total
    return value if q is None else value - q


def unrolled(first, count, one):
    unroll = max(n for n in range(1, 13) if count % n == 0)

    def some(i, carry):
        for u in range(unroll):
            one(first + i * unroll + u)
        return carry

    lax.fori_loop(0, count // unroll, some, 0)


def at_rows(block, size=BLOCK):
    return pl.ds(pl.multiple_of(block * BLOCK, BLOCK), size)


class Shape:
    def __init__(self, block_rows, per_row, width, groups):
        self.rows = block_rows
        self.inner = block_rows - 2 * REACH
        self.core = block_rows - 4 * REACH
        self.chunks = width // LANES
        self.width = width
        self.vec_bits = (groups - 1).bit_length()
        self.bits_at = block_rows * per_row


def put_sends(shape, table_ref, source_ref, sends, lanes):
    half = source_ref.shape[0] // 2
    for b, ref, at in sends:
        other = 1 - table_ref[shape.bits_at + b]
        rows = pl.ds(pl.multiple_of(other * half, BLOCK), half)
        ref[at : at + half, lanes if ref.shape[1] == source_ref.shape[1] else slice(None)] = source_ref[rows, lanes]


def interior(step, chunk, shape, chain, common, parts, q):
    call = Call(chain).scalars(*common[:2]).reads(*common[2:], parts)
    if q is not None:
        call.reads(q)
    call.writes(shaped((shape.inner * BLOCK, LANES))).writes(shaped(parts.shape, BF16))

    def body(ins, outs, scratch):
        def one(row):
            old = None if q is None else ins[5][at_rows(row - REACH), :]
            value = new_rows(step, chunk, ins[:4], ins[4], row, old)
            outs[0][at_rows(row - REACH), :] = value
            put_parts(outs[1], pl.multiple_of((row + REACH) * BLOCK, BLOCK), value)

        unrolled(REACH, shape.inner, one)

    flops = 8 * shape.inner * BLOCK * LANES * common[2].shape[2]
    return call(body, "interior", cost(flops, 8 * common[2].size))


def core_rows(step, chunk, shape, chain, common, parts, q, mid, before):
    call = Call(chain).scalars(*common[:2]).reads(*common[2:], parts, q, mid).writes(shaped(parts.shape, BF16))
    core = shape.core * BLOCK
    before = before or [None, None]
    call.writes(shaped((core, shape.width)), before[0]).writes(shaped((core // 2, shape.width)), before[1])
    for _ in range(1, shape.vec_bits):
        call.writes(shaped((core // 2 + (shape.chunks - chunk) * SPARE, LANES)))
    lanes = slice(chunk * LANES, (chunk + 1) * LANES)

    def body(ins, outs, scratch):
        def one(row):
            value = new_rows(step - 1, chunk, ins[:4], ins[4], row, ins[5][at_rows(row - REACH), :])
            put_parts(outs[0], pl.multiple_of((row + REACH) * BLOCK, BLOCK), value)

        def two(row):
            old = ins[6][at_rows(row - REACH), :]
            outs[1][at_rows(row - 2 * REACH), lanes] = new_rows(step, chunk, ins[:4], outs[0], row, old)

        unrolled(REACH, shape.inner, one)
        unrolled(2 * REACH, shape.core, two)
        put_sends(shape, ins[0], outs[1], [(b, outs[2 + b], 0) for b in range(shape.vec_bits)], lanes)

    out = call(body, "core_rows", cost(0, 0))
    return (None, out[0]), out[1:3], out[3:]


def ring(step, chunk, shape, chain, common, parts, mid, before):
    call = Call(chain).scalars(*common[:2]).reads(*common[2:], parts, mid)
    before = before or [None] * (1 + shape.vec_bits)
    for n, one_before in enumerate(before):
        call.writes(shaped((2 * SIZE if n < 2 else SIZE, shape.width)), one_before)
    lanes = slice(chunk * LANES, (chunk + 1) * LANES)

    def body(ins, outs, scratch):
        for side, first in enumerate((REACH, shape.rows - 2 * REACH)):
            for r in range(REACH):
                row = first + r
                old = ins[5][at_rows(row - REACH), :]
                rows = pl.ds((side * REACH + r) * BLOCK, BLOCK)
                outs[0][rows, lanes] = new_rows(step, chunk, ins[:4], ins[4], row, old)
        put_sends(shape, ins[0], outs[0], [(b, outs[1 + b], 0) for b in range(shape.vec_bits)], lanes)

    return call(body, "ring", cost(0, 0))


def border(step, chunk, shape, chain, common, halo, q, parts, following, joined=None):
    call = Call(chain).scalars(*common[:2]).reads(*common[2:], *halo)
    if q is not None:
        call.reads(*q)
    call.writes(shaped(parts.shape, BF16), parts).writes(shaped(parts.shape, BF16), following)
    for before in joined or (None, None):
        call.writes(shaped((SIZE, shape.width if joined else LANES)), before)
    lanes = slice(chunk * LANES, (chunk + 1) * LANES) if joined else slice(None)

    def body(ins, outs, scratch):
        put_parts(outs[0], 0, ins[4][...])
        put_parts(outs[0], (shape.rows + REACH) * BLOCK, ins[5][...])
        for side, first in enumerate((0, shape.rows - REACH)):
            for r in range(REACH):
                rows = slice(r * BLOCK, (r + 1) * BLOCK)
                old = None if q is None else ins[6 + side][rows]
                value = new_rows(step, chunk, ins[:4], outs[0], first + r, old)
                outs[2 + side][rows, lanes] = value
                put_parts(outs[1], (first + r + REACH) * BLOCK, value)

    flops = 16 * SIZE * LANES * common[2].shape[2]
    _, following, low, high = call(body, "border", cost(flops, 4 * common[2].size))
    return low, high, following


def last_border(step, chunk, shape, chain, common, halo, q, parts, near, before, got, passed):
    call = Call(chain).scalars(*common[:2]).reads(*common[2:], *halo, *q)
    got_at = len(call.args)
    for arrays in got:
        call.reads(*arrays)
    call.writes(shaped(parts.shape, BF16), parts).writes(shaped(near.shape), near)
    before = before or [None] * shape.vec_bits
    for n, one_before in enumerate(before):
        call.writes(shaped((SIZE if n else 2 * SIZE, shape.width)), one_before)
    got_to = len(call.outs)
    for arrays in got:
        call.writes(shaped((shape.core * BLOCK // 2, shape.width)))
    call.passes(*passed)
    lanes = slice(chunk * LANES, (chunk + 1) * LANES)

    def body(ins, outs, scratch):
        put_parts(outs[0], 0, ins[4][:SIZE, lanes])
        put_parts(outs[0], (shape.rows + REACH) * BLOCK, ins[5][:SIZE, lanes])
        for side, first in enumerate((0, shape.rows - REACH)):
            for r in range(REACH):
                old = ins[6 + side][r * BLOCK : (r + 1) * BLOCK]
                rows = pl.ds((side * REACH + r) * BLOCK, BLOCK)
                outs[2][rows, lanes] = new_rows(step, chunk, ins[:4], outs[0], first + r, old)
        sends = [(0, outs[1], SIZE)] + [(b, outs[2 + b], 0) for b in range(1, shape.vec_bits)]
        put_sends(shape, ins[0], outs[2], sends, lanes)
        for n, arrays in enumerate(got):
            for c in range(len(arrays)):
                rows = slice(0, shape.core * BLOCK // 2)
                outs[got_to + n][:, c * LANES : (c + 1) * LANES] = ins[got_at + n * len(arrays) + c][rows]

    out = call(body, "last_border", cost(0, 0))
    joined, passed = out[got_to : got_to + len(got)], out[got_to + len(got) :][: len(passed)]
    return out[1], out[2 : 2 + shape.vec_bits], joined, passed


def gram_sums(shape, chain, table, kinds, own, got, before, piece, result=()):
    width = shape.width
    call = Call(chain).scalars(table).reads(*own)
    places = {}
    for d in kinds:
        if d:
            for n, (arrays, offset) in enumerate(got[d]):
                places[d, n] = (len(call.args), len(arrays), offset)
                call.reads(*arrays)
    before_at = len(call.args)
    if before is not None:
        call.reads(before)
    if piece:
        kept = shaped((len(kinds) * width // piece // 2, width, piece))
        call.writes(kept).writes(kept)
    else:
        call.writes(shaped((len(kinds), width, width)))
    result_at = len(call.args)
    for array, *_ in result:
        call.reads(array)
    if result:
        call.writes(shaped((shape.rows * BLOCK, width)), None, ANYWHERE)

    def products(left, right):
        total = jnp.dot(left[0], right[1], preferred_element_type=F32)
        total += jnp.dot(left[1], right[0], preferred_element_type=F32)
        return total + jnp.dot(left[0], right[0], preferred_element_type=F32)

    def body(ins, outs, scratch):
        table_ref = ins[0]
        copies = []
        for n, (_, start, rows, to) in enumerate(result):
            source = ins[result_at + n].at[pl.ds(start, rows)]
            copies.append(pltpu.make_async_copy(source, outs[-1].at[pl.ds(to, rows)], scratch[0].at[n]))
            copies[-1].start()
        totals = [ins[before_at][n] if before is not None else jnp.zeros((width, width), F32) for n in range(len(kinds))]
        for n in range(len(own)):
            ref = ins[1 + n]
            half = ref.shape[0] // 2
            for at in range(0, half, SIZE):
                sides = [ref[at : at + SIZE], ref[half + at : half + at + SIZE]]
                chosen = {}
                for m, d in enumerate(kinds):
                    if d == 0:
                        for side in sides:
                            totals[m] += 0.5 * products(two_parts(side.T), two_parts(side))
                        continue
                    b = d.bit_length() - 1
                    if b not in chosen:
                        first = table_ref[shape.bits_at + b] == 0
                        chosen[b] = two_parts(jnp.where(first, sides[0], sides[1]).T)
                    where, count, offset = places[d, n]
                    other = [ins[where + c][offset + at : offset + at + SIZE] for c in range(count)]
                    other = other[0] if count == 1 else jnp.concatenate(other, axis=1)
                    totals[m] += products(chosen[b], two_parts(other))
        for m, total in enumerate(totals):
            if not piece:
                outs[0][m] = total
                continue
            pairs = width // piece // 2
            even = table_ref[shape.bits_at + shape.vec_bits] == 0
            for t in range(pairs):
                one = total[:, 2 * t * piece : (2 * t + 1) * piece]
                two = total[:, (2 * t + 1) * piece : (2 * t + 2) * piece]
                outs[0][m * pairs + t] = jnp.where(even, one, two)
                outs[1][m * pairs + t] = jnp.where(even, two, one)
        for copy in copies:
            copy.wait()

    rows = sum(a.shape[0] for a in own)
    flops = 3 * rows * width * width * (len(kinds) + 1)
    scratch = [pltpu.SemaphoreType.DMA((len(result),))] if result else []
    out = call(body, "gram_sums", cost(flops, 8 * rows * width), scratch)
    return out if piece or result else out[0]


def fold(shape, chain, table, level, pairs, passed=()):
    call = Call(chain).scalars(table)
    count = 0
    for keep, got in pairs:
        call.reads(keep, got)
        count += keep.shape[0]
    half = shaped((count // 2, *pairs[0][0].shape[1:]))
    call.writes(half).writes(half).passes(*passed)

    def body(ins, outs, scratch):
        bit_at = shape.bits_at + shape.vec_bits
        even = ins[0][bit_at + level] == 0
        sums = []
        for n in range(len(pairs)):
            for m in range(ins[1 + 2 * n].shape[0]):
                sums.append(ins[1 + 2 * n][m] + ins[2 + 2 * n][m])
        for n in range(count // 2):
            outs[0][n] = jnp.where(even, sums[2 * n], sums[2 * n + 1])
            outs[1][n] = jnp.where(even, sums[2 * n + 1], sums[2 * n])

    return call(body, "fold", cost(0, 8 * count * pairs[0][0][0].size))


def add_blocks(chain, table, keep, got, tiles):
    rows, columns = keep.shape[1:]
    size = rows // tiles
    call = Call(chain).scalars(table).reads(keep, got).writes(shaped((rows, columns)))
    for _ in range(tiles):
        call.writes(shaped((size, columns)))

    def body(ins, outs, scratch):
        outs[0][...] = ins[1][0] + ins[2][0]
        for n in range(tiles):
            number = lax.rem(ins[0][ins[0].shape[0] - 1] + n, tiles)
            outs[1 + n][...] = outs[0][pl.ds(pl.multiple_of(number * size, size), size), :]

    return call(body, "add_blocks", cost(0, 0))


def assemble(chain, table, share, turned, scale):
    tiles = len(turned)
    rows, columns = share.shape
    size = rows // tiles
    call = Call(chain).scalars(table).reads(share, *turned).writes(shaped((rows, columns)))

    def body(ins, outs, scratch):
        number = ins[0][ins[0].shape[0] - 1]
        flipped = [ins[2 + n][...].T for n in range(tiles)]
        for t in range(tiles):
            which = lax.rem(number - t + tiles, tiles)
            tile = flipped[0]
            for n in range(1, tiles):
                tile = jnp.where(which == n, flipped[n], tile)
            at = slice(t * size, (t + 1) * size)
            outs[0][at] = (ins[1][at] + tile) * scale

    return call(body, "assemble", cost(0, 0))[0]


def on_device(hamiltonian, columns, vectors, coefficients):
    block_rows, per_row = columns.shape
    peers = lax.axis_size("rows")
    groups = lax.axis_size("vecs")
    total_blocks = block_rows * peers
    width = vectors.shape[1]
    shape = Shape(block_rows, per_row, width, groups)
    chunks = shape.chunks
    rows_at, vecs_at = lax.axis_index("rows"), lax.axis_index("vecs")
    up = [(i, (i + 1) % peers) for i in range(peers)]
    down = [(j, i) for i, j in up]

    def exchange(first, last):
        return lax.ppermute(last, "rows", up), lax.ppermute(first, "rows", down)

    chain = Chain()
    lanes = [slice(c * LANES, (c + 1) * LANES) for c in range(chunks)]
    halo = [exchange(vectors[:SIZE, l], vectors[-SIZE:, l]) for l in lanes]

    local = jnp.arange(block_rows, dtype=jnp.int32)
    offsets = (columns - (rows_at * block_rows + local)[:, None] + REACH) % total_blocks
    slots = (offsets + (local % REACH)[:, None]).reshape(-1)
    per_group = peers // groups
    piece = width // per_group
    wanted = rows_at ^ (vecs_at * per_group)
    levels = (peers - 1).bit_length()
    bits = [(vecs_at >> b) & 1 for b in range(shape.vec_bits)] + [(wanted >> b) & 1 for b in range(levels)]
    bits.append(rows_at % per_group)
    table = jnp.concatenate([slots, jnp.stack(bits).astype(jnp.int32)])

    parts_h, vectors, parts = prepare(shape, chain, table, hamiltonian, vectors)
    common = (table, coefficients, parts_h, vectors)

    terms, older, inner, core_sends = ([None] * chunks for _ in range(4))
    core = rims = ends = None
    wide = (None, None)

    def swapped(x, distance):
        return lax.ppermute(x, "vecs", [(i, i ^ distance) for i in range(groups)])

    def received(sends):
        return {d: swapped(sends[d.bit_length() - 2], d) for d in range(2, groups, 2)}

    def forwarded(got):
        out = {}
        for d, rows in got.items():
            out[d], out[d + 1] = rows, swapped(rows, 1)
        return out

    def inside(step, c):
        nonlocal core, rims
        q = older[c] and older[c][1]
        if step < ORDER - 1:
            inner[c] = interior(step, c, shape, chain, common, parts[c], q)
        elif step == ORDER - 1:
            inner[c], core, core_sends[c] = core_rows(ORDER, c, shape, chain, common, parts[c], q, terms[c][1], core)
        else:
            rims = ring(step, c, shape, chain, common, parts[c], q, rims)

    for step in range(1, ORDER):
        for c in range(chunks):
            inside(step, c)
            q = older[c] and (older[c][0], older[c][2])
            late = step == ORDER - 1
            low, high, following = border(
                step, c, shape, chain, common, halo[c], q, parts[c], inner[c][1], wide if late else ()
            )
            if late:
                wide = (low, high)
            else:
                halo[c] = exchange(low, high)
            older[c], terms[c], parts[c] = terms[c], (low, inner[c][0], high), following
    last_halo = exchange(*wide)
    got_core = [received(sends) for sends in core_sends]
    for c in range(chunks):
        inside(ORDER, c)
    got_rims = received(rims[2:])
    near = rims[1]
    for c in range(chunks):
        q = (older[c][0], older[c][2])
        got = [[rows[d] for rows in got_core] for d in range(2, groups, 2)] if c == 0 else []
        passed = [core[1], *got_rims.values()] if c == chunks - 1 else []
        near, ends, joined, passed = last_border(
            ORDER, c, shape, chain, common, last_halo, q, parts[c], near, ends, got, passed
        )
        if c == 0:
            all_core = {2 * n + 2: rows for n, rows in enumerate(joined)}
    near_core = passed[0]
    got_core = forwarded(all_core)
    got_rims = forwarded(dict(zip(got_rims, passed[1:])))
    got_ends = received(ends[1:])

    kinds, far = tuple(range(min(2, groups))), tuple(range(2, groups))
    swaps = [[(i, i ^ (1 << level)) for i in range(peers)] for level in range(levels)]
    sums = gram_sums(shape, chain, table, kinds, [core[0]], {1: [([swapped(near_core, 1)], 0)]}, None, 0)
    near = swapped(near, 1)
    last = block_rows * BLOCK - SIZE
    result = [(core[0], 0, core[0].shape[0], 2 * SIZE), (rims[0], 0, SIZE, SIZE), (rims[0], SIZE, SIZE, last - SIZE)]
    result += [(ends[0], 0, SIZE, 0), (ends[0], SIZE, SIZE, last)]
    arrived = {1: [([near], 0), ([near], SIZE)]}
    whole = [] if far else result
    keep, send, *rest = gram_sums(shape, chain, table, kinds, [rims[0], ends[0]], arrived, sums, piece, whole)
    shares = [(keep, lax.ppermute(send, "rows", swaps[0]))]
    if far:
        arrived = {d: [([got_core[d]], 0), ([got_rims[d]], 0)] for d in far}
        sums, *rest = gram_sums(shape, chain, table, far, [core[0], rims[0]], arrived, None, 0, result)
        keep, send, *rows = fold(shape, chain, table, 1, shares, got_ends.values())
        shares = [(keep, lax.ppermute(send, "rows", swaps[1]))]
        got_ends = forwarded(dict(zip(got_ends, rows)))
        arrived = {d: [([got_ends[d]], 0)] for d in far}
        keep, send = gram_sums(shape, chain, table, far, [ends[0]], arrived, sums, piece)
        shares.append((keep, lax.ppermute(send, "rows", swaps[0])))
    filtered = rest[0]

    for level in range(1, levels - 1):
        ahead = shares[:1] if level == 1 and len(shares) > 1 else []
        joined = [shares] if shares[0][0].shape[0] == 1 and not ahead else [[pair] for pair in shares[len(ahead) :]]
        folded = [fold(shape, chain, table, level, pairs) for pairs in joined]
        shares = ahead + [(keep, lax.ppermute(send, "rows", swaps[level])) for keep, send in folded]

    keep, send = fold(shape, chain, table, levels - 1, shares)
    share, *tiles = add_blocks(chain, table, keep, lax.ppermute(send, "rows", swaps[-1]), per_group)
    turned = []
    for n in range(per_group):
        pairs = []
        for i in range(peers):
            for g in range(groups):
                to = (g * per_group + (i + n) % per_group) * groups + i // per_group
                pairs.append((i * groups + g, to))
        turned.append(lax.ppermute(tiles[n], ("rows", "vecs"), pairs))
    gram = assemble(chain, table, share, turned, 1.0 / (total_blocks * BLOCK))
    return filtered, gram


def solution(mesh):
    return jax.shard_map(
        on_device,
        mesh=mesh,
        in_specs=(P("rows", None, None, None), P("rows", None), P("rows", "vecs"), P()),
        out_specs=(P("rows", "vecs"), P("vecs", "rows")),
        check_vma=False,
    )
```

```python
import functools

import jax
import jax.numpy as jnp
from jax import lax
from jax.experimental import pallas as pl
from jax.experimental.pallas import tpu as pltpu
from jax.sharding import PartitionSpec as P

BLOCK = 128
REACH = 4
ORDER = 6
LANES = 128
SIZE = REACH * BLOCK
SPARE = 32
F32 = jnp.float32
BF16 = jnp.bfloat16
WHOLE = pl.BlockSpec(memory_space=pltpu.VMEM)
ANYWHERE = pl.BlockSpec(memory_space=pl.ANY)
SCALARS = pl.BlockSpec(memory_space=pltpu.SMEM)


def shaped(shape, dtype=F32):
    return jax.ShapeDtypeStruct(shape, dtype)


def cost(flops, moved):
    return pl.CostEstimate(flops=flops, bytes_accessed=moved, transcendentals=0)


class Call:
    def __init__(self, chain):
        self.chain = chain
        self.args, self.specs, self.outs, self.out_specs, self.aliases = [], [], [], [], {}

    def anywhere(self, *arrays):
        self.args += arrays
        self.specs += [ANYWHERE] * len(arrays)
        return self

    def scalars(self, *arrays):
        self.args += arrays
        self.specs += [SCALARS] * len(arrays)
        return self

    def reads(self, *arrays):
        self.args += arrays
        self.specs += [WHOLE] * len(arrays)
        return self

    def writes(self, shape, before=None, spec=WHOLE):
        if before is not None:
            self.aliases[len(self.args)] = len(self.outs)
            self.args.append(before)
            self.specs.append(spec)
        self.outs.append(shape)
        self.out_specs.append(spec)
        return self

    def passes(self, *arrays):
        for array in arrays:
            self.writes(shaped(array.shape, array.dtype), array, ANYWHERE)
        return self

    def __call__(self, body, name, estimate, scratch=(), mib=16):
        if self.chain.token is not None:
            self.anywhere(self.chain.token)
        self.writes(shaped((8, LANES)))
        count = len(self.args)

        def kernel(*refs):
            ins, outs = refs[:count], refs[count : count + len(self.outs)]
            outs[-1][...] = jnp.zeros((8, LANES), F32)
            body(ins, outs[:-1], refs[count + len(self.outs) :])

        *results, self.chain.token = pl.pallas_call(
            kernel,
            in_specs=self.specs,
            out_specs=self.out_specs,
            out_shape=self.outs,
            scratch_shapes=scratch,
            input_output_aliases=self.aliases,
            compiler_params=pltpu.CompilerParams(vmem_limit_bytes=mib * 1024 * 1024),
            cost_estimate=estimate,
            name=name,
        )(*self.args)
        return results


class Chain:
    token = None


def two_parts(x):
    high = x.astype(BF16)
    low = (x - high.astype(F32)).astype(BF16)
    return high, low


def put_parts(ref, start, value):
    high, low = two_parts(value)
    ref[pl.ds(start, value.shape[0]), :LANES] = high
    ref[pl.ds(start, value.shape[0]), LANES:] = low


def prepare(shape, chain, table, hamiltonian, vectors):
    rows, per_row = hamiltonian.shape[:2]
    strips, slots = rows // REACH, 4
    far = [pltpu.with_memory_space_constraint(x, pltpu.HBM) for x in (hamiltonian, vectors)]
    call = Call(chain).scalars(table).anywhere(*far)
    call.writes(shaped((rows, 2 * BLOCK, per_row * BLOCK), BF16)).writes(shaped(vectors.shape))
    for _ in range(shape.chunks):
        call.writes(shaped((vectors.shape[0] + 2 * SIZE, 2 * LANES), BF16))
    for _ in range(2 * (shape.chunks - 1)):
        call.writes(shaped((SIZE, LANES)))

    def body(ins, outs, scratch):
        h_ref, v_ref = ins[1], ins[2]
        parts_h, copy_v = outs[:2]
        held, sems, v_sem = scratch

        def fetch(g):
            slot = lax.rem(g, slots)
            return pltpu.make_async_copy(h_ref.at[pl.ds(g * REACH, REACH)], held.at[slot], sems.at[slot])

        def split(g, carry):
            slot = lax.rem(g, slots)
            fetch(g).wait()
            for r in range(REACH):
                for k in range(per_row):
                    high, low = two_parts(held[slot, r, k])
                    parts_h[g * REACH + r, :BLOCK, k * BLOCK : (k + 1) * BLOCK] = high
                    parts_h[g * REACH + r, BLOCK:, k * BLOCK : (k + 1) * BLOCK] = low

            @pl.when(g + slots < strips)
            def _():
                fetch(g + slots).start()

            return carry

        def split_v(g, carry):
            at = pl.multiple_of(g * SIZE, SIZE)
            for c in range(shape.chunks):
                put_parts(outs[2 + c], pl.multiple_of(at + SIZE, SIZE), copy_v[pl.ds(at, SIZE), c * LANES : (c + 1) * LANES])
            return carry

        copy = pltpu.make_async_copy(v_ref, copy_v, v_sem)
        for g in range(min(slots, strips)):
            fetch(jnp.int32(g)).start()
        copy.start()
        lax.fori_loop(0, strips // 2, split, 0)
        copy.wait()
        lax.fori_loop(0, strips, split_v, 0)
        for c in range(1, shape.chunks):
            lanes = slice(c * LANES, (c + 1) * LANES)
            outs[shape.chunks + 2 * c][...] = copy_v[:SIZE, lanes]
            outs[shape.chunks + 2 * c + 1][...] = copy_v[-SIZE:, lanes]
        lax.fori_loop(strips // 2, strips, split, 0)

    scratch = [pltpu.VMEM((slots, REACH, *hamiltonian.shape[1:]), F32), pltpu.SemaphoreType.DMA((slots,)), pltpu.SemaphoreType.DMA]
    out = call(body, "prepare", cost(0, 8 * hamiltonian.size), scratch)
    sends = out[2 + shape.chunks :]
    return out[0], out[1], out[2 : 2 + shape.chunks], [sends[2 * c : 2 * c + 2] for c in range(shape.chunks - 1)]


def scales(step, coef_ref):
    here, by = coef_ref[ORDER - step], 2.0
    if step == 1:
        by = 2.0 * coef_ref[ORDER]
    elif step == 2:
        here = here - coef_ref[ORDER]
    elif step == ORDER:
        by = 1.0
    return here, by


def new_rows(step, chunk, common, parts_ref, row, q):
    table_ref, coef_ref, h_ref, v_ref = common
    per_row = h_ref.shape[2] // BLOCK
    base = (row // REACH) * REACH
    picked = []
    for k in range(per_row):
        start = pl.multiple_of((table_ref[row * per_row + k] + base) * BLOCK, BLOCK)
        picked.append(parts_ref[pl.ds(start, BLOCK), :])
    both = jnp.dot(h_ref[row], jnp.concatenate(picked, axis=0), preferred_element_type=F32)
    top, bottom = both[:BLOCK], both[BLOCK:]
    total = top[:, :LANES] + ((top[:, LANES:] + bottom[:, :LANES]) + bottom[:, LANES:])
    here, by = scales(step, coef_ref)
    whole = pl.ds(pl.multiple_of(row * BLOCK, BLOCK), BLOCK)
    value = here * v_ref[whole, chunk * LANES : (chunk + 1) * LANES] + by * total
    return value if q is None else value - q


def unrolled(first, count, one):
    unroll = max(n for n in range(1, 13) if count % n == 0)

    def some(i, carry):
        for u in range(unroll):
            one(first + i * unroll + u)
        return carry

    lax.fori_loop(0, count // unroll, some, 0)


def at_rows(block, size=BLOCK):
    return pl.ds(pl.multiple_of(block * BLOCK, BLOCK), size)


class Shape:
    def __init__(self, block_rows, per_row, width, groups):
        self.rows = block_rows
        self.inner = block_rows - 2 * REACH
        self.core = block_rows - 4 * REACH
        self.chunks = width // LANES
        self.width = width
        self.vec_bits = (groups - 1).bit_length()
        self.bits_at = block_rows * per_row


def put_sends(shape, table_ref, source_ref, sends, lanes):
    half = source_ref.shape[0] // 2
    for b, ref, at in sends:
        other = 1 - table_ref[shape.bits_at + b]
        rows = pl.ds(pl.multiple_of(other * half, BLOCK), half)
        ref[at : at + half, lanes if ref.shape[1] == source_ref.shape[1] else slice(None)] = source_ref[rows, lanes]


def interior(step, chunk, shape, chain, common, parts, q):
    call = Call(chain).scalars(*common[:2]).reads(*common[2:], parts)
    if q is not None:
        call.reads(q)
    call.writes(shaped((shape.inner * BLOCK, LANES))).writes(shaped(parts.shape, BF16))

    def body(ins, outs, scratch):
        def one(row):
            old = None if q is None else ins[5][at_rows(row - REACH), :]
            value = new_rows(step, chunk, ins[:4], ins[4], row, old)
            outs[0][at_rows(row - REACH), :] = value
            put_parts(outs[1], pl.multiple_of((row + REACH) * BLOCK, BLOCK), value)

        unrolled(REACH, shape.inner, one)

    flops = 8 * shape.inner * BLOCK * LANES * common[2].shape[2]
    return call(body, "interior", cost(flops, 8 * common[2].size))


def core_rows(step, chunk, shape, chain, common, parts, q, mid, before):
    call = Call(chain).scalars(*common[:2]).reads(*common[2:], parts, q, mid).writes(shaped(parts.shape, BF16))
    core = shape.core * BLOCK
    before = before or [None, None]
    call.writes(shaped((core, shape.width)), before[0]).writes(shaped((core // 2, shape.width)), before[1])
    for _ in range(1, shape.vec_bits):
        call.writes(shaped((core // 2 + (shape.chunks - chunk) * SPARE, LANES)))
    lanes = slice(chunk * LANES, (chunk + 1) * LANES)

    def body(ins, outs, scratch):
        def one(row):
            value = new_rows(step - 1, chunk, ins[:4], ins[4], row, ins[5][at_rows(row - REACH), :])
            put_parts(outs[0], pl.multiple_of((row + REACH) * BLOCK, BLOCK), value)

        def two(row):
            old = ins[6][at_rows(row - REACH), :]
            outs[1][at_rows(row - 2 * REACH), lanes] = new_rows(step, chunk, ins[:4], outs[0], row, old)

        unrolled(REACH, shape.inner, one)
        unrolled(2 * REACH, shape.core, two)
        put_sends(shape, ins[0], outs[1], [(b, outs[2 + b], 0) for b in range(shape.vec_bits)], lanes)

    out = call(body, "core_rows", cost(0, 0))
    return (None, out[0]), out[1:3], out[3:]


def ring(step, chunk, shape, chain, common, parts, mid, before):
    call = Call(chain).scalars(*common[:2]).reads(*common[2:], parts, mid)
    before = before or [None] * (1 + shape.vec_bits)
    for n, one_before in enumerate(before):
        call.writes(shaped((2 * SIZE if n < 2 else SIZE, shape.width)), one_before)
    lanes = slice(chunk * LANES, (chunk + 1) * LANES)

    def body(ins, outs, scratch):
        for side, first in enumerate((REACH, shape.rows - 2 * REACH)):
            for r in range(REACH):
                row = first + r
                old = ins[5][at_rows(row - REACH), :]
                rows = pl.ds((side * REACH + r) * BLOCK, BLOCK)
                outs[0][rows, lanes] = new_rows(step, chunk, ins[:4], ins[4], row, old)
        put_sends(shape, ins[0], outs[0], [(b, outs[1 + b], 0) for b in range(shape.vec_bits)], lanes)

    return call(body, "ring", cost(0, 0))


def border(step, chunk, shape, chain, common, halo, q, parts, following, joined=None):
    call = Call(chain).scalars(*common[:2]).reads(*common[2:], *halo)
    if q is not None:
        call.reads(*q)
    call.writes(shaped(parts.shape, BF16), parts).writes(shaped(parts.shape, BF16), following)
    for before in joined or (None, None):
        call.writes(shaped((SIZE, shape.width if joined else LANES)), before)
    lanes = slice(chunk * LANES, (chunk + 1) * LANES) if joined else slice(None)

    def body(ins, outs, scratch):
        put_parts(outs[0], 0, ins[4][...])
        put_parts(outs[0], (shape.rows + REACH) * BLOCK, ins[5][...])
        for side, first in enumerate((0, shape.rows - REACH)):
            for r in range(REACH):
                rows = slice(r * BLOCK, (r + 1) * BLOCK)
                old = None if q is None else ins[6 + side][rows]
                value = new_rows(step, chunk, ins[:4], outs[0], first + r, old)
                outs[2 + side][rows, lanes] = value
                put_parts(outs[1], (first + r + REACH) * BLOCK, value)

    flops = 16 * SIZE * LANES * common[2].shape[2]
    _, following, low, high = call(body, "border", cost(flops, 4 * common[2].size))
    return low, high, following


def last_border(step, chunk, shape, chain, common, halo, q, parts, near, before, got, passed):
    call = Call(chain).scalars(*common[:2]).reads(*common[2:], *halo, *q)
    got_at = len(call.args)
    for arrays in got:
        call.reads(*arrays)
    call.writes(shaped(parts.shape, BF16), parts).writes(shaped(near.shape), near)
    before = before or [None] * shape.vec_bits
    for n, one_before in enumerate(before):
        call.writes(shaped((SIZE if n else 2 * SIZE, shape.width)), one_before)
    got_to = len(call.outs)
    for arrays in got:
        call.writes(shaped((shape.core * BLOCK // 2, shape.width)))
    call.passes(*passed)
    lanes = slice(chunk * LANES, (chunk + 1) * LANES)

    def body(ins, outs, scratch):
        put_parts(outs[0], 0, ins[4][:SIZE, lanes])
        put_parts(outs[0], (shape.rows + REACH) * BLOCK, ins[5][:SIZE, lanes])
        for side, first in enumerate((0, shape.rows - REACH)):
            for r in range(REACH):
                old = ins[6 + side][r * BLOCK : (r + 1) * BLOCK]
                rows = pl.ds((side * REACH + r) * BLOCK, BLOCK)
                outs[2][rows, lanes] = new_rows(step, chunk, ins[:4], outs[0], first + r, old)
        sends = [(0, outs[1], SIZE)] + [(b, outs[2 + b], 0) for b in range(1, shape.vec_bits)]
        put_sends(shape, ins[0], outs[2], sends, lanes)
        for n, arrays in enumerate(got):
            for c in range(len(arrays)):
                rows = slice(0, shape.core * BLOCK // 2)
                outs[got_to + n][:, c * LANES : (c + 1) * LANES] = ins[got_at + n * len(arrays) + c][rows]

    out = call(body, "last_border", cost(0, 0))
    joined, passed = out[got_to : got_to + len(got)], out[got_to + len(got) :][: len(passed)]
    return out[1], out[2 : 2 + shape.vec_bits], joined, passed


def gram_sums(shape, chain, table, kinds, own, got, before, piece, result=(), both=False):
    width = shape.width
    call = Call(chain).scalars(table).reads(*own)
    places = {}
    for d in kinds:
        if d:
            for n, (arrays, offset) in enumerate(got[d]):
                places[d, n] = (len(call.args), len(arrays), offset)
                call.reads(*arrays)
    before_at = len(call.args)
    if before is not None:
        call.reads(before)
    if piece:
        kept = shaped((len(kinds) * width // piece // 2, width // 2 if both else width, piece))
        for _ in range(4 if both else 2):
            call.writes(kept)
    else:
        call.writes(shaped((len(kinds), width, width)))
    result_at = len(call.args)
    for array, *_ in result:
        call.reads(array)
    if result:
        call.writes(shaped((shape.rows * BLOCK, width)), None, ANYWHERE)

    def products(left, right):
        total = jnp.dot(left[0], right[1], preferred_element_type=F32)
        total += jnp.dot(left[1], right[0], preferred_element_type=F32)
        return total + jnp.dot(left[0], right[0], preferred_element_type=F32)

    def body(ins, outs, scratch):
        table_ref = ins[0]
        copies = []
        for n, (_, start, rows, to) in enumerate(result):
            source = ins[result_at + n].at[pl.ds(start, rows)]
            copies.append(pltpu.make_async_copy(source, outs[-1].at[pl.ds(to, rows)], scratch[0].at[n]))
            copies[-1].start()
        totals = [ins[before_at][n] if before is not None else jnp.zeros((width, width), F32) for n in range(len(kinds))]
        for n in range(len(own)):
            ref = ins[1 + n]
            half = ref.shape[0] // 2
            for at in range(0, half, SIZE):
                sides = [ref[at : at + SIZE], ref[half + at : half + at + SIZE]]
                chosen = {}
                for m, d in enumerate(kinds):
                    if d == 0:
                        for side in sides:
                            totals[m] += 0.5 * products(two_parts(side.T), two_parts(side))
                        continue
                    b = d.bit_length() - 1
                    if b not in chosen:
                        first = table_ref[shape.bits_at + b] == 0
                        chosen[b] = two_parts(jnp.where(first, sides[0], sides[1]).T)
                    where, count, offset = places[d, n]
                    other = [ins[where + c][offset + at : offset + at + SIZE] for c in range(count)]
                    other = other[0] if count == 1 else jnp.concatenate(other, axis=1)
                    totals[m] += products(chosen[b], two_parts(other))
        bit_at = shape.bits_at + shape.vec_bits
        for m in range(0, len(kinds) if both else 0, 2):
            first, second = table_ref[bit_at] == 0, table_ref[bit_at + 1] == 0
            half = width // 2
            for n in range(2):
                one, two = totals[m + n][:half, :piece], totals[m + n][:half, piece:]
                outs[0][m + n] = jnp.where(first, one, two)
                outs[1][m + n] = jnp.where(first, two, one)
                columns = slice(n * piece, (n + 1) * piece)
                one, two = totals[m][half:, columns], totals[m + 1][half:, columns]
                outs[2][m + n] = jnp.where(second, one, two)
                outs[3][m + n] = jnp.where(second, two, one)
        for m, total in enumerate([] if both else totals):
            if not piece:
                outs[0][m] = total
                continue
            pairs = width // piece // 2
            even = table_ref[bit_at] == 0
            for t in range(pairs):
                one = total[:, 2 * t * piece : (2 * t + 1) * piece]
                two = total[:, (2 * t + 1) * piece : (2 * t + 2) * piece]
                outs[0][m * pairs + t] = jnp.where(even, one, two)
                outs[1][m * pairs + t] = jnp.where(even, two, one)
        for copy in copies:
            copy.wait()

    rows = sum(a.shape[0] for a in own)
    flops = 3 * rows * width * width * (len(kinds) + 1)
    scratch = [pltpu.SemaphoreType.DMA((len(result),))] if result else []
    out = call(body, "gram_sums", cost(flops, 8 * rows * width), scratch)
    return out if piece or result else out[0]


def fold(shape, chain, table, level, pairs, passed=()):
    call = Call(chain).scalars(table)
    count = sum(arrays[0].shape[0] for arrays in pairs)
    for arrays in pairs:
        call.reads(*arrays)
    rows = sum(a.shape[1] for a in pairs[0][::2])
    half = shaped((count // 2, rows, pairs[0][0].shape[2]))
    call.writes(half).writes(half).passes(*passed)

    def body(ins, outs, scratch):
        bit_at = shape.bits_at + shape.vec_bits
        even = ins[0][bit_at + level] == 0
        sums, at = [], 1
        for arrays in pairs:
            for m in range(arrays[0].shape[0]):
                parts = [ins[at + n][m] + ins[at + n + 1][m] for n in range(0, len(arrays), 2)]
                sums.append(jnp.concatenate(parts, axis=0) if len(parts) > 1 else parts[0])
            at += len(arrays)
        for n in range(count // 2):
            outs[0][n] = jnp.where(even, sums[2 * n], sums[2 * n + 1])
            outs[1][n] = jnp.where(even, sums[2 * n + 1], sums[2 * n])

    return call(body, "fold", cost(0, 8 * count * pairs[0][0][0].size))


def fold_two(shape, chain, table, upper, lower):
    half = shaped((upper[0].shape[0] // 2, *upper[0].shape[1:]))
    call = Call(chain).scalars(table).reads(*upper, *lower)
    for _ in range(4):
        call.writes(half)

    def body(ins, outs, scratch):
        bit_at = shape.bits_at + shape.vec_bits
        for n, level in enumerate((1, 0)):
            even = ins[0][bit_at + level] == 0
            keep, got = ins[1 + 2 * n], ins[2 + 2 * n]
            for m in range(half.shape[0]):
                one, two = keep[2 * m] + got[2 * m], keep[2 * m + 1] + got[2 * m + 1]
                outs[2 * n][m] = jnp.where(even, one, two)
                outs[2 * n + 1][m] = jnp.where(even, two, one)

    return call(body, "fold_two", cost(0, 0))


def add_blocks(chain, table, keep, got, tiles):
    rows, columns = keep.shape[1:]
    size = rows // tiles
    call = Call(chain).scalars(table).reads(keep, got).writes(shaped((rows, columns)))
    for _ in range(tiles):
        call.writes(shaped((size, columns)))

    def body(ins, outs, scratch):
        outs[0][...] = ins[1][0] + ins[2][0]
        for n in range(tiles):
            number = lax.rem(ins[0][ins[0].shape[0] - 1] + n, tiles)
            outs[1 + n][...] = outs[0][pl.ds(pl.multiple_of(number * size, size), size), :]

    return call(body, "add_blocks", cost(0, 0))


def assemble(chain, table, share, turned, scale):
    tiles = len(turned)
    rows, columns = share.shape
    size = rows // tiles
    call = Call(chain).scalars(table).reads(share, *turned).writes(shaped((rows, columns)))

    def body(ins, outs, scratch):
        number = ins[0][ins[0].shape[0] - 1]
        flipped = [ins[2 + n][...].T for n in range(tiles)]
        for t in range(tiles):
            which = lax.rem(number - t + tiles, tiles)
            tile = flipped[0]
            for n in range(1, tiles):
                tile = jnp.where(which == n, flipped[n], tile)
            at = slice(t * size, (t + 1) * size)
            outs[0][at] = (ins[1][at] + tile) * scale

    return call(body, "assemble", cost(0, 0))[0]


def on_device(hamiltonian, columns, vectors, coefficients):
    block_rows, per_row = columns.shape
    peers = lax.axis_size("rows")
    groups = lax.axis_size("vecs")
    total_blocks = block_rows * peers
    width = vectors.shape[1]
    shape = Shape(block_rows, per_row, width, groups)
    chunks = shape.chunks
    rows_at, vecs_at = lax.axis_index("rows"), lax.axis_index("vecs")
    up = [(i, (i + 1) % peers) for i in range(peers)]
    down = [(j, i) for i, j in up]

    def exchange(first, last):
        return lax.ppermute(last, "rows", up), lax.ppermute(first, "rows", down)

    chain = Chain()
    halo = [exchange(vectors[:SIZE, :LANES], vectors[-SIZE:, :LANES])]

    local = jnp.arange(block_rows, dtype=jnp.int32)
    offsets = (columns - (rows_at * block_rows + local)[:, None] + REACH) % total_blocks
    slots = (offsets + (local % REACH)[:, None]).reshape(-1)
    per_group = peers // groups
    piece = width // per_group
    wanted = rows_at ^ (vecs_at * per_group)
    levels = (peers - 1).bit_length()
    bits = [(vecs_at >> b) & 1 for b in range(shape.vec_bits)] + [(wanted >> b) & 1 for b in range(levels)]
    bits.append(rows_at % per_group)
    table = jnp.concatenate([slots, jnp.stack(bits).astype(jnp.int32)])

    parts_h, vectors, parts, sends = prepare(shape, chain, table, hamiltonian, vectors)
    halo += [exchange(*strips) for strips in sends]
    common = (table, coefficients, parts_h, vectors)

    terms, older, inner, core_sends = ([None] * chunks for _ in range(4))
    core = rims = ends = None
    wide = (None, None)

    def swapped(x, distance):
        return lax.ppermute(x, "vecs", [(i, i ^ distance) for i in range(groups)])

    def received(sends):
        return {d: swapped(sends[d.bit_length() - 2], d) for d in range(2, groups, 2)}

    def forwarded(got):
        out = {}
        for d, rows in got.items():
            out[d], out[d + 1] = rows, swapped(rows, 1)
        return out

    def inside(step, c):
        nonlocal core, rims
        q = older[c] and older[c][1]
        if step < ORDER - 1:
            inner[c] = interior(step, c, shape, chain, common, parts[c], q)
        elif step == ORDER - 1:
            inner[c], core, core_sends[c] = core_rows(ORDER, c, shape, chain, common, parts[c], q, terms[c][1], core)
        else:
            rims = ring(step, c, shape, chain, common, parts[c], q, rims)

    for step in range(1, ORDER):
        for c in range(chunks):
            inside(step, c)
            q = older[c] and (older[c][0], older[c][2])
            late = step == ORDER - 1
            low, high, following = border(
                step, c, shape, chain, common, halo[c], q, parts[c], inner[c][1], wide if late else ()
            )
            if late:
                wide = (low, high)
            else:
                halo[c] = exchange(low, high)
            older[c], terms[c], parts[c] = terms[c], (low, inner[c][0], high), following
    last_halo = exchange(*wide)
    got_core = [received(sends) for sends in core_sends]
    for c in range(chunks):
        inside(ORDER, c)
    got_rims = received(rims[2:])
    near = rims[1]
    for c in range(chunks):
        q = (older[c][0], older[c][2])
        got = [[rows[d] for rows in got_core] for d in range(2, groups, 2)] if c == 0 else []
        passed = [core[1], *got_rims.values()] if c == chunks - 1 else []
        near, ends, joined, passed = last_border(
            ORDER, c, shape, chain, common, last_halo, q, parts[c], near, ends, got, passed
        )
        if c == 0:
            all_core = {2 * n + 2: rows for n, rows in enumerate(joined)}
    near_core = passed[0]
    got_core = forwarded(all_core)
    got_rims = forwarded(dict(zip(got_rims, passed[1:])))
    got_ends = received(ends[1:])

    kinds, far = tuple(range(min(2, groups))), tuple(range(2, groups))
    swaps = [[(i, i ^ (1 << level)) for i in range(peers)] for level in range(levels)]
    sums = gram_sums(shape, chain, table, kinds, [core[0]], {1: [([swapped(near_core, 1)], 0)]}, None, 0)
    near = swapped(near, 1)
    last = block_rows * BLOCK - SIZE
    result = [(core[0], 0, core[0].shape[0], 2 * SIZE), (rims[0], 0, SIZE, SIZE), (rims[0], SIZE, SIZE, last - SIZE)]
    result += [(ends[0], 0, SIZE, 0), (ends[0], SIZE, SIZE, last)]
    arrived = {1: [([near], 0), ([near], SIZE)]}
    whole = [] if far else result
    keep, send, *rest = gram_sums(shape, chain, table, kinds, [rims[0], ends[0]], arrived, sums, piece, whole)
    shares = [(keep, lax.ppermute(send, "rows", swaps[0]))]
    if far:
        arrived = {d: [([got_core[d]], 0), ([got_rims[d]], 0)] for d in far}
        sums, *rest = gram_sums(shape, chain, table, far, [core[0], rims[0]], arrived, None, 0, result)
        keep, send, *rows = fold(shape, chain, table, 1, shares, got_ends.values())
        shares = [(keep, lax.ppermute(send, "rows", swaps[1]))]
        got_ends = forwarded(dict(zip(got_ends, rows)))
        arrived = {d: [([got_ends[d]], 0)] for d in far}
        both = per_group == 2 and levels > 2
        made = gram_sums(shape, chain, table, far, [ends[0]], arrived, sums, piece, (), both)
        if both:
            upper = (made[0], lax.ppermute(made[1], "rows", swaps[0]))
            lower = (made[2], lax.ppermute(made[3], "rows", swaps[1]))
            made = fold_two(shape, chain, table, upper, lower)
            shares.append(
                (made[0], lax.ppermute(made[1], "rows", swaps[1]), made[2], lax.ppermute(made[3], "rows", swaps[0]))
            )
        else:
            shares.append((made[0], lax.ppermute(made[1], "rows", swaps[0])))
    filtered = rest[0]

    for level in range(1, levels - 1):
        ahead = [pair for n, pair in enumerate(shares) if level == 1 and len(shares) > 1 and (n == 0 or len(pair) > 2)]
        if len(ahead) == len(shares):
            continue
        joined = [shares] if shares[0][0].shape[0] == 1 and not ahead else [[pair] for pair in shares[len(ahead) :]]
        folded = [fold(shape, chain, table, level, pairs) for pairs in joined]
        shares = ahead + [(keep, lax.ppermute(send, "rows", swaps[level])) for keep, send in folded]

    keep, send = fold(shape, chain, table, levels - 1, shares)
    share, *tiles = add_blocks(chain, table, keep, lax.ppermute(send, "rows", swaps[-1]), per_group)
    turned = []
    for n in range(per_group):
        pairs = []
        for i in range(peers):
            for g in range(groups):
                to = (g * per_group + (i + n) % per_group) * groups + i // per_group
                pairs.append((i * groups + g, to))
        turned.append(lax.ppermute(tiles[n], ("rows", "vecs"), pairs))
    gram = assemble(chain, table, share, turned, 1.0 / (total_blocks * BLOCK))
    return filtered, gram


def solution(mesh):
    return jax.shard_map(
        on_device,
        mesh=mesh,
        in_specs=(P("rows", None, None, None), P("rows", None), P("rows", "vecs"), P()),
        out_specs=(P("rows", "vecs"), P("vecs", "rows")),
        check_vma=False,
    )
```

```python
import functools

import jax
import jax.numpy as jnp
from jax import lax
from jax.experimental import pallas as pl
from jax.experimental.pallas import tpu as pltpu
from jax.sharding import PartitionSpec as P

BLOCK = 128
REACH = 4
ORDER = 6
LANES = 128
SIZE = REACH * BLOCK
SPARE = 32
F32 = jnp.float32
BF16 = jnp.bfloat16
WHOLE = pl.BlockSpec(memory_space=pltpu.VMEM)
ANYWHERE = pl.BlockSpec(memory_space=pl.ANY)
SCALARS = pl.BlockSpec(memory_space=pltpu.SMEM)


def shaped(shape, dtype=F32):
    return jax.ShapeDtypeStruct(shape, dtype)


def cost(flops, moved):
    return pl.CostEstimate(flops=flops, bytes_accessed=moved, transcendentals=0)


class Call:
    def __init__(self, chain):
        self.chain = chain
        self.args, self.specs, self.outs, self.out_specs, self.aliases = [], [], [], [], {}

    def anywhere(self, *arrays):
        self.args += arrays
        self.specs += [ANYWHERE] * len(arrays)
        return self

    def scalars(self, *arrays):
        self.args += arrays
        self.specs += [SCALARS] * len(arrays)
        return self

    def reads(self, *arrays):
        self.args += arrays
        self.specs += [WHOLE] * len(arrays)
        return self

    def writes(self, shape, before=None, spec=WHOLE):
        if before is not None:
            self.aliases[len(self.args)] = len(self.outs)
            self.args.append(before)
            self.specs.append(spec)
        self.outs.append(shape)
        self.out_specs.append(spec)
        return self

    def passes(self, *arrays):
        for array in arrays:
            self.writes(shaped(array.shape, array.dtype), array, ANYWHERE)
        return self

    def __call__(self, body, name, estimate, scratch=(), mib=16):
        if self.chain.token is not None:
            self.anywhere(self.chain.token)
        self.writes(shaped((8, LANES)))
        count = len(self.args)

        def kernel(*refs):
            ins, outs = refs[:count], refs[count : count + len(self.outs)]
            outs[-1][...] = jnp.zeros((8, LANES), F32)
            body(ins, outs[:-1], refs[count + len(self.outs) :])

        *results, self.chain.token = pl.pallas_call(
            kernel,
            in_specs=self.specs,
            out_specs=self.out_specs,
            out_shape=self.outs,
            scratch_shapes=scratch,
            input_output_aliases=self.aliases,
            compiler_params=pltpu.CompilerParams(vmem_limit_bytes=mib * 1024 * 1024),
            cost_estimate=estimate,
            name=name,
        )(*self.args)
        return results


class Chain:
    token = None


def two_parts(x):
    high = x.astype(BF16)
    low = (x - high.astype(F32)).astype(BF16)
    return high, low


def put_parts(ref, start, value):
    high, low = two_parts(value)
    ref[pl.ds(start, value.shape[0]), :LANES] = high
    ref[pl.ds(start, value.shape[0]), LANES:] = low


def prepare(shape, chain, table, hamiltonian, vectors):
    rows, per_row = hamiltonian.shape[:2]
    strips, slots = rows // REACH, 4
    far = [pltpu.with_memory_space_constraint(x, pltpu.HBM) for x in (hamiltonian, vectors)]
    call = Call(chain).scalars(table).anywhere(*far)
    call.writes(shaped((rows, 2 * BLOCK, per_row * BLOCK), BF16)).writes(shaped(vectors.shape))
    for _ in range(shape.chunks):
        call.writes(shaped((vectors.shape[0] + 2 * SIZE, 2 * LANES), BF16))
    for _ in range(2 * (shape.chunks - 1)):
        call.writes(shaped((SIZE, LANES)))

    def body(ins, outs, scratch):
        h_ref, v_ref = ins[1], ins[2]
        parts_h, copy_v = outs[:2]
        held, sems, v_sem = scratch

        def fetch(g):
            slot = lax.rem(g, slots)
            return pltpu.make_async_copy(h_ref.at[pl.ds(g * REACH, REACH)], held.at[slot], sems.at[slot])

        def split(g, carry):
            slot = lax.rem(g, slots)
            fetch(g).wait()
            for r in range(REACH):
                for k in range(per_row):
                    high, low = two_parts(held[slot, r, k])
                    parts_h[g * REACH + r, :BLOCK, k * BLOCK : (k + 1) * BLOCK] = high
                    parts_h[g * REACH + r, BLOCK:, k * BLOCK : (k + 1) * BLOCK] = low

            @pl.when(g + slots < strips)
            def _():
                fetch(g + slots).start()

            return carry

        def split_v(g, carry):
            at = pl.multiple_of(g * SIZE, SIZE)
            for c in range(shape.chunks):
                put_parts(outs[2 + c], pl.multiple_of(at + SIZE, SIZE), copy_v[pl.ds(at, SIZE), c * LANES : (c + 1) * LANES])
            return carry

        copy = pltpu.make_async_copy(v_ref, copy_v, v_sem)
        for g in range(min(slots, strips)):
            fetch(jnp.int32(g)).start()
        copy.start()
        lax.fori_loop(0, strips // 2, split, 0)
        copy.wait()
        lax.fori_loop(0, strips, split_v, 0)
        for c in range(1, shape.chunks):
            lanes = slice(c * LANES, (c + 1) * LANES)
            outs[shape.chunks + 2 * c][...] = copy_v[:SIZE, lanes]
            outs[shape.chunks + 2 * c + 1][...] = copy_v[-SIZE:, lanes]
        lax.fori_loop(strips // 2, strips, split, 0)

    scratch = [pltpu.VMEM((slots, REACH, *hamiltonian.shape[1:]), F32), pltpu.SemaphoreType.DMA((slots,)), pltpu.SemaphoreType.DMA]
    out = call(body, "prepare", cost(0, 8 * hamiltonian.size), scratch)
    sends = out[2 + shape.chunks :]
    return out[0], out[1], out[2 : 2 + shape.chunks], [sends[2 * c : 2 * c + 2] for c in range(shape.chunks - 1)]


def scales(step, coef_ref):
    here, by = coef_ref[ORDER - step], 2.0
    if step == 1:
        by = 2.0 * coef_ref[ORDER]
    elif step == 2:
        here = here - coef_ref[ORDER]
    elif step == ORDER:
        by = 1.0
    return here, by


def new_rows(step, chunk, common, parts_ref, row, q):
    table_ref, coef_ref, h_ref, v_ref = common
    per_row = h_ref.shape[2] // BLOCK
    base = (row // REACH) * REACH
    picked = []
    for k in range(per_row):
        start = pl.multiple_of((table_ref[row * per_row + k] + base) * BLOCK, BLOCK)
        picked.append(parts_ref[pl.ds(start, BLOCK), :])
    both = jnp.dot(h_ref[row], jnp.concatenate(picked, axis=0), preferred_element_type=F32)
    top, bottom = both[:BLOCK], both[BLOCK:]
    total = top[:, :LANES] + ((top[:, LANES:] + bottom[:, :LANES]) + bottom[:, LANES:])
    here, by = scales(step, coef_ref)
    whole = pl.ds(pl.multiple_of(row * BLOCK, BLOCK), BLOCK)
    value = here * v_ref[whole, chunk * LANES : (chunk + 1) * LANES] + by * total
    return value if q is None else value - q


def unrolled(first, count, one):
    unroll = max(n for n in range(1, 13) if count % n == 0)

    def some(i, carry):
        for u in range(unroll):
            one(first + i * unroll + u)
        return carry

    lax.fori_loop(0, count // unroll, some, 0)


def at_rows(block, size=BLOCK):
    return pl.ds(pl.multiple_of(block * BLOCK, BLOCK), size)


class Shape:
    def __init__(self, block_rows, per_row, width, groups):
        self.rows = block_rows
        self.inner = block_rows - 2 * REACH
        self.core = block_rows - 4 * REACH
        self.chunks = width // LANES
        self.width = width
        self.vec_bits = (groups - 1).bit_length()
        self.bits_at = block_rows * per_row


def put_sends(shape, table_ref, source_ref, sends, lanes):
    half = source_ref.shape[0] // 2
    for b, ref, at in sends:
        other = 1 - table_ref[shape.bits_at + b]
        rows = pl.ds(pl.multiple_of(other * half, BLOCK), half)
        ref[at : at + half, lanes if ref.shape[1] == source_ref.shape[1] else slice(None)] = source_ref[rows, lanes]


def interior(step, chunk, shape, chain, common, parts, q):
    call = Call(chain).scalars(*common[:2]).reads(*common[2:], parts)
    if q is not None:
        call.reads(q)
    call.writes(shaped((shape.inner * BLOCK, LANES))).writes(shaped(parts.shape, BF16))

    def body(ins, outs, scratch):
        def one(row):
            old = None if q is None else ins[5][at_rows(row - REACH), :]
            value = new_rows(step, chunk, ins[:4], ins[4], row, old)
            outs[0][at_rows(row - REACH), :] = value
            put_parts(outs[1], pl.multiple_of((row + REACH) * BLOCK, BLOCK), value)

        unrolled(REACH, shape.inner, one)

    flops = 8 * shape.inner * BLOCK * LANES * common[2].shape[2]
    return call(body, "interior", cost(flops, 8 * common[2].size))


def core_rows(step, chunk, shape, chain, common, parts, q, mid, before):
    call = Call(chain).scalars(*common[:2]).reads(*common[2:], parts, q, mid).writes(shaped(parts.shape, BF16))
    core = shape.core * BLOCK
    before = before or [None, None]
    call.writes(shaped((core, shape.width)), before[0]).writes(shaped((core // 2, shape.width)), before[1])
    for _ in range(1, shape.vec_bits):
        call.writes(shaped((core // 2 + (shape.chunks - chunk) * SPARE, LANES)))
    lanes = slice(chunk * LANES, (chunk + 1) * LANES)

    def body(ins, outs, scratch):
        def one(row):
            value = new_rows(step - 1, chunk, ins[:4], ins[4], row, ins[5][at_rows(row - REACH), :])
            put_parts(outs[0], pl.multiple_of((row + REACH) * BLOCK, BLOCK), value)

        def two(row):
            old = ins[6][at_rows(row - REACH), :]
            outs[1][at_rows(row - 2 * REACH), lanes] = new_rows(step, chunk, ins[:4], outs[0], row, old)

        unrolled(REACH, shape.inner, one)
        unrolled(2 * REACH, shape.core, two)
        put_sends(shape, ins[0], outs[1], [(b, outs[2 + b], 0) for b in range(shape.vec_bits)], lanes)

    out = call(body, "core_rows", cost(0, 0))
    return (None, out[0]), out[1:3], out[3:]


def ring(step, chunk, shape, chain, common, parts, mid, before):
    call = Call(chain).scalars(*common[:2]).reads(*common[2:], parts, mid)
    before = before or [None] * (1 + shape.vec_bits)
    for n, one_before in enumerate(before):
        call.writes(shaped((2 * SIZE if n < 2 else SIZE, shape.width)), one_before)
    lanes = slice(chunk * LANES, (chunk + 1) * LANES)

    def body(ins, outs, scratch):
        for side, first in enumerate((REACH, shape.rows - 2 * REACH)):
            for r in range(REACH):
                row = first + r
                old = ins[5][at_rows(row - REACH), :]
                rows = pl.ds((side * REACH + r) * BLOCK, BLOCK)
                outs[0][rows, lanes] = new_rows(step, chunk, ins[:4], ins[4], row, old)
        put_sends(shape, ins[0], outs[0], [(b, outs[1 + b], 0) for b in range(shape.vec_bits)], lanes)

    return call(body, "ring", cost(0, 0))


def border(step, chunk, shape, chain, common, halo, q, parts, following, joined=None):
    call = Call(chain).scalars(*common[:2]).reads(*common[2:], *halo)
    if q is not None:
        call.reads(*q)
    call.writes(shaped(parts.shape, BF16), parts).writes(shaped(parts.shape, BF16), following)
    for before in joined or (None, None):
        call.writes(shaped((SIZE, shape.width if joined else LANES)), before)
    lanes = slice(chunk * LANES, (chunk + 1) * LANES) if joined else slice(None)

    def body(ins, outs, scratch):
        put_parts(outs[0], 0, ins[4][...])
        put_parts(outs[0], (shape.rows + REACH) * BLOCK, ins[5][...])
        for side, first in enumerate((0, shape.rows - REACH)):
            for r in range(REACH):
                rows = slice(r * BLOCK, (r + 1) * BLOCK)
                old = None if q is None else ins[6 + side][rows]
                value = new_rows(step, chunk, ins[:4], outs[0], first + r, old)
                outs[2 + side][rows, lanes] = value
                put_parts(outs[1], (first + r + REACH) * BLOCK, value)

    flops = 16 * SIZE * LANES * common[2].shape[2]
    _, following, low, high = call(body, "border", cost(flops, 4 * common[2].size))
    return low, high, following


def last_border(step, chunk, shape, chain, common, halo, q, parts, near, before, got, passed):
    call = Call(chain).scalars(*common[:2]).reads(*common[2:], *halo, *q)
    got_at = len(call.args)
    for arrays in got:
        call.reads(*arrays)
    call.writes(shaped(parts.shape, BF16), parts).writes(shaped(near.shape), near)
    before = before or [None] * shape.vec_bits
    for n, one_before in enumerate(before):
        call.writes(shaped((SIZE if n else 2 * SIZE, shape.width)), one_before)
    got_to = len(call.outs)
    for arrays in got:
        call.writes(shaped((shape.core * BLOCK // 2, shape.width)))
    call.passes(*passed)
    lanes = slice(chunk * LANES, (chunk + 1) * LANES)

    def body(ins, outs, scratch):
        put_parts(outs[0], 0, ins[4][:SIZE, lanes])
        put_parts(outs[0], (shape.rows + REACH) * BLOCK, ins[5][:SIZE, lanes])
        for side, first in enumerate((0, shape.rows - REACH)):
            for r in range(REACH):
                old = ins[6 + side][r * BLOCK : (r + 1) * BLOCK]
                rows = pl.ds((side * REACH + r) * BLOCK, BLOCK)
                outs[2][rows, lanes] = new_rows(step, chunk, ins[:4], outs[0], first + r, old)
        sends = [(0, outs[1], SIZE)] + [(b, outs[2 + b], 0) for b in range(1, shape.vec_bits)]
        put_sends(shape, ins[0], outs[2], sends, lanes)
        for n, arrays in enumerate(got):
            for c in range(len(arrays)):
                rows = slice(0, shape.core * BLOCK // 2)
                outs[got_to + n][:, c * LANES : (c + 1) * LANES] = ins[got_at + n * len(arrays) + c][rows]

    out = call(body, "last_border", cost(0, 0))
    joined, passed = out[got_to : got_to + len(got)], out[got_to + len(got) :][: len(passed)]
    return out[1], out[2 : 2 + shape.vec_bits], joined, passed


def gram_sums(shape, chain, table, kinds, own, got, before, piece, result=(), both=False):
    width = shape.width
    call = Call(chain).scalars(table).reads(*own)
    places = {}
    for d in kinds:
        if d:
            for n, (arrays, offset) in enumerate(got[d]):
                places[d, n] = (len(call.args), len(arrays), offset)
                call.reads(*arrays)
    before_at = len(call.args)
    if before is not None:
        call.reads(before)
    if piece:
        kept = shaped((len(kinds) * width // piece // 2, width // 2 if both else width, piece))
        for _ in range(4 if both else 2):
            call.writes(kept)
    else:
        call.writes(shaped((len(kinds), width, width)))
    result_at = len(call.args)
    for array, *_ in result:
        call.reads(array)
    if result:
        call.writes(shaped((shape.rows * BLOCK, width)), None, ANYWHERE)

    def products(left, right):
        total = jnp.dot(left[0], right[1], preferred_element_type=F32)
        total += jnp.dot(left[1], right[0], preferred_element_type=F32)
        return total + jnp.dot(left[0], right[0], preferred_element_type=F32)

    def body(ins, outs, scratch):
        table_ref = ins[0]
        copies = []
        for n, (_, start, rows, to) in enumerate(result):
            source = ins[result_at + n].at[pl.ds(start, rows)]
            copies.append(pltpu.make_async_copy(source, outs[-1].at[pl.ds(to, rows)], scratch[0].at[n]))
            copies[-1].start()
        totals = [ins[before_at][n] if before is not None else jnp.zeros((width, width), F32) for n in range(len(kinds))]
        for n in range(len(own)):
            ref = ins[1 + n]
            half = ref.shape[0] // 2
            for at in range(0, half, SIZE):
                sides = [ref[at : at + SIZE], ref[half + at : half + at + SIZE]]
                chosen = {}
                for m, d in enumerate(kinds):
                    if d == 0:
                        for side in sides:
                            totals[m] += 0.5 * products(two_parts(side.T), two_parts(side))
                        continue
                    b = d.bit_length() - 1
                    if b not in chosen:
                        first = table_ref[shape.bits_at + b] == 0
                        chosen[b] = two_parts(jnp.where(first, sides[0], sides[1]).T)
                    where, count, offset = places[d, n]
                    other = [ins[where + c][offset + at : offset + at + SIZE] for c in range(count)]
                    other = other[0] if count == 1 else jnp.concatenate(other, axis=1)
                    totals[m] += products(chosen[b], two_parts(other))
        bit_at = shape.bits_at + shape.vec_bits
        for m in range(0, len(kinds) if both else 0, 2):
            first, second = table_ref[bit_at] == 0, table_ref[bit_at + 1] == 0
            half = width // 2
            for n in range(2):
                one, two = totals[m + n][:half, :piece], totals[m + n][:half, piece:]
                outs[0][m + n] = jnp.where(first, one, two)
                outs[1][m + n] = jnp.where(first, two, one)
                columns = slice(n * piece, (n + 1) * piece)
                one, two = totals[m][half:, columns], totals[m + 1][half:, columns]
                outs[2][m + n] = jnp.where(second, one, two)
                outs[3][m + n] = jnp.where(second, two, one)
        for m, total in enumerate([] if both else totals):
            if not piece:
                outs[0][m] = total
                continue
            pairs = width // piece // 2
            even = table_ref[bit_at] == 0
            for t in range(pairs):
                one = total[:, 2 * t * piece : (2 * t + 1) * piece]
                two = total[:, (2 * t + 1) * piece : (2 * t + 2) * piece]
                outs[0][m * pairs + t] = jnp.where(even, one, two)
                outs[1][m * pairs + t] = jnp.where(even, two, one)
        for copy in copies:
            copy.wait()

    rows = sum(a.shape[0] for a in own)
    flops = 3 * rows * width * width * (len(kinds) + 1)
    scratch = [pltpu.SemaphoreType.DMA((len(result),))] if result else []
    out = call(body, "gram_sums", cost(flops, 8 * rows * width), scratch)
    return out if piece or result else out[0]


def fold(shape, chain, table, level, pairs, passed=()):
    call = Call(chain).scalars(table)
    count = sum(arrays[0].shape[0] for arrays in pairs)
    for arrays in pairs:
        call.reads(*arrays)
    rows = sum(a.shape[1] for a in pairs[0][::2])
    half = shaped((count // 2, rows, pairs[0][0].shape[2]))
    call.writes(half).writes(half).passes(*passed)

    def body(ins, outs, scratch):
        bit_at = shape.bits_at + shape.vec_bits
        even = ins[0][bit_at + level] == 0
        sums, at = [], 1
        for arrays in pairs:
            for m in range(arrays[0].shape[0]):
                parts = [ins[at + n][m] + ins[at + n + 1][m] for n in range(0, len(arrays), 2)]
                sums.append(jnp.concatenate(parts, axis=0) if len(parts) > 1 else parts[0])
            at += len(arrays)
        for n in range(count // 2):
            outs[0][n] = jnp.where(even, sums[2 * n], sums[2 * n + 1])
            outs[1][n] = jnp.where(even, sums[2 * n + 1], sums[2 * n])

    return call(body, "fold", cost(0, 8 * count * pairs[0][0][0].size))


def fold_two(shape, chain, table, upper, lower):
    half = shaped((upper[0].shape[0] // 2, *upper[0].shape[1:]))
    call = Call(chain).scalars(table).reads(*upper, *lower)
    for _ in range(4):
        call.writes(half)

    def body(ins, outs, scratch):
        bit_at = shape.bits_at + shape.vec_bits
        for n, level in enumerate((1, 0)):
            even = ins[0][bit_at + level] == 0
            keep, got = ins[1 + 2 * n], ins[2 + 2 * n]
            for m in range(half.shape[0]):
                one, two = keep[2 * m] + got[2 * m], keep[2 * m + 1] + got[2 * m + 1]
                outs[2 * n][m] = jnp.where(even, one, two)
                outs[2 * n + 1][m] = jnp.where(even, two, one)

    return call(body, "fold_two", cost(0, 0))


def add_blocks(chain, table, keep, got, tiles):
    rows, columns = keep.shape[1:]
    size = rows // tiles
    call = Call(chain).scalars(table).reads(keep, got).writes(shaped((rows, columns)))
    for _ in range(tiles):
        call.writes(shaped((size, columns)))

    def body(ins, outs, scratch):
        outs[0][...] = ins[1][0] + ins[2][0]
        for n in range(tiles):
            number = lax.rem(ins[0][ins[0].shape[0] - 1] + n, tiles)
            outs[1 + n][...] = outs[0][pl.ds(pl.multiple_of(number * size, size), size), :]

    return call(body, "add_blocks", cost(0, 0))


def assemble(chain, table, share, turned, scale):
    tiles = len(turned)
    rows, columns = share.shape
    size = rows // tiles
    call = Call(chain).scalars(table).reads(share, *turned).writes(shaped((rows, columns)))

    def body(ins, outs, scratch):
        number = ins[0][ins[0].shape[0] - 1]
        flipped = [ins[2 + n][...].T for n in range(tiles)]
        for t in range(tiles):
            which = lax.rem(number - t + tiles, tiles)
            tile = flipped[0]
            for n in range(1, tiles):
                tile = jnp.where(which == n, flipped[n], tile)
            at = slice(t * size, (t + 1) * size)
            outs[0][at] = (ins[1][at] + tile) * scale

    return call(body, "assemble", cost(0, 0))[0]


def on_device(hamiltonian, columns, vectors, coefficients):
    block_rows, per_row = columns.shape
    peers = lax.axis_size("rows")
    groups = lax.axis_size("vecs")
    total_blocks = block_rows * peers
    width = vectors.shape[1]
    shape = Shape(block_rows, per_row, width, groups)
    chunks = shape.chunks
    rows_at, vecs_at = lax.axis_index("rows"), lax.axis_index("vecs")
    up = [(i, (i + 1) % peers) for i in range(peers)]
    down = [(j, i) for i, j in up]

    def exchange(first, last):
        return lax.ppermute(last, "rows", up), lax.ppermute(first, "rows", down)

    chain = Chain()
    halo = [exchange(vectors[:SIZE, :LANES], vectors[-SIZE:, :LANES])]

    local = jnp.arange(block_rows, dtype=jnp.int32)
    offsets = (columns - (rows_at * block_rows + local)[:, None] + REACH) % total_blocks
    slots = (offsets + (local % REACH)[:, None]).reshape(-1)
    per_group = peers // groups
    piece = width // per_group
    wanted = rows_at ^ (vecs_at * per_group)
    levels = (peers - 1).bit_length()
    bits = [(vecs_at >> b) & 1 for b in range(shape.vec_bits)] + [(wanted >> b) & 1 for b in range(levels)]
    bits.append(rows_at % per_group)
    table = jnp.concatenate([slots, jnp.stack(bits).astype(jnp.int32)])

    parts_h, vectors, parts, sends = prepare(shape, chain, table, hamiltonian, vectors)
    halo += [exchange(*strips) for strips in sends]
    common = (table, coefficients, parts_h, vectors)

    terms, older, inner, core_sends = ([None] * chunks for _ in range(4))
    core = rims = ends = None
    wide = (None, None)

    def swapped(x, distance):
        return lax.ppermute(x, "vecs", [(i, i ^ distance) for i in range(groups)])

    def received(sends):
        return {d: swapped(sends[d.bit_length() - 2], d) for d in range(2, groups, 2)}

    def forwarded(got):
        out = {}
        for d, rows in got.items():
            out[d], out[d + 1] = rows, swapped(rows, 1)
        return out

    def inside(step, c):
        nonlocal core, rims
        q = older[c] and older[c][1]
        if step < ORDER - 1:
            inner[c] = interior(step, c, shape, chain, common, parts[c], q)
        elif step == ORDER - 1:
            inner[c], core, core_sends[c] = core_rows(ORDER, c, shape, chain, common, parts[c], q, terms[c][1], core)
        else:
            rims = ring(step, c, shape, chain, common, parts[c], q, rims)

    for step in range(1, ORDER):
        for c in range(chunks):
            inside(step, c)
            q = older[c] and (older[c][0], older[c][2])
            late = step == ORDER - 1
            low, high, following = border(
                step, c, shape, chain, common, halo[c], q, parts[c], inner[c][1], wide if late else ()
            )
            if late:
                wide = (low, high)
            else:
                halo[c] = exchange(low, high)
            older[c], terms[c], parts[c] = terms[c], (low, inner[c][0], high), following
    last_halo = exchange(*wide)
    got_core = [received(sends) for sends in core_sends]
    for c in range(chunks):
        inside(ORDER, c)
    got_rims = received(rims[2:])
    near = rims[1]
    for c in range(chunks):
        q = (older[c][0], older[c][2])
        got = [[rows[d] for rows in got_core] for d in range(2, groups, 2)] if c == 0 else []
        passed = [core[1], *got_rims.values()] if c == chunks - 1 else []
        near, ends, joined, passed = last_border(
            ORDER, c, shape, chain, common, last_halo, q, parts[c], near, ends, got, passed
        )
        if c == 0:
            all_core = {2 * n + 2: rows for n, rows in enumerate(joined)}
    near_core = passed[0]
    got_core = forwarded(all_core)
    got_rims = forwarded(dict(zip(got_rims, passed[1:])))
    got_ends = received(ends[1:])

    kinds, far = tuple(range(min(2, groups))), tuple(range(2, groups))
    swaps = [[(i, i ^ (1 << level)) for i in range(peers)] for level in range(levels)]
    near_core, near = swapped(near_core, 1), swapped(near, 1)
    last = block_rows * BLOCK - SIZE
    result = [(core[0], 0, core[0].shape[0], 2 * SIZE), (rims[0], 0, SIZE, SIZE), (rims[0], SIZE, SIZE, last - SIZE)]
    result += [(ends[0], 0, SIZE, 0), (ends[0], SIZE, SIZE, last)]
    arrived = {1: [([near_core], 0), ([near], 0), ([near], SIZE)]}
    whole = [] if far else result
    keep, send, *rest = gram_sums(shape, chain, table, kinds, [core[0], rims[0], ends[0]], arrived, None, piece, whole)
    shares = [(keep, lax.ppermute(send, "rows", swaps[0]))]
    if far:
        arrived = {d: [([got_core[d]], 0), ([got_rims[d]], 0)] for d in far}
        sums, *rest = gram_sums(shape, chain, table, far, [core[0], rims[0]], arrived, None, 0, result)
        keep, send, *rows = fold(shape, chain, table, 1, shares, got_ends.values())
        shares = [(keep, lax.ppermute(send, "rows", swaps[1]))]
        got_ends = forwarded(dict(zip(got_ends, rows)))
        arrived = {d: [([got_ends[d]], 0)] for d in far}
        both = per_group == 2 and levels > 2
        made = gram_sums(shape, chain, table, far, [ends[0]], arrived, sums, piece, (), both)
        if both:
            upper = (made[0], lax.ppermute(made[1], "rows", swaps[0]))
            lower = (made[2], lax.ppermute(made[3], "rows", swaps[1]))
            made = fold_two(shape, chain, table, upper, lower)
            shares.append(
                (made[0], lax.ppermute(made[1], "rows", swaps[1]), made[2], lax.ppermute(made[3], "rows", swaps[0]))
            )
        else:
            shares.append((made[0], lax.ppermute(made[1], "rows", swaps[0])))
    filtered = rest[0]

    for level in range(1, levels - 1):
        ahead = [pair for n, pair in enumerate(shares) if level == 1 and len(shares) > 1 and (n == 0 or len(pair) > 2)]
        if len(ahead) == len(shares):
            continue
        joined = [shares] if shares[0][0].shape[0] == 1 and not ahead else [[pair] for pair in shares[len(ahead) :]]
        folded = [fold(shape, chain, table, level, pairs) for pairs in joined]
        shares = ahead + [(keep, lax.ppermute(send, "rows", swaps[level])) for keep, send in folded]

    keep, send = fold(shape, chain, table, levels - 1, shares)
    share, *tiles = add_blocks(chain, table, keep, lax.ppermute(send, "rows", swaps[-1]), per_group)
    turned = []
    for n in range(per_group):
        pairs = []
        for i in range(peers):
            for g in range(groups):
                to = (g * per_group + (i + n) % per_group) * groups + i // per_group
                pairs.append((i * groups + g, to))
        turned.append(lax.ppermute(tiles[n], ("rows", "vecs"), pairs))
    gram = assemble(chain, table, share, turned, 1.0 / (total_blocks * BLOCK))
    return filtered, gram


def solution(mesh):
    return jax.shard_map(
        on_device,
        mesh=mesh,
        in_specs=(P("rows", None, None, None), P("rows", None), P("rows", "vecs"), P()),
        out_specs=(P("rows", "vecs"), P("vecs", "rows")),
        check_vma=False,
    )
```

```python
import functools

import jax
import jax.numpy as jnp
from jax import lax
from jax.experimental import pallas as pl
from jax.experimental.pallas import tpu as pltpu
from jax.sharding import PartitionSpec as P

BLOCK = 128
REACH = 4
ORDER = 6
LANES = 128
SIZE = REACH * BLOCK
SPARE = 32
EARLY = 32
F32 = jnp.float32
BF16 = jnp.bfloat16
WHOLE = pl.BlockSpec(memory_space=pltpu.VMEM)
ANYWHERE = pl.BlockSpec(memory_space=pl.ANY)
SCALARS = pl.BlockSpec(memory_space=pltpu.SMEM)


def shaped(shape, dtype=F32):
    return jax.ShapeDtypeStruct(shape, dtype)


def cost(flops, moved):
    return pl.CostEstimate(flops=flops, bytes_accessed=moved, transcendentals=0)


class Call:
    def __init__(self, chain):
        self.chain = chain
        self.args, self.specs, self.outs, self.out_specs, self.aliases = [], [], [], [], {}

    def anywhere(self, *arrays):
        self.args += arrays
        self.specs += [ANYWHERE] * len(arrays)
        return self

    def scalars(self, *arrays):
        self.args += arrays
        self.specs += [SCALARS] * len(arrays)
        return self

    def reads(self, *arrays):
        self.args += arrays
        self.specs += [WHOLE] * len(arrays)
        return self

    def writes(self, shape, before=None, spec=WHOLE):
        if before is not None:
            self.aliases[len(self.args)] = len(self.outs)
            self.args.append(before)
            self.specs.append(spec)
        self.outs.append(shape)
        self.out_specs.append(spec)
        return self

    def passes(self, *arrays):
        for array in arrays:
            self.writes(shaped(array.shape, array.dtype), array, ANYWHERE)
        return self

    def __call__(self, body, name, estimate, scratch=(), mib=16):
        if self.chain.token is not None:
            self.anywhere(self.chain.token)
        self.writes(shaped((8, LANES)))
        count = len(self.args)

        def kernel(*refs):
            ins, outs = refs[:count], refs[count : count + len(self.outs)]
            outs[-1][...] = jnp.zeros((8, LANES), F32)
            body(ins, outs[:-1], refs[count + len(self.outs) :])

        *results, self.chain.token = pl.pallas_call(
            kernel,
            in_specs=self.specs,
            out_specs=self.out_specs,
            out_shape=self.outs,
            scratch_shapes=scratch,
            input_output_aliases=self.aliases,
            compiler_params=pltpu.CompilerParams(vmem_limit_bytes=mib * 1024 * 1024),
            cost_estimate=estimate,
            name=name,
        )(*self.args)
        return results


class Chain:
    token = None


def two_parts(x):
    high = x.astype(BF16)
    low = (x - high.astype(F32)).astype(BF16)
    return high, low


def put_parts(ref, start, value):
    high, low = two_parts(value)
    ref[pl.ds(start, value.shape[0]), :LANES] = high
    ref[pl.ds(start, value.shape[0]), LANES:] = low


def prepare(shape, chain, table, hamiltonian, vectors):
    rows, per_row = hamiltonian.shape[:2]
    strips, slots = rows // REACH, 4
    far = [pltpu.with_memory_space_constraint(x, pltpu.HBM) for x in (hamiltonian, vectors)]
    call = Call(chain).scalars(table).anywhere(*far)
    call.writes(shaped((rows, 2 * BLOCK, per_row * BLOCK), BF16)).writes(shaped(vectors.shape))
    for _ in range(shape.chunks):
        call.writes(shaped((vectors.shape[0] + 2 * SIZE, 2 * LANES), BF16))
    for _ in range(2 * (shape.chunks - 1)):
        call.writes(shaped((SIZE, LANES)))

    def body(ins, outs, scratch):
        h_ref, v_ref = ins[1], ins[2]
        parts_h, copy_v = outs[:2]
        held, sems, v_sem = scratch

        def fetch(g):
            slot = lax.rem(g, slots)
            return pltpu.make_async_copy(h_ref.at[pl.ds(g * REACH, REACH)], held.at[slot], sems.at[slot])

        def split(g, carry):
            slot = lax.rem(g, slots)
            fetch(g).wait()
            for r in range(REACH):
                for k in range(per_row):
                    high, low = two_parts(held[slot, r, k])
                    parts_h[g * REACH + r, :BLOCK, k * BLOCK : (k + 1) * BLOCK] = high
                    parts_h[g * REACH + r, BLOCK:, k * BLOCK : (k + 1) * BLOCK] = low

            @pl.when(g + slots < strips)
            def _():
                fetch(g + slots).start()

            return carry

        def split_v(g, carry):
            at = pl.multiple_of(g * SIZE, SIZE)
            for c in range(shape.chunks):
                put_parts(outs[2 + c], pl.multiple_of(at + SIZE, SIZE), copy_v[pl.ds(at, SIZE), c * LANES : (c + 1) * LANES])
            return carry

        copy = pltpu.make_async_copy(v_ref, copy_v, v_sem)
        for g in range(min(slots, strips)):
            fetch(jnp.int32(g)).start()
        copy.start()
        lax.fori_loop(0, strips // 2, split, 0)
        copy.wait()
        lax.fori_loop(0, strips, split_v, 0)
        for c in range(1, shape.chunks):
            lanes = slice(c * LANES, (c + 1) * LANES)
            outs[shape.chunks + 2 * c][...] = copy_v[:SIZE, lanes]
            outs[shape.chunks + 2 * c + 1][...] = copy_v[-SIZE:, lanes]
        lax.fori_loop(strips // 2, strips, split, 0)

    scratch = [pltpu.VMEM((slots, REACH, *hamiltonian.shape[1:]), F32), pltpu.SemaphoreType.DMA((slots,)), pltpu.SemaphoreType.DMA]
    out = call(body, "prepare", cost(0, 8 * hamiltonian.size), scratch)
    sends = out[2 + shape.chunks :]
    return out[0], out[1], out[2 : 2 + shape.chunks], [sends[2 * c : 2 * c + 2] for c in range(shape.chunks - 1)]


def scales(step, coef_ref):
    here, by = coef_ref[ORDER - step], 2.0
    if step == 1:
        by = 2.0 * coef_ref[ORDER]
    elif step == 2:
        here = here - coef_ref[ORDER]
    elif step == ORDER:
        by = 1.0
    return here, by


def new_rows(step, chunk, common, parts_ref, row, q):
    table_ref, coef_ref, h_ref, v_ref = common
    per_row = h_ref.shape[2] // BLOCK
    base = (row // REACH) * REACH
    picked = []
    for k in range(per_row):
        start = pl.multiple_of((table_ref[row * per_row + k] + base) * BLOCK, BLOCK)
        picked.append(parts_ref[pl.ds(start, BLOCK), :])
    both = jnp.dot(h_ref[row], jnp.concatenate(picked, axis=0), preferred_element_type=F32)
    top, bottom = both[:BLOCK], both[BLOCK:]
    total = top[:, :LANES] + ((top[:, LANES:] + bottom[:, :LANES]) + bottom[:, LANES:])
    here, by = scales(step, coef_ref)
    whole = pl.ds(pl.multiple_of(row * BLOCK, BLOCK), BLOCK)
    value = here * v_ref[whole, chunk * LANES : (chunk + 1) * LANES] + by * total
    return value if q is None else value - q


def unrolled(first, count, one):
    unroll = max(n for n in range(1, 13) if count % n == 0)

    def some(i, carry):
        for u in range(unroll):
            one(first + i * unroll + u)
        return carry

    lax.fori_loop(0, count // unroll, some, 0)


def at_rows(block, size=BLOCK):
    return pl.ds(pl.multiple_of(block * BLOCK, BLOCK), size)


class Shape:
    def __init__(self, block_rows, per_row, width, groups):
        self.rows = block_rows
        self.inner = block_rows - 2 * REACH
        self.core = block_rows - 4 * REACH
        self.chunks = width // LANES
        self.width = width
        self.vec_bits = (groups - 1).bit_length()
        self.bits_at = block_rows * per_row


def put_sends(shape, table_ref, source_ref, sends, lanes):
    half = source_ref.shape[0] // 2
    for b, ref, at in sends:
        other = 1 - table_ref[shape.bits_at + b]
        rows = pl.ds(pl.multiple_of(other * half, BLOCK), half)
        ref[at : at + half, lanes if ref.shape[1] == source_ref.shape[1] else slice(None)] = source_ref[rows, lanes]


def interior(step, chunk, shape, chain, common, parts, q):
    call = Call(chain).scalars(*common[:2]).reads(*common[2:], parts)
    if q is not None:
        call.reads(q)
    call.writes(shaped((shape.inner * BLOCK, LANES))).writes(shaped(parts.shape, BF16))

    def body(ins, outs, scratch):
        def one(row):
            old = None if q is None else ins[5][at_rows(row - REACH), :]
            value = new_rows(step, chunk, ins[:4], ins[4], row, old)
            outs[0][at_rows(row - REACH), :] = value
            put_parts(outs[1], pl.multiple_of((row + REACH) * BLOCK, BLOCK), value)

        unrolled(REACH, shape.inner, one)

    flops = 8 * shape.inner * BLOCK * LANES * common[2].shape[2]
    return call(body, "interior", cost(flops, 8 * common[2].size))


def core_rows(step, chunk, shape, chain, common, parts, q, mid, before):
    call = Call(chain).scalars(*common[:2]).reads(*common[2:], parts, q, mid).writes(shaped(parts.shape, BF16))
    core = shape.core * BLOCK
    before = before or [None, None]
    call.writes(shaped((core, shape.width)), before[0]).writes(shaped((core // 2, shape.width)), before[1])
    for _ in range(1, shape.vec_bits):
        call.writes(shaped((core // 2 + (shape.chunks - chunk) * SPARE, LANES)))
    lanes = slice(chunk * LANES, (chunk + 1) * LANES)

    def body(ins, outs, scratch):
        def one(row):
            value = new_rows(step - 1, chunk, ins[:4], ins[4], row, ins[5][at_rows(row - REACH), :])
            put_parts(outs[0], pl.multiple_of((row + REACH) * BLOCK, BLOCK), value)

        def two(row):
            old = ins[6][at_rows(row - REACH), :]
            outs[1][at_rows(row - 2 * REACH), lanes] = new_rows(step, chunk, ins[:4], outs[0], row, old)

        unrolled(REACH, shape.inner, one)
        unrolled(2 * REACH, shape.core, two)
        put_sends(shape, ins[0], outs[1], [(b, outs[2 + b], 0) for b in range(shape.vec_bits)], lanes)

    out = call(body, "core_rows", cost(0, 0))
    return (None, out[0]), out[1:3], out[3:]


def ring(step, chunk, shape, chain, common, parts, mid, before):
    call = Call(chain).scalars(*common[:2]).reads(*common[2:], parts, mid)
    before = before or [None] * (1 + shape.vec_bits)
    for n, one_before in enumerate(before):
        call.writes(shaped((2 * SIZE if n < 2 else SIZE, shape.width)), one_before)
    lanes = slice(chunk * LANES, (chunk + 1) * LANES)

    def body(ins, outs, scratch):
        for side, first in enumerate((REACH, shape.rows - 2 * REACH)):
            for r in range(REACH):
                row = first + r
                old = ins[5][at_rows(row - REACH), :]
                rows = pl.ds((side * REACH + r) * BLOCK, BLOCK)
                outs[0][rows, lanes] = new_rows(step, chunk, ins[:4], ins[4], row, old)
        put_sends(shape, ins[0], outs[0], [(b, outs[1 + b], 0) for b in range(shape.vec_bits)], lanes)

    return call(body, "ring", cost(0, 0))


def border(step, chunk, shape, chain, common, halo, q, parts, following, joined=None):
    call = Call(chain).scalars(*common[:2]).reads(*common[2:], *halo)
    if q is not None:
        call.reads(*q)
    call.writes(shaped(parts.shape, BF16), parts).writes(shaped(parts.shape, BF16), following)
    call.writes(shaped((SIZE, shape.width if joined else LANES)), joined[0] if joined else None)
    call.writes(shaped((SIZE + (joined[1] if joined else 0), LANES)))
    lanes = slice(chunk * LANES, (chunk + 1) * LANES) if joined else slice(None)

    def body(ins, outs, scratch):
        put_parts(outs[0], 0, ins[4][...])
        put_parts(outs[0], (shape.rows + REACH) * BLOCK, ins[5][...])
        for side, first in enumerate((0, shape.rows - REACH)):
            for r in range(REACH):
                rows = slice(r * BLOCK, (r + 1) * BLOCK)
                old = None if q is None else ins[6 + side][rows]
                value = new_rows(step, chunk, ins[:4], outs[0], first + r, old)
                outs[2 + side][rows, slice(None) if side else lanes] = value
                put_parts(outs[1], (first + r + REACH) * BLOCK, value)

    flops = 16 * SIZE * LANES * common[2].shape[2]
    _, following, low, high = call(body, "border", cost(flops, 4 * common[2].size))
    return low, high, following


def last_border(step, chunk, shape, chain, common, halo, q, parts, near, before, got, passed):
    call = Call(chain).scalars(*common[:2]).reads(*common[2:], *halo, *q)
    got_at = len(call.args)
    for arrays in got:
        call.reads(*arrays)
    call.writes(shaped(parts.shape, BF16), parts).writes(shaped(near.shape), near)
    before = before or [None] * shape.vec_bits
    for n, one_before in enumerate(before):
        call.writes(shaped((SIZE if n else 2 * SIZE, shape.width)), one_before)
    got_to = len(call.outs)
    for arrays in got:
        call.writes(shaped((shape.core * BLOCK // 2, shape.width)))
    call.passes(*passed)
    lanes = slice(chunk * LANES, (chunk + 1) * LANES)

    def body(ins, outs, scratch):
        put_parts(outs[0], 0, ins[4][:SIZE])
        put_parts(outs[0], (shape.rows + REACH) * BLOCK, ins[5][:, lanes])
        for side, first in enumerate((0, shape.rows - REACH)):
            for r in range(REACH):
                old = ins[6 + side][r * BLOCK : (r + 1) * BLOCK]
                rows = pl.ds((side * REACH + r) * BLOCK, BLOCK)
                outs[2][rows, lanes] = new_rows(step, chunk, ins[:4], outs[0], first + r, old)
        sends = [(0, outs[1], SIZE)] + [(b, outs[2 + b], 0) for b in range(1, shape.vec_bits)]
        put_sends(shape, ins[0], outs[2], sends, lanes)
        for n, arrays in enumerate(got):
            for c in range(len(arrays)):
                rows = slice(0, shape.core * BLOCK // 2)
                outs[got_to + n][:, c * LANES : (c + 1) * LANES] = ins[got_at + n * len(arrays) + c][rows]

    out = call(body, "last_border", cost(0, 0))
    joined, passed = out[got_to : got_to + len(got)], out[got_to + len(got) :][: len(passed)]
    return out[1], out[2 : 2 + shape.vec_bits], joined, passed


def gram_sums(shape, chain, table, kinds, own, got, before, piece, result=(), both=False):
    width = shape.width
    call = Call(chain).scalars(table).reads(*own)
    places = {}
    for d in kinds:
        if d:
            for n, (arrays, offset) in enumerate(got[d]):
                places[d, n] = (len(call.args), len(arrays), offset)
                call.reads(*arrays)
    before_at = len(call.args)
    if before is not None:
        call.reads(before)
    if piece:
        kept = shaped((len(kinds) * width // piece // 2, width // 2 if both else width, piece))
        for _ in range(4 if both else 2):
            call.writes(kept)
    else:
        call.writes(shaped((len(kinds), width, width)))
    result_at = len(call.args)
    for array, *_ in result:
        call.reads(array)
    if result:
        call.writes(shaped((shape.rows * BLOCK, width)), None, ANYWHERE)

    def products(left, right):
        total = jnp.dot(left[0], right[1], preferred_element_type=F32)
        total += jnp.dot(left[1], right[0], preferred_element_type=F32)
        return total + jnp.dot(left[0], right[0], preferred_element_type=F32)

    def body(ins, outs, scratch):
        table_ref = ins[0]
        copies = []
        for n, (_, start, rows, to) in enumerate(result):
            source = ins[result_at + n].at[pl.ds(start, rows)]
            copies.append(pltpu.make_async_copy(source, outs[-1].at[pl.ds(to, rows)], scratch[0].at[n]))
            copies[-1].start()
        totals = [ins[before_at][n] if before is not None else jnp.zeros((width, width), F32) for n in range(len(kinds))]
        for n in range(len(own)):
            ref = ins[1 + n]
            half = ref.shape[0] // 2
            for at in range(0, half, SIZE):
                sides = [ref[at : at + SIZE], ref[half + at : half + at + SIZE]]
                chosen = {}
                for m, d in enumerate(kinds):
                    if d == 0:
                        for side in sides:
                            totals[m] += 0.5 * products(two_parts(side.T), two_parts(side))
                        continue
                    b = d.bit_length() - 1
                    if b not in chosen:
                        first = table_ref[shape.bits_at + b] == 0
                        chosen[b] = two_parts(jnp.where(first, sides[0], sides[1]).T)
                    where, count, offset = places[d, n]
                    other = [ins[where + c][offset + at : offset + at + SIZE] for c in range(count)]
                    other = other[0] if count == 1 else jnp.concatenate(other, axis=1)
                    totals[m] += products(chosen[b], two_parts(other))
        bit_at = shape.bits_at + shape.vec_bits
        for m in range(0, len(kinds) if both else 0, 2):
            first, second = table_ref[bit_at] == 0, table_ref[bit_at + 1] == 0
            half = width // 2
            for n in range(2):
                one, two = totals[m + n][:half, :piece], totals[m + n][:half, piece:]
                outs[0][m + n] = jnp.where(first, one, two)
                outs[1][m + n] = jnp.where(first, two, one)
                columns = slice(n * piece, (n + 1) * piece)
                one, two = totals[m][half:, columns], totals[m + 1][half:, columns]
                outs[2][m + n] = jnp.where(second, one, two)
                outs[3][m + n] = jnp.where(second, two, one)
        for m, total in enumerate([] if both else totals):
            if not piece:
                outs[0][m] = total
                continue
            pairs = width // piece // 2
            even = table_ref[bit_at] == 0
            for t in range(pairs):
                one = total[:, 2 * t * piece : (2 * t + 1) * piece]
                two = total[:, (2 * t + 1) * piece : (2 * t + 2) * piece]
                outs[0][m * pairs + t] = jnp.where(even, one, two)
                outs[1][m * pairs + t] = jnp.where(even, two, one)
        for copy in copies:
            copy.wait()

    rows = sum(a.shape[0] for a in own)
    flops = 3 * rows * width * width * (len(kinds) + 1)
    scratch = [pltpu.SemaphoreType.DMA((len(result),))] if result else []
    out = call(body, "gram_sums", cost(flops, 8 * rows * width), scratch)
    return out if piece or result else out[0]


def fold(shape, chain, table, level, pairs, passed=()):
    call = Call(chain).scalars(table)
    count = sum(arrays[0].shape[0] for arrays in pairs)
    for arrays in pairs:
        call.reads(*arrays)
    rows = sum(a.shape[1] for a in pairs[0][::2])
    half = shaped((count // 2, rows, pairs[0][0].shape[2]))
    call.writes(half).writes(half).passes(*passed)

    def body(ins, outs, scratch):
        bit_at = shape.bits_at + shape.vec_bits
        even = ins[0][bit_at + level] == 0
        sums, at = [], 1
        for arrays in pairs:
            for m in range(arrays[0].shape[0]):
                parts = [ins[at + n][m] + ins[at + n + 1][m] for n in range(0, len(arrays), 2)]
                sums.append(jnp.concatenate(parts, axis=0) if len(parts) > 1 else parts[0])
            at += len(arrays)
        for n in range(count // 2):
            outs[0][n] = jnp.where(even, sums[2 * n], sums[2 * n + 1])
            outs[1][n] = jnp.where(even, sums[2 * n + 1], sums[2 * n])

    return call(body, "fold", cost(0, 8 * count * pairs[0][0][0].size))


def fold_two(shape, chain, table, upper, lower):
    half = shaped((upper[0].shape[0] // 2, *upper[0].shape[1:]))
    call = Call(chain).scalars(table).reads(*upper, *lower)
    for _ in range(4):
        call.writes(half)

    def body(ins, outs, scratch):
        bit_at = shape.bits_at + shape.vec_bits
        for n, level in enumerate((1, 0)):
            even = ins[0][bit_at + level] == 0
            keep, got = ins[1 + 2 * n], ins[2 + 2 * n]
            for m in range(half.shape[0]):
                one, two = keep[2 * m] + got[2 * m], keep[2 * m + 1] + got[2 * m + 1]
                outs[2 * n][m] = jnp.where(even, one, two)
                outs[2 * n + 1][m] = jnp.where(even, two, one)

    return call(body, "fold_two", cost(0, 0))


def add_blocks(chain, table, keep, got, tiles):
    rows, columns = keep.shape[1:]
    size = rows // tiles
    call = Call(chain).scalars(table).reads(keep, got).writes(shaped((rows, columns)))
    for _ in range(tiles):
        call.writes(shaped((size, columns)))

    def body(ins, outs, scratch):
        outs[0][...] = ins[1][0] + ins[2][0]
        for n in range(tiles):
            number = lax.rem(ins[0][ins[0].shape[0] - 1] + n, tiles)
            outs[1 + n][...] = outs[0][pl.ds(pl.multiple_of(number * size, size), size), :]

    return call(body, "add_blocks", cost(0, 0))


def assemble(chain, table, share, turned, scale):
    tiles = len(turned)
    rows, columns = share.shape
    size = rows // tiles
    call = Call(chain).scalars(table).reads(share, *turned).writes(shaped((rows, columns)))

    def body(ins, outs, scratch):
        number = ins[0][ins[0].shape[0] - 1]
        flipped = [ins[2 + n][...].T for n in range(tiles)]
        for t in range(tiles):
            which = lax.rem(number - t + tiles, tiles)
            tile = flipped[0]
            for n in range(1, tiles):
                tile = jnp.where(which == n, flipped[n], tile)
            at = slice(t * size, (t + 1) * size)
            outs[0][at] = (ins[1][at] + tile) * scale

    return call(body, "assemble", cost(0, 0))[0]


def on_device(hamiltonian, columns, vectors, coefficients):
    block_rows, per_row = columns.shape
    peers = lax.axis_size("rows")
    groups = lax.axis_size("vecs")
    total_blocks = block_rows * peers
    width = vectors.shape[1]
    shape = Shape(block_rows, per_row, width, groups)
    chunks = shape.chunks
    rows_at, vecs_at = lax.axis_index("rows"), lax.axis_index("vecs")
    up = [(i, (i + 1) % peers) for i in range(peers)]
    down = [(j, i) for i, j in up]

    def exchange(first, last):
        return lax.ppermute(last, "rows", up), lax.ppermute(first, "rows", down)

    chain = Chain()
    halo = [exchange(vectors[:SIZE, :LANES], vectors[-SIZE:, :LANES])]

    local = jnp.arange(block_rows, dtype=jnp.int32)
    offsets = (columns - (rows_at * block_rows + local)[:, None] + REACH) % total_blocks
    slots = (offsets + (local % REACH)[:, None]).reshape(-1)
    per_group = peers // groups
    piece = width // per_group
    wanted = rows_at ^ (vecs_at * per_group)
    levels = (peers - 1).bit_length()
    bits = [(vecs_at >> b) & 1 for b in range(shape.vec_bits)] + [(wanted >> b) & 1 for b in range(levels)]
    bits.append(rows_at % per_group)
    table = jnp.concatenate([slots, jnp.stack(bits).astype(jnp.int32)])

    parts_h, vectors, parts, sends = prepare(shape, chain, table, hamiltonian, vectors)
    halo += [exchange(*strips) for strips in sends]
    common = (table, coefficients, parts_h, vectors)

    terms, older, inner, core_sends = ([None] * chunks for _ in range(4))
    core = rims = ends = None
    wide, before = None, [None] * chunks

    def swapped(x, distance):
        return lax.ppermute(x, "vecs", [(i, i ^ distance) for i in range(groups)])

    def received(sends):
        return {d: swapped(sends[d.bit_length() - 2], d) for d in range(2, groups, 2)}

    def forwarded(got):
        out = {}
        for d, rows in got.items():
            out[d], out[d + 1] = rows, swapped(rows, 1)
        return out

    def inside(step, c):
        nonlocal core, rims
        q = older[c] and older[c][1]
        if step < ORDER - 1:
            inner[c] = interior(step, c, shape, chain, common, parts[c], q)
        elif step == ORDER - 1:
            inner[c], core, core_sends[c] = core_rows(ORDER, c, shape, chain, common, parts[c], q, terms[c][1], core)
        else:
            rims = ring(step, c, shape, chain, common, parts[c], q, rims)

    for step in range(1, ORDER):
        for c in range(chunks):
            inside(step, c)
            q = older[c] and (older[c][0], older[c][2])
            late = step == ORDER - 1
            spare = (chunks - 1 - c) * EARLY
            low, high, following = border(
                step, c, shape, chain, common, halo[c], q, parts[c], inner[c][1], (wide, spare) if late else ()
            )
            if late:
                wide, before[c] = low, lax.ppermute(high, "rows", up)
            else:
                halo[c] = exchange(low, high)
            older[c], terms[c], parts[c] = terms[c], (low, inner[c][0], high), following
    after = lax.ppermute(wide, "rows", down)
    got_core = [received(sends) for sends in core_sends]
    for c in range(chunks):
        inside(ORDER, c)
    got_rims = received(rims[2:])
    near = rims[1]
    for c in range(chunks):
        q = (older[c][0], older[c][2])
        got = [[rows[d] for rows in got_core] for d in range(2, groups, 2)] if c == 0 else []
        passed = [core[1], *got_rims.values()] if c == chunks - 1 else []
        near, ends, joined, passed = last_border(
            ORDER, c, shape, chain, common, (before[c], after), q, parts[c], near, ends, got, passed
        )
        if c == 0:
            all_core = {2 * n + 2: rows for n, rows in enumerate(joined)}
    near_core = passed[0]
    got_core = forwarded(all_core)
    got_rims = forwarded(dict(zip(got_rims, passed[1:])))
    got_ends = received(ends[1:])

    kinds, far = tuple(range(min(2, groups))), tuple(range(2, groups))
    swaps = [[(i, i ^ (1 << level)) for i in range(peers)] for level in range(levels)]
    near_core, near = swapped(near_core, 1), swapped(near, 1)
    last = block_rows * BLOCK - SIZE
    result = [(core[0], 0, core[0].shape[0], 2 * SIZE), (rims[0], 0, SIZE, SIZE), (rims[0], SIZE, SIZE, last - SIZE)]
    result += [(ends[0], 0, SIZE, 0), (ends[0], SIZE, SIZE, last)]
    arrived = {1: [([near_core], 0), ([near], 0), ([near], SIZE)]}
    whole = [] if far else result
    keep, send, *rest = gram_sums(shape, chain, table, kinds, [core[0], rims[0], ends[0]], arrived, None, piece, whole)
    shares = [(keep, lax.ppermute(send, "rows", swaps[0]))]
    if far:
        arrived = {d: [([got_core[d]], 0), ([got_rims[d]], 0)] for d in far}
        sums, *rest = gram_sums(shape, chain, table, far, [core[0], rims[0]], arrived, None, 0, result)
        keep, send, *rows = fold(shape, chain, table, 1, shares, got_ends.values())
        shares = [(keep, lax.ppermute(send, "rows", swaps[1]))]
        got_ends = forwarded(dict(zip(got_ends, rows)))
        arrived = {d: [([got_ends[d]], 0)] for d in far}
        both = per_group == 2 and levels > 2
        made = gram_sums(shape, chain, table, far, [ends[0]], arrived, sums, piece, (), both)
        if both:
            upper = (made[0], lax.ppermute(made[1], "rows", swaps[0]))
            lower = (made[2], lax.ppermute(made[3], "rows", swaps[1]))
            made = fold_two(shape, chain, table, upper, lower)
            shares.append(
                (made[0], lax.ppermute(made[1], "rows", swaps[1]), made[2], lax.ppermute(made[3], "rows", swaps[0]))
            )
        else:
            shares.append((made[0], lax.ppermute(made[1], "rows", swaps[0])))
    filtered = rest[0]

    for level in range(1, levels - 1):
        ahead = [pair for n, pair in enumerate(shares) if level == 1 and len(shares) > 1 and (n == 0 or len(pair) > 2)]
        if len(ahead) == len(shares):
            continue
        joined = [shares] if shares[0][0].shape[0] == 1 and not ahead else [[pair] for pair in shares[len(ahead) :]]
        folded = [fold(shape, chain, table, level, pairs) for pairs in joined]
        shares = ahead + [(keep, lax.ppermute(send, "rows", swaps[level])) for keep, send in folded]

    keep, send = fold(shape, chain, table, levels - 1, shares)
    share, *tiles = add_blocks(chain, table, keep, lax.ppermute(send, "rows", swaps[-1]), per_group)
    turned = []
    for n in range(per_group):
        pairs = []
        for i in range(peers):
            for g in range(groups):
                to = (g * per_group + (i + n) % per_group) * groups + i // per_group
                pairs.append((i * groups + g, to))
        turned.append(lax.ppermute(tiles[n], ("rows", "vecs"), pairs))
    gram = assemble(chain, table, share, turned, 1.0 / (total_blocks * BLOCK))
    return filtered, gram


def solution(mesh):
    return jax.shard_map(
        on_device,
        mesh=mesh,
        in_specs=(P("rows", None, None, None), P("rows", None), P("rows", "vecs"), P()),
        out_specs=(P("rows", "vecs"), P("vecs", "rows")),
        check_vma=False,
    )
```

```python
import functools

import jax
import jax.numpy as jnp
from jax import lax
from jax.experimental import pallas as pl
from jax.experimental.pallas import tpu as pltpu
from jax.sharding import PartitionSpec as P

BLOCK = 128
REACH = 4
ORDER = 6
LANES = 128
SIZE = REACH * BLOCK
SPARE = 32
EARLY = 32
F32 = jnp.float32
BF16 = jnp.bfloat16
WHOLE = pl.BlockSpec(memory_space=pltpu.VMEM)
ANYWHERE = pl.BlockSpec(memory_space=pl.ANY)
SCALARS = pl.BlockSpec(memory_space=pltpu.SMEM)


def shaped(shape, dtype=F32):
    return jax.ShapeDtypeStruct(shape, dtype)


def cost(flops, moved):
    return pl.CostEstimate(flops=flops, bytes_accessed=moved, transcendentals=0)


class Call:
    def __init__(self, chain):
        self.chain = chain
        self.args, self.specs, self.outs, self.out_specs, self.aliases = [], [], [], [], {}

    def anywhere(self, *arrays):
        self.args += arrays
        self.specs += [ANYWHERE] * len(arrays)
        return self

    def scalars(self, *arrays):
        self.args += arrays
        self.specs += [SCALARS] * len(arrays)
        return self

    def reads(self, *arrays):
        self.args += arrays
        self.specs += [WHOLE] * len(arrays)
        return self

    def writes(self, shape, before=None, spec=WHOLE):
        if before is not None:
            self.aliases[len(self.args)] = len(self.outs)
            self.args.append(before)
            self.specs.append(spec)
        self.outs.append(shape)
        self.out_specs.append(spec)
        return self

    def passes(self, *arrays):
        for array in arrays:
            self.writes(shaped(array.shape, array.dtype), array, ANYWHERE)
        return self

    def __call__(self, body, name, estimate, scratch=(), mib=16):
        if self.chain.token is not None:
            self.anywhere(self.chain.token)
        self.writes(shaped((8, LANES)))
        count = len(self.args)

        def kernel(*refs):
            ins, outs = refs[:count], refs[count : count + len(self.outs)]
            outs[-1][...] = jnp.zeros((8, LANES), F32)
            body(ins, outs[:-1], refs[count + len(self.outs) :])

        *results, self.chain.token = pl.pallas_call(
            kernel,
            in_specs=self.specs,
            out_specs=self.out_specs,
            out_shape=self.outs,
            scratch_shapes=scratch,
            input_output_aliases=self.aliases,
            compiler_params=pltpu.CompilerParams(vmem_limit_bytes=mib * 1024 * 1024),
            cost_estimate=estimate,
            name=name,
        )(*self.args)
        return results


class Chain:
    token = None


def two_parts(x):
    high = x.astype(BF16)
    low = (x - high.astype(F32)).astype(BF16)
    return high, low


def put_parts(ref, start, value):
    high, low = two_parts(value)
    ref[pl.ds(start, value.shape[0]), :LANES] = high
    ref[pl.ds(start, value.shape[0]), LANES:] = low


def prepare(shape, chain, table, hamiltonian, vectors):
    rows, per_row = hamiltonian.shape[:2]
    strips, slots = rows // REACH, 4
    far = [pltpu.with_memory_space_constraint(x, pltpu.HBM) for x in (hamiltonian, vectors)]
    call = Call(chain).scalars(table).anywhere(*far)
    call.writes(shaped((rows, 2 * BLOCK, per_row * BLOCK), BF16)).writes(shaped(vectors.shape))
    for _ in range(shape.chunks):
        call.writes(shaped((vectors.shape[0] + 2 * SIZE, 2 * LANES), BF16))
    for _ in range(2 * (shape.chunks - 1)):
        call.writes(shaped((SIZE, LANES)))

    def body(ins, outs, scratch):
        h_ref, v_ref = ins[1], ins[2]
        parts_h, copy_v = outs[:2]
        held, sems, v_sem = scratch

        def fetch(g):
            slot = lax.rem(g, slots)
            return pltpu.make_async_copy(h_ref.at[pl.ds(g * REACH, REACH)], held.at[slot], sems.at[slot])

        def split(g, carry):
            slot = lax.rem(g, slots)
            fetch(g).wait()
            for r in range(REACH):
                for k in range(per_row):
                    high, low = two_parts(held[slot, r, k])
                    parts_h[g * REACH + r, :BLOCK, k * BLOCK : (k + 1) * BLOCK] = high
                    parts_h[g * REACH + r, BLOCK:, k * BLOCK : (k + 1) * BLOCK] = low

            @pl.when(g + slots < strips)
            def _():
                fetch(g + slots).start()

            return carry

        def split_v(g, carry):
            at = pl.multiple_of(g * SIZE, SIZE)
            for c in range(shape.chunks):
                put_parts(outs[2 + c], pl.multiple_of(at + SIZE, SIZE), copy_v[pl.ds(at, SIZE), c * LANES : (c + 1) * LANES])
            return carry

        copy = pltpu.make_async_copy(v_ref, copy_v, v_sem)
        for g in range(min(slots, strips)):
            fetch(jnp.int32(g)).start()
        copy.start()
        lax.fori_loop(0, strips // 2, split, 0)
        copy.wait()
        lax.fori_loop(0, strips, split_v, 0)
        for c in range(1, shape.chunks):
            lanes = slice(c * LANES, (c + 1) * LANES)
            outs[shape.chunks + 2 * c][...] = copy_v[:SIZE, lanes]
            outs[shape.chunks + 2 * c + 1][...] = copy_v[-SIZE:, lanes]
        lax.fori_loop(strips // 2, strips, split, 0)

    scratch = [pltpu.VMEM((slots, REACH, *hamiltonian.shape[1:]), F32), pltpu.SemaphoreType.DMA((slots,)), pltpu.SemaphoreType.DMA]
    out = call(body, "prepare", cost(0, 8 * hamiltonian.size), scratch)
    sends = out[2 + shape.chunks :]
    return out[0], out[1], out[2 : 2 + shape.chunks], [sends[2 * c : 2 * c + 2] for c in range(shape.chunks - 1)]


def scales(step, coef_ref):
    here, by = coef_ref[ORDER - step], 2.0
    if step == 1:
        by = 2.0 * coef_ref[ORDER]
    elif step == 2:
        here = here - coef_ref[ORDER]
    elif step == ORDER:
        by = 1.0
    return here, by


def new_rows(step, chunk, common, parts_ref, row, q):
    table_ref, coef_ref, h_ref, v_ref = common
    per_row = h_ref.shape[2] // BLOCK
    base = (row // REACH) * REACH
    picked = []
    for k in range(per_row):
        start = pl.multiple_of((table_ref[row * per_row + k] + base) * BLOCK, BLOCK)
        picked.append(parts_ref[pl.ds(start, BLOCK), :])
    both = jnp.dot(h_ref[row], jnp.concatenate(picked, axis=0), preferred_element_type=F32)
    top, bottom = both[:BLOCK], both[BLOCK:]
    total = top[:, :LANES] + ((top[:, LANES:] + bottom[:, :LANES]) + bottom[:, LANES:])
    here, by = scales(step, coef_ref)
    whole = pl.ds(pl.multiple_of(row * BLOCK, BLOCK), BLOCK)
    value = here * v_ref[whole, chunk * LANES : (chunk + 1) * LANES] + by * total
    return value if q is None else value - q


def unrolled(first, count, one):
    unroll = max(n for n in range(1, 13) if count % n == 0)

    def some(i, carry):
        for u in range(unroll):
            one(first + i * unroll + u)
        return carry

    lax.fori_loop(0, count // unroll, some, 0)


def at_rows(block, size=BLOCK):
    return pl.ds(pl.multiple_of(block * BLOCK, BLOCK), size)


class Shape:
    def __init__(self, block_rows, per_row, width, groups):
        self.rows = block_rows
        self.inner = block_rows - 2 * REACH
        self.core = block_rows - 4 * REACH
        self.chunks = width // LANES
        self.width = width
        self.vec_bits = (groups - 1).bit_length()
        self.bits_at = block_rows * per_row


def put_sends(shape, table_ref, source_ref, sends, lanes):
    half = source_ref.shape[0] // 2
    for b, ref, at in sends:
        other = 1 - table_ref[shape.bits_at + b]
        rows = pl.ds(pl.multiple_of(other * half, BLOCK), half)
        ref[at : at + half, lanes if ref.shape[1] == source_ref.shape[1] else slice(None)] = source_ref[rows, lanes]


def interior(step, chunk, shape, chain, common, parts, q):
    call = Call(chain).scalars(*common[:2]).reads(*common[2:], parts)
    if q is not None:
        call.reads(q)
    call.writes(shaped((shape.inner * BLOCK, LANES))).writes(shaped(parts.shape, BF16))

    def body(ins, outs, scratch):
        def one(row):
            old = None if q is None else ins[5][at_rows(row - REACH), :]
            value = new_rows(step, chunk, ins[:4], ins[4], row, old)
            outs[0][at_rows(row - REACH), :] = value
            put_parts(outs[1], pl.multiple_of((row + REACH) * BLOCK, BLOCK), value)

        unrolled(REACH, shape.inner, one)

    flops = 8 * shape.inner * BLOCK * LANES * common[2].shape[2]
    return call(body, "interior", cost(flops, 8 * common[2].size))


def core_rows(step, chunk, shape, chain, common, parts, q, mid, before):
    call = Call(chain).scalars(*common[:2]).reads(*common[2:], parts, q, mid).writes(shaped(parts.shape, BF16))
    core = shape.core * BLOCK
    before = before or [None, None]
    call.writes(shaped((core, shape.width)), before[0]).writes(shaped((core // 2, shape.width)), before[1])
    for _ in range(1, shape.vec_bits):
        call.writes(shaped((core // 2 + (shape.chunks - chunk) * SPARE, LANES)))
    lanes = slice(chunk * LANES, (chunk + 1) * LANES)

    def body(ins, outs, scratch):
        def one(row):
            value = new_rows(step - 1, chunk, ins[:4], ins[4], row, ins[5][at_rows(row - REACH), :])
            put_parts(outs[0], pl.multiple_of((row + REACH) * BLOCK, BLOCK), value)

        def two(row):
            old = ins[6][at_rows(row - REACH), :]
            outs[1][at_rows(row - 2 * REACH), lanes] = new_rows(step, chunk, ins[:4], outs[0], row, old)

        unrolled(REACH, shape.inner, one)
        unrolled(2 * REACH, shape.core, two)
        put_sends(shape, ins[0], outs[1], [(b, outs[2 + b], 0) for b in range(shape.vec_bits)], lanes)

    out = call(body, "core_rows", cost(0, 0))
    return (None, out[0]), out[1:3], out[3:]


def ring(step, chunk, shape, chain, common, parts, mid, before):
    call = Call(chain).scalars(*common[:2]).reads(*common[2:], parts, mid)
    before = before or [None] * (1 + shape.vec_bits)
    for n, one_before in enumerate(before):
        call.writes(shaped((2 * SIZE if n < 2 else SIZE, shape.width)), one_before)
    lanes = slice(chunk * LANES, (chunk + 1) * LANES)

    def body(ins, outs, scratch):
        for side, first in enumerate((REACH, shape.rows - 2 * REACH)):
            for r in range(REACH):
                row = first + r
                old = ins[5][at_rows(row - REACH), :]
                rows = pl.ds((side * REACH + r) * BLOCK, BLOCK)
                outs[0][rows, lanes] = new_rows(step, chunk, ins[:4], ins[4], row, old)
        put_sends(shape, ins[0], outs[0], [(b, outs[1 + b], 0) for b in range(shape.vec_bits)], lanes)

    return call(body, "ring", cost(0, 0))


def border(step, chunk, shape, chain, common, halo, q, parts, following, joined=None):
    call = Call(chain).scalars(*common[:2]).reads(*common[2:], *halo)
    if q is not None:
        call.reads(*q)
    call.writes(shaped(parts.shape, BF16), parts).writes(shaped(parts.shape, BF16), following)
    call.writes(shaped((SIZE, shape.width if joined else LANES)), joined[0] if joined else None)
    call.writes(shaped((SIZE + (joined[1] if joined else 0), LANES)))
    lanes = slice(chunk * LANES, (chunk + 1) * LANES) if joined else slice(None)

    def body(ins, outs, scratch):
        put_parts(outs[0], 0, ins[4][...])
        put_parts(outs[0], (shape.rows + REACH) * BLOCK, ins[5][...])
        for side, first in enumerate((0, shape.rows - REACH)):
            for r in range(REACH):
                rows = slice(r * BLOCK, (r + 1) * BLOCK)
                old = None if q is None else ins[6 + side][rows]
                value = new_rows(step, chunk, ins[:4], outs[0], first + r, old)
                outs[2 + side][rows, slice(None) if side else lanes] = value
                put_parts(outs[1], (first + r + REACH) * BLOCK, value)

    flops = 16 * SIZE * LANES * common[2].shape[2]
    _, following, low, high = call(body, "border", cost(flops, 4 * common[2].size))
    return low, high, following


def last_border(step, chunk, shape, chain, common, halo, q, parts, near, before, got, passed):
    call = Call(chain).scalars(*common[:2]).reads(*common[2:], *halo, *q)
    got_at = len(call.args)
    for arrays in got:
        call.reads(*arrays)
    call.writes(shaped(parts.shape, BF16), parts).writes(shaped(near.shape), near)
    before = before or [None] * shape.vec_bits
    for n, one_before in enumerate(before):
        call.writes(shaped((SIZE if n else 2 * SIZE, shape.width)), one_before)
    got_to = len(call.outs)
    for arrays in got:
        call.writes(shaped((shape.core * BLOCK // 2, shape.width)))
    call.passes(*passed)
    lanes = slice(chunk * LANES, (chunk + 1) * LANES)

    def body(ins, outs, scratch):
        put_parts(outs[0], 0, ins[4][:SIZE])
        put_parts(outs[0], (shape.rows + REACH) * BLOCK, ins[5][:, lanes])
        for side, first in enumerate((0, shape.rows - REACH)):
            for r in range(REACH):
                old = ins[6 + side][r * BLOCK : (r + 1) * BLOCK]
                rows = pl.ds((side * REACH + r) * BLOCK, BLOCK)
                outs[2][rows, lanes] = new_rows(step, chunk, ins[:4], outs[0], first + r, old)
        sends = [(0, outs[1], SIZE)] + [(b, outs[2 + b], 0) for b in range(1, shape.vec_bits)]
        put_sends(shape, ins[0], outs[2], sends, lanes)
        for n, arrays in enumerate(got):
            for c in range(len(arrays)):
                rows = slice(0, shape.core * BLOCK // 2)
                outs[got_to + n][:, c * LANES : (c + 1) * LANES] = ins[got_at + n * len(arrays) + c][rows]

    out = call(body, "last_border", cost(0, 0))
    joined, passed = out[got_to : got_to + len(got)], out[got_to + len(got) :][: len(passed)]
    return out[1], out[2 : 2 + shape.vec_bits], joined, passed


def gram_sums(shape, chain, table, kinds, own, got, before, piece, result=(), both=False, done=0):
    width = shape.width
    call = Call(chain).scalars(table).reads(*own)
    places = {}
    for d in kinds:
        if d:
            for n, (arrays, offset) in enumerate(got[d]):
                places[d, n] = (len(call.args), len(arrays), offset)
                call.reads(*arrays)
    before_at = len(call.args)
    if before is not None:
        call.reads(before)
    if piece:
        kept = shaped((len(kinds) * width // piece // 2, width // 2 if both else width, piece))
        for _ in range(4 if both else 2):
            call.writes(kept)
    else:
        call.writes(shaped((len(kinds), width, width)))
    result_at = len(call.args)
    for array, *_ in result:
        call.reads(array)
    if result:
        call.writes(shaped((shape.rows * BLOCK, width)), None, ANYWHERE)

    def products(left, right):
        total = jnp.dot(left[0], right[1], preferred_element_type=F32)
        total += jnp.dot(left[1], right[0], preferred_element_type=F32)
        return total + jnp.dot(left[0], right[0], preferred_element_type=F32)

    def body(ins, outs, scratch):
        table_ref = ins[0]
        copies = []
        for n, (_, start, rows, to) in enumerate(result):
            source = ins[result_at + n].at[pl.ds(start, rows)]
            copies.append(pltpu.make_async_copy(source, outs[-1].at[pl.ds(to, rows)], scratch[0].at[n]))
            copies[-1].start()
        summed = 0 if before is None else before.shape[0]
        totals = [ins[before_at][n] if n < summed else jnp.zeros((width, width), F32) for n in range(len(kinds))]
        for n in range(len(own)):
            ref = ins[1 + n]
            half = ref.shape[0] // 2
            for at in range(0, half, SIZE):
                sides = [ref[at : at + SIZE], ref[half + at : half + at + SIZE]]
                chosen = {}
                for m, d in enumerate(kinds):
                    if d == 0 and n < done:
                        continue
                    if d == 0:
                        for side in sides:
                            (left, _), (high, low) = two_parts(side.T), two_parts(side)
                            totals[m] += jnp.dot(left, low, preferred_element_type=F32)
                            totals[m] += 0.5 * jnp.dot(left, high, preferred_element_type=F32)
                        continue
                    b = d.bit_length() - 1
                    if b not in chosen:
                        first = table_ref[shape.bits_at + b] == 0
                        chosen[b] = two_parts(jnp.where(first, sides[0], sides[1]).T)
                    where, count, offset = places[d, n]
                    other = [ins[where + c][offset + at : offset + at + SIZE] for c in range(count)]
                    other = other[0] if count == 1 else jnp.concatenate(other, axis=1)
                    totals[m] += products(chosen[b], two_parts(other))
        bit_at = shape.bits_at + shape.vec_bits
        for m in range(0, len(kinds) if both else 0, 2):
            first, second = table_ref[bit_at] == 0, table_ref[bit_at + 1] == 0
            half = width // 2
            for n in range(2):
                one, two = totals[m + n][:half, :piece], totals[m + n][:half, piece:]
                outs[0][m + n] = jnp.where(first, one, two)
                outs[1][m + n] = jnp.where(first, two, one)
                columns = slice(n * piece, (n + 1) * piece)
                one, two = totals[m][half:, columns], totals[m + 1][half:, columns]
                outs[2][m + n] = jnp.where(second, one, two)
                outs[3][m + n] = jnp.where(second, two, one)
        for m, total in enumerate([] if both else totals):
            if not piece:
                outs[0][m] = total
                continue
            pairs = width // piece // 2
            even = table_ref[bit_at] == 0
            for t in range(pairs):
                one = total[:, 2 * t * piece : (2 * t + 1) * piece]
                two = total[:, (2 * t + 1) * piece : (2 * t + 2) * piece]
                outs[0][m * pairs + t] = jnp.where(even, one, two)
                outs[1][m * pairs + t] = jnp.where(even, two, one)
        for copy in copies:
            copy.wait()

    rows = sum(a.shape[0] for a in own)
    flops = 3 * rows * width * width * (len(kinds) + 1)
    scratch = [pltpu.SemaphoreType.DMA((len(result),))] if result else []
    out = call(body, "gram_sums", cost(flops, 8 * rows * width), scratch)
    return out if piece or result else out[0]


def fold(shape, chain, table, level, pairs, passed=()):
    call = Call(chain).scalars(table)
    count = sum(arrays[0].shape[0] for arrays in pairs)
    for arrays in pairs:
        call.reads(*arrays)
    rows = sum(a.shape[1] for a in pairs[0][::2])
    half = shaped((count // 2, rows, pairs[0][0].shape[2]))
    call.writes(half).writes(half).passes(*passed)

    def body(ins, outs, scratch):
        bit_at = shape.bits_at + shape.vec_bits
        even = ins[0][bit_at + level] == 0
        sums, at = [], 1
        for arrays in pairs:
            for m in range(arrays[0].shape[0]):
                parts = [ins[at + n][m] + ins[at + n + 1][m] for n in range(0, len(arrays), 2)]
                sums.append(jnp.concatenate(parts, axis=0) if len(parts) > 1 else parts[0])
            at += len(arrays)
        for n in range(count // 2):
            outs[0][n] = jnp.where(even, sums[2 * n], sums[2 * n + 1])
            outs[1][n] = jnp.where(even, sums[2 * n + 1], sums[2 * n])

    return call(body, "fold", cost(0, 8 * count * pairs[0][0][0].size))


def fold_two(shape, chain, table, upper, lower):
    half = shaped((upper[0].shape[0] // 2, *upper[0].shape[1:]))
    call = Call(chain).scalars(table).reads(*upper, *lower)
    for _ in range(4):
        call.writes(half)

    def body(ins, outs, scratch):
        bit_at = shape.bits_at + shape.vec_bits
        for n, level in enumerate((1, 0)):
            even = ins[0][bit_at + level] == 0
            keep, got = ins[1 + 2 * n], ins[2 + 2 * n]
            for m in range(half.shape[0]):
                one, two = keep[2 * m] + got[2 * m], keep[2 * m + 1] + got[2 * m + 1]
                outs[2 * n][m] = jnp.where(even, one, two)
                outs[2 * n + 1][m] = jnp.where(even, two, one)

    return call(body, "fold_two", cost(0, 0))


def add_blocks(chain, table, keep, got, tiles):
    rows, columns = keep.shape[1:]
    size = rows // tiles
    call = Call(chain).scalars(table).reads(keep, got).writes(shaped((rows, columns)))
    for _ in range(tiles):
        call.writes(shaped((size, columns)))

    def body(ins, outs, scratch):
        outs[0][...] = ins[1][0] + ins[2][0]
        for n in range(tiles):
            number = lax.rem(ins[0][ins[0].shape[0] - 1] + n, tiles)
            outs[1 + n][...] = outs[0][pl.ds(pl.multiple_of(number * size, size), size), :]

    return call(body, "add_blocks", cost(0, 0))


def assemble(chain, table, share, turned, scale):
    tiles = len(turned)
    rows, columns = share.shape
    size = rows // tiles
    call = Call(chain).scalars(table).reads(share, *turned).writes(shaped((rows, columns)))

    def body(ins, outs, scratch):
        number = ins[0][ins[0].shape[0] - 1]
        flipped = [ins[2 + n][...].T for n in range(tiles)]
        for t in range(tiles):
            which = lax.rem(number - t + tiles, tiles)
            tile = flipped[0]
            for n in range(1, tiles):
                tile = jnp.where(which == n, flipped[n], tile)
            at = slice(t * size, (t + 1) * size)
            outs[0][at] = (ins[1][at] + tile) * scale

    return call(body, "assemble", cost(0, 0))[0]


def on_device(hamiltonian, columns, vectors, coefficients):
    block_rows, per_row = columns.shape
    peers = lax.axis_size("rows")
    groups = lax.axis_size("vecs")
    total_blocks = block_rows * peers
    width = vectors.shape[1]
    shape = Shape(block_rows, per_row, width, groups)
    chunks = shape.chunks
    rows_at, vecs_at = lax.axis_index("rows"), lax.axis_index("vecs")
    up = [(i, (i + 1) % peers) for i in range(peers)]
    down = [(j, i) for i, j in up]

    def exchange(first, last):
        return lax.ppermute(last, "rows", up), lax.ppermute(first, "rows", down)

    chain = Chain()
    halo = [exchange(vectors[:SIZE, :LANES], vectors[-SIZE:, :LANES])]

    local = jnp.arange(block_rows, dtype=jnp.int32)
    offsets = (columns - (rows_at * block_rows + local)[:, None] + REACH) % total_blocks
    slots = (offsets + (local % REACH)[:, None]).reshape(-1)
    per_group = peers // groups
    piece = width // per_group
    wanted = rows_at ^ (vecs_at * per_group)
    levels = (peers - 1).bit_length()
    bits = [(vecs_at >> b) & 1 for b in range(shape.vec_bits)] + [(wanted >> b) & 1 for b in range(levels)]
    bits.append(rows_at % per_group)
    table = jnp.concatenate([slots, jnp.stack(bits).astype(jnp.int32)])

    parts_h, vectors, parts, sends = prepare(shape, chain, table, hamiltonian, vectors)
    halo += [exchange(*strips) for strips in sends]
    common = (table, coefficients, parts_h, vectors)

    terms, older, inner, core_sends = ([None] * chunks for _ in range(4))
    core = rims = ends = None
    wide, before = None, [None] * chunks

    def swapped(x, distance):
        return lax.ppermute(x, "vecs", [(i, i ^ distance) for i in range(groups)])

    def received(sends):
        return {d: swapped(sends[d.bit_length() - 2], d) for d in range(2, groups, 2)}

    def forwarded(got):
        out = {}
        for d, rows in got.items():
            out[d], out[d + 1] = rows, swapped(rows, 1)
        return out

    def inside(step, c):
        nonlocal core, rims
        q = older[c] and older[c][1]
        if step < ORDER - 1:
            inner[c] = interior(step, c, shape, chain, common, parts[c], q)
        elif step == ORDER - 1:
            inner[c], core, core_sends[c] = core_rows(ORDER, c, shape, chain, common, parts[c], q, terms[c][1], core)
        else:
            rims = ring(step, c, shape, chain, common, parts[c], q, rims)

    for step in range(1, ORDER):
        for c in range(chunks):
            inside(step, c)
            q = older[c] and (older[c][0], older[c][2])
            late = step == ORDER - 1
            spare = (chunks - 1 - c) * EARLY
            low, high, following = border(
                step, c, shape, chain, common, halo[c], q, parts[c], inner[c][1], (wide, spare) if late else ()
            )
            if late:
                wide, before[c] = low, lax.ppermute(high, "rows", up)
            else:
                halo[c] = exchange(low, high)
            older[c], terms[c], parts[c] = terms[c], (low, inner[c][0], high), following
    after = lax.ppermute(wide, "rows", down)
    got_core = [received(sends) for sends in core_sends]
    for c in range(chunks):
        inside(ORDER, c)
    got_rims = received(rims[2:])
    diagonal = gram_sums(shape, chain, table, (0,), [core[0], rims[0]], {}, None, 0)
    near = rims[1]
    for c in range(chunks):
        q = (older[c][0], older[c][2])
        got = [[rows[d] for rows in got_core] for d in range(2, groups, 2)] if c == 0 else []
        passed = [core[1], *got_rims.values()] if c == chunks - 1 else []
        near, ends, joined, passed = last_border(
            ORDER, c, shape, chain, common, (before[c], after), q, parts[c], near, ends, got, passed
        )
        if c == 0:
            all_core = {2 * n + 2: rows for n, rows in enumerate(joined)}
    near_core = passed[0]
    got_core = forwarded(all_core)
    got_rims = forwarded(dict(zip(got_rims, passed[1:])))
    got_ends = received(ends[1:])

    kinds, far = tuple(range(min(2, groups))), tuple(range(2, groups))
    swaps = [[(i, i ^ (1 << level)) for i in range(peers)] for level in range(levels)]
    near_core, near = swapped(near_core, 1), swapped(near, 1)
    last = block_rows * BLOCK - SIZE
    result = [(core[0], 0, core[0].shape[0], 2 * SIZE), (rims[0], 0, SIZE, SIZE), (rims[0], SIZE, SIZE, last - SIZE)]
    result += [(ends[0], 0, SIZE, 0), (ends[0], SIZE, SIZE, last)]
    arrived = {1: [([near_core], 0), ([near], 0), ([near], SIZE)]}
    whole = [] if far else result
    keep, send, *rest = gram_sums(shape, chain, table, kinds, [core[0], rims[0], ends[0]], arrived, diagonal, piece, whole, done=2)
    shares = [(keep, lax.ppermute(send, "rows", swaps[0]))]
    if far:
        arrived = {d: [([got_core[d]], 0), ([got_rims[d]], 0)] for d in far}
        sums, *rest = gram_sums(shape, chain, table, far, [core[0], rims[0]], arrived, None, 0, result)
        keep, send, *rows = fold(shape, chain, table, 1, shares, got_ends.values())
        shares = [(keep, lax.ppermute(send, "rows", swaps[1]))]
        got_ends = forwarded(dict(zip(got_ends, rows)))
        arrived = {d: [([got_ends[d]], 0)] for d in far}
        both = per_group == 2 and levels > 2
        made = gram_sums(shape, chain, table, far, [ends[0]], arrived, sums, piece, (), both)
        if both:
            upper = (made[0], lax.ppermute(made[1], "rows", swaps[0]))
            lower = (made[2], lax.ppermute(made[3], "rows", swaps[1]))
            made = fold_two(shape, chain, table, upper, lower)
            shares.append(
                (made[0], lax.ppermute(made[1], "rows", swaps[1]), made[2], lax.ppermute(made[3], "rows", swaps[0]))
            )
        else:
            shares.append((made[0], lax.ppermute(made[1], "rows", swaps[0])))
    filtered = rest[0]

    for level in range(1, levels - 1):
        ahead = [pair for n, pair in enumerate(shares) if level == 1 and len(shares) > 1 and (n == 0 or len(pair) > 2)]
        if len(ahead) == len(shares):
            continue
        joined = [shares] if shares[0][0].shape[0] == 1 and not ahead else [[pair] for pair in shares[len(ahead) :]]
        folded = [fold(shape, chain, table, level, pairs) for pairs in joined]
        shares = ahead + [(keep, lax.ppermute(send, "rows", swaps[level])) for keep, send in folded]

    keep, send = fold(shape, chain, table, levels - 1, shares)
    share, *tiles = add_blocks(chain, table, keep, lax.ppermute(send, "rows", swaps[-1]), per_group)
    turned = []
    for n in range(per_group):
        pairs = []
        for i in range(peers):
            for g in range(groups):
                to = (g * per_group + (i + n) % per_group) * groups + i // per_group
                pairs.append((i * groups + g, to))
        turned.append(lax.ppermute(tiles[n], ("rows", "vecs"), pairs))
    gram = assemble(chain, table, share, turned, 1.0 / (total_blocks * BLOCK))
    return filtered, gram


def solution(mesh):
    return jax.shard_map(
        on_device,
        mesh=mesh,
        in_specs=(P("rows", None, None, None), P("rows", None), P("rows", "vecs"), P()),
        out_specs=(P("rows", "vecs"), P("vecs", "rows")),
        check_vma=False,
    )
```

```python
import functools

import jax
import jax.numpy as jnp
from jax import lax
from jax.experimental import pallas as pl
from jax.experimental.pallas import tpu as pltpu
from jax.sharding import PartitionSpec as P

BLOCK = 128
REACH = 4
ORDER = 6
LANES = 128
SIZE = REACH * BLOCK
SPARE = 32
EARLY = 32
F32 = jnp.float32
BF16 = jnp.bfloat16
WHOLE = pl.BlockSpec(memory_space=pltpu.VMEM)
ANYWHERE = pl.BlockSpec(memory_space=pl.ANY)
SCALARS = pl.BlockSpec(memory_space=pltpu.SMEM)


def shaped(shape, dtype=F32):
    return jax.ShapeDtypeStruct(shape, dtype)


def cost(flops, moved):
    return pl.CostEstimate(flops=flops, bytes_accessed=moved, transcendentals=0)


class Call:
    def __init__(self, chain):
        self.chain = chain
        self.args, self.specs, self.outs, self.out_specs, self.aliases = [], [], [], [], {}

    def anywhere(self, *arrays):
        self.args += arrays
        self.specs += [ANYWHERE] * len(arrays)
        return self

    def scalars(self, *arrays):
        self.args += arrays
        self.specs += [SCALARS] * len(arrays)
        return self

    def reads(self, *arrays):
        self.args += arrays
        self.specs += [WHOLE] * len(arrays)
        return self

    def writes(self, shape, before=None, spec=WHOLE):
        if before is not None:
            self.aliases[len(self.args)] = len(self.outs)
            self.args.append(before)
            self.specs.append(spec)
        self.outs.append(shape)
        self.out_specs.append(spec)
        return self

    def passes(self, *arrays):
        for array in arrays:
            self.writes(shaped(array.shape, array.dtype), array, ANYWHERE)
        return self

    def __call__(self, body, name, estimate, scratch=(), mib=16):
        if self.chain.token is not None:
            self.anywhere(self.chain.token)
        self.writes(shaped((8, LANES)))
        count = len(self.args)

        def kernel(*refs):
            ins, outs = refs[:count], refs[count : count + len(self.outs)]
            outs[-1][...] = jnp.zeros((8, LANES), F32)
            body(ins, outs[:-1], refs[count + len(self.outs) :])

        *results, self.chain.token = pl.pallas_call(
            kernel,
            in_specs=self.specs,
            out_specs=self.out_specs,
            out_shape=self.outs,
            scratch_shapes=scratch,
            input_output_aliases=self.aliases,
            compiler_params=pltpu.CompilerParams(vmem_limit_bytes=mib * 1024 * 1024),
            cost_estimate=estimate,
            name=name,
        )(*self.args)
        return results


class Chain:
    token = None


def two_parts(x):
    high = x.astype(BF16)
    low = (x - high.astype(F32)).astype(BF16)
    return high, low


def put_parts(ref, start, value):
    high, low = two_parts(value)
    ref[pl.ds(start, value.shape[0]), :LANES] = high
    ref[pl.ds(start, value.shape[0]), LANES:] = low


def prepare(shape, chain, table, hamiltonian, vectors):
    rows, per_row = hamiltonian.shape[:2]
    strips, slots = rows // REACH, 4
    far = [pltpu.with_memory_space_constraint(x, pltpu.HBM) for x in (hamiltonian, vectors)]
    call = Call(chain).scalars(table).anywhere(*far)
    call.writes(shaped((rows, 2 * BLOCK, per_row * BLOCK), BF16)).writes(shaped(vectors.shape))
    for _ in range(shape.chunks):
        call.writes(shaped((vectors.shape[0] + 2 * SIZE, 2 * LANES), BF16))
    for _ in range(2 * (shape.chunks - 1)):
        call.writes(shaped((SIZE, LANES)))

    def body(ins, outs, scratch):
        h_ref, v_ref = ins[1], ins[2]
        parts_h, copy_v = outs[:2]
        held, sems, v_sem = scratch

        def fetch(g):
            slot = lax.rem(g, slots)
            return pltpu.make_async_copy(h_ref.at[pl.ds(g * REACH, REACH)], held.at[slot], sems.at[slot])

        def split(g, carry):
            slot = lax.rem(g, slots)
            fetch(g).wait()
            for r in range(REACH):
                for k in range(per_row):
                    high, low = two_parts(held[slot, r, k])
                    parts_h[g * REACH + r, :BLOCK, k * BLOCK : (k + 1) * BLOCK] = high
                    parts_h[g * REACH + r, BLOCK:, k * BLOCK : (k + 1) * BLOCK] = low

            @pl.when(g + slots < strips)
            def _():
                fetch(g + slots).start()

            return carry

        def split_v(g, carry):
            at = pl.multiple_of(g * SIZE, SIZE)
            for c in range(shape.chunks):
                put_parts(outs[2 + c], pl.multiple_of(at + SIZE, SIZE), copy_v[pl.ds(at, SIZE), c * LANES : (c + 1) * LANES])
            return carry

        copy = pltpu.make_async_copy(v_ref, copy_v, v_sem)
        for g in range(min(slots, strips)):
            fetch(jnp.int32(g)).start()
        copy.start()
        lax.fori_loop(0, strips // 2, split, 0)
        copy.wait()
        lax.fori_loop(0, strips, split_v, 0)
        for c in range(1, shape.chunks):
            lanes = slice(c * LANES, (c + 1) * LANES)
            outs[shape.chunks + 2 * c][...] = copy_v[:SIZE, lanes]
            outs[shape.chunks + 2 * c + 1][...] = copy_v[-SIZE:, lanes]
        lax.fori_loop(strips // 2, strips, split, 0)

    scratch = [pltpu.VMEM((slots, REACH, *hamiltonian.shape[1:]), F32), pltpu.SemaphoreType.DMA((slots,)), pltpu.SemaphoreType.DMA]
    out = call(body, "prepare", cost(0, 8 * hamiltonian.size), scratch)
    sends = out[2 + shape.chunks :]
    return out[0], out[1], out[2 : 2 + shape.chunks], [sends[2 * c : 2 * c + 2] for c in range(shape.chunks - 1)]


def scales(step, coef_ref):
    here, by = coef_ref[ORDER - step], 2.0
    if step == 1:
        by = 2.0 * coef_ref[ORDER]
    elif step == 2:
        here = here - coef_ref[ORDER]
    elif step == ORDER:
        by = 1.0
    return here, by


def new_rows(step, chunk, common, parts_ref, row, q):
    table_ref, coef_ref, h_ref, v_ref = common
    per_row = h_ref.shape[2] // BLOCK
    base = (row // REACH) * REACH
    picked = []
    for k in range(per_row):
        start = pl.multiple_of((table_ref[row * per_row + k] + base) * BLOCK, BLOCK)
        picked.append(parts_ref[pl.ds(start, BLOCK), :])
    both = jnp.dot(h_ref[row], jnp.concatenate(picked, axis=0), preferred_element_type=F32)
    top, bottom = both[:BLOCK], both[BLOCK:]
    total = top[:, :LANES] + ((top[:, LANES:] + bottom[:, :LANES]) + bottom[:, LANES:])
    here, by = scales(step, coef_ref)
    whole = pl.ds(pl.multiple_of(row * BLOCK, BLOCK), BLOCK)
    value = here * v_ref[whole, chunk * LANES : (chunk + 1) * LANES] + by * total
    return value if q is None else value - q


def unrolled(first, count, one):
    unroll = max(n for n in range(1, 13) if count % n == 0)

    def some(i, carry):
        for u in range(unroll):
            one(first + i * unroll + u)
        return carry

    lax.fori_loop(0, count // unroll, some, 0)


def at_rows(block, size=BLOCK):
    return pl.ds(pl.multiple_of(block * BLOCK, BLOCK), size)


class Shape:
    def __init__(self, block_rows, per_row, width, groups):
        self.rows = block_rows
        self.inner = block_rows - 2 * REACH
        self.core = block_rows - 4 * REACH
        self.chunks = width // LANES
        self.width = width
        self.vec_bits = (groups - 1).bit_length()
        self.bits_at = block_rows * per_row


def put_sends(shape, table_ref, source_ref, sends, lanes):
    half = source_ref.shape[0] // 2
    for b, ref, at in sends:
        other = 1 - table_ref[shape.bits_at + b]
        rows = pl.ds(pl.multiple_of(other * half, BLOCK), half)
        ref[at : at + half, lanes if ref.shape[1] == source_ref.shape[1] else slice(None)] = source_ref[rows, lanes]


def interior(step, chunk, shape, chain, common, parts, q):
    call = Call(chain).scalars(*common[:2]).reads(*common[2:], parts)
    if q is not None:
        call.reads(q)
    call.writes(shaped((shape.inner * BLOCK, LANES))).writes(shaped(parts.shape, BF16))

    def body(ins, outs, scratch):
        def one(row):
            old = None if q is None else ins[5][at_rows(row - REACH), :]
            value = new_rows(step, chunk, ins[:4], ins[4], row, old)
            outs[0][at_rows(row - REACH), :] = value
            put_parts(outs[1], pl.multiple_of((row + REACH) * BLOCK, BLOCK), value)

        unrolled(REACH, shape.inner, one)

    flops = 8 * shape.inner * BLOCK * LANES * common[2].shape[2]
    return call(body, "interior", cost(flops, 8 * common[2].size))


def core_rows(step, chunk, shape, chain, common, parts, q, mid, before):
    call = Call(chain).scalars(*common[:2]).reads(*common[2:], parts, q, mid).writes(shaped(parts.shape, BF16))
    core = shape.core * BLOCK
    before = before or [None, None]
    call.writes(shaped((core, shape.width)), before[0]).writes(shaped((core // 2 + SIZE, shape.width)), before[1])
    for _ in range(1, shape.vec_bits):
        call.writes(shaped((core // 2 + (shape.chunks - chunk) * SPARE, LANES)))
    lanes = slice(chunk * LANES, (chunk + 1) * LANES)

    def body(ins, outs, scratch):
        def one(row):
            value = new_rows(step - 1, chunk, ins[:4], ins[4], row, ins[5][at_rows(row - REACH), :])
            put_parts(outs[0], pl.multiple_of((row + REACH) * BLOCK, BLOCK), value)

        def two(row):
            old = ins[6][at_rows(row - REACH), :]
            outs[1][at_rows(row - 2 * REACH), lanes] = new_rows(step, chunk, ins[:4], outs[0], row, old)

        unrolled(REACH, shape.inner, one)
        unrolled(2 * REACH, shape.core, two)
        put_sends(shape, ins[0], outs[1], [(b, outs[2 + b], 0) for b in range(shape.vec_bits)], lanes)

    out = call(body, "core_rows", cost(0, 0))
    return (None, out[0]), out[1:3], out[3:]


def ring(step, chunk, shape, chain, common, parts, mid, near, before):
    call = Call(chain).scalars(*common[:2]).reads(*common[2:], parts, mid)
    call.writes(shaped(near.shape), near)
    before = before or [None] * shape.vec_bits
    for n, one_before in enumerate(before):
        call.writes(shaped((SIZE if n else 2 * SIZE, shape.width)), one_before)
    lanes = slice(chunk * LANES, (chunk + 1) * LANES)

    def body(ins, outs, scratch):
        for side, first in enumerate((REACH, shape.rows - 2 * REACH)):
            for r in range(REACH):
                row = first + r
                old = ins[5][at_rows(row - REACH), :]
                rows = pl.ds((side * REACH + r) * BLOCK, BLOCK)
                outs[1][rows, lanes] = new_rows(step, chunk, ins[:4], ins[4], row, old)
        sends = [(0, outs[0], near.shape[0] - SIZE)] + [(b, outs[1 + b], 0) for b in range(1, shape.vec_bits)]
        put_sends(shape, ins[0], outs[1], sends, lanes)

    near, *rims = call(body, "ring", cost(0, 0))
    return near, rims


def border(step, chunk, shape, chain, common, halo, q, parts, following, joined=None):
    call = Call(chain).scalars(*common[:2]).reads(*common[2:], *halo)
    if q is not None:
        call.reads(*q)
    call.writes(shaped(parts.shape, BF16), parts).writes(shaped(parts.shape, BF16), following)
    call.writes(shaped((SIZE, shape.width if joined else LANES)), joined[0] if joined else None)
    call.writes(shaped((SIZE + (joined[1] if joined else 0), LANES)))
    lanes = slice(chunk * LANES, (chunk + 1) * LANES) if joined else slice(None)

    def body(ins, outs, scratch):
        put_parts(outs[0], 0, ins[4][...])
        put_parts(outs[0], (shape.rows + REACH) * BLOCK, ins[5][...])
        for side, first in enumerate((0, shape.rows - REACH)):
            for r in range(REACH):
                rows = slice(r * BLOCK, (r + 1) * BLOCK)
                old = None if q is None else ins[6 + side][rows]
                value = new_rows(step, chunk, ins[:4], outs[0], first + r, old)
                outs[2 + side][rows, slice(None) if side else lanes] = value
                put_parts(outs[1], (first + r + REACH) * BLOCK, value)

    flops = 16 * SIZE * LANES * common[2].shape[2]
    _, following, low, high = call(body, "border", cost(flops, 4 * common[2].size))
    return low, high, following


def last_border(step, chunk, shape, chain, common, halo, q, parts, before, got):
    call = Call(chain).scalars(*common[:2]).reads(*common[2:], *halo, *q)
    got_at = len(call.args)
    for arrays in got:
        call.reads(*arrays)
    call.writes(shaped(parts.shape, BF16), parts)
    before = before or [None] * (1 + shape.vec_bits)
    for n, one_before in enumerate(before):
        call.writes(shaped((SIZE if n else 2 * SIZE, shape.width)), one_before)
    got_to = len(call.outs)
    for arrays in got:
        call.writes(shaped((shape.core * BLOCK // 2, shape.width)))
    lanes = slice(chunk * LANES, (chunk + 1) * LANES)

    def body(ins, outs, scratch):
        put_parts(outs[0], 0, ins[4][:SIZE])
        put_parts(outs[0], (shape.rows + REACH) * BLOCK, ins[5][:, lanes])
        for side, first in enumerate((0, shape.rows - REACH)):
            for r in range(REACH):
                old = ins[6 + side][r * BLOCK : (r + 1) * BLOCK]
                rows = pl.ds((side * REACH + r) * BLOCK, BLOCK)
                outs[1][rows, lanes] = new_rows(step, chunk, ins[:4], outs[0], first + r, old)
        put_sends(shape, ins[0], outs[1], [(b, outs[2 + b], 0) for b in range(shape.vec_bits)], lanes)
        for n, arrays in enumerate(got):
            for c in range(len(arrays)):
                rows = slice(0, shape.core * BLOCK // 2)
                outs[got_to + n][:, c * LANES : (c + 1) * LANES] = ins[got_at + n * len(arrays) + c][rows]

    out = call(body, "last_border", cost(0, 0))
    return out[1 : 2 + shape.vec_bits], out[got_to:]


def gram_sums(shape, chain, table, kinds, own, got, before, piece, result=(), both=False, done=0):
    width = shape.width
    call = Call(chain).scalars(table).reads(*own)
    places = {}
    for d in kinds:
        if d:
            for n, (arrays, offset) in enumerate(got[d]):
                places[d, n] = (len(call.args), len(arrays), offset)
                call.reads(*arrays)
    before_at = len(call.args)
    if before is not None:
        call.reads(before)
    if piece:
        kept = shaped((len(kinds) * width // piece // 2, width // 2 if both else width, piece))
        for _ in range(4 if both else 2):
            call.writes(kept)
    else:
        call.writes(shaped((len(kinds), width, width)))
    result_at = len(call.args)
    for array, *_ in result:
        call.reads(array)
    if result:
        call.writes(shaped((shape.rows * BLOCK, width)), None, ANYWHERE)

    def products(left, right):
        total = jnp.dot(left[0], right[1], preferred_element_type=F32)
        total += jnp.dot(left[1], right[0], preferred_element_type=F32)
        return total + jnp.dot(left[0], right[0], preferred_element_type=F32)

    def body(ins, outs, scratch):
        table_ref = ins[0]
        copies = []
        for n, (_, start, rows, to) in enumerate(result):
            source = ins[result_at + n].at[pl.ds(start, rows)]
            copies.append(pltpu.make_async_copy(source, outs[-1].at[pl.ds(to, rows)], scratch[0].at[n]))
            copies[-1].start()
        summed = 0 if before is None else before.shape[0]
        totals = [ins[before_at][n] if n < summed else jnp.zeros((width, width), F32) for n in range(len(kinds))]
        for n in range(len(own)):
            ref = ins[1 + n]
            half = ref.shape[0] // 2
            for at in range(0, half, SIZE):
                sides = [ref[at : at + SIZE], ref[half + at : half + at + SIZE]]
                chosen = {}
                for m, d in enumerate(kinds):
                    if d == 0 and n < done:
                        continue
                    if d == 0:
                        for side in sides:
                            (left, _), (high, low) = two_parts(side.T), two_parts(side)
                            totals[m] += jnp.dot(left, low, preferred_element_type=F32)
                            totals[m] += 0.5 * jnp.dot(left, high, preferred_element_type=F32)
                        continue
                    b = d.bit_length() - 1
                    if b not in chosen:
                        first = table_ref[shape.bits_at + b] == 0
                        chosen[b] = two_parts(jnp.where(first, sides[0], sides[1]).T)
                    where, count, offset = places[d, n]
                    other = [ins[where + c][offset + at : offset + at + SIZE] for c in range(count)]
                    other = other[0] if count == 1 else jnp.concatenate(other, axis=1)
                    totals[m] += products(chosen[b], two_parts(other))
        bit_at = shape.bits_at + shape.vec_bits
        for m in range(0, len(kinds) if both else 0, 2):
            first, second = table_ref[bit_at] == 0, table_ref[bit_at + 1] == 0
            half = width // 2
            for n in range(2):
                one, two = totals[m + n][:half, :piece], totals[m + n][:half, piece:]
                outs[0][m + n] = jnp.where(first, one, two)
                outs[1][m + n] = jnp.where(first, two, one)
                columns = slice(n * piece, (n + 1) * piece)
                one, two = totals[m][half:, columns], totals[m + 1][half:, columns]
                outs[2][m + n] = jnp.where(second, one, two)
                outs[3][m + n] = jnp.where(second, two, one)
        for m, total in enumerate([] if both else totals):
            if not piece:
                outs[0][m] = total
                continue
            pairs = width // piece // 2
            even = table_ref[bit_at] == 0
            for t in range(pairs):
                one = total[:, 2 * t * piece : (2 * t + 1) * piece]
                two = total[:, (2 * t + 1) * piece : (2 * t + 2) * piece]
                outs[0][m * pairs + t] = jnp.where(even, one, two)
                outs[1][m * pairs + t] = jnp.where(even, two, one)
        for copy in copies:
            copy.wait()

    rows = sum(a.shape[0] for a in own)
    flops = 3 * rows * width * width * (len(kinds) + 1)
    scratch = [pltpu.SemaphoreType.DMA((len(result),))] if result else []
    out = call(body, "gram_sums", cost(flops, 8 * rows * width), scratch)
    return out if piece or result else out[0]


def fold(shape, chain, table, level, pairs, passed=()):
    call = Call(chain).scalars(table)
    count = sum(arrays[0].shape[0] for arrays in pairs)
    for arrays in pairs:
        call.reads(*arrays)
    rows = sum(a.shape[1] for a in pairs[0][::2])
    half = shaped((count // 2, rows, pairs[0][0].shape[2]))
    call.writes(half).writes(half).passes(*passed)

    def body(ins, outs, scratch):
        bit_at = shape.bits_at + shape.vec_bits
        even = ins[0][bit_at + level] == 0
        sums, at = [], 1
        for arrays in pairs:
            for m in range(arrays[0].shape[0]):
                parts = [ins[at + n][m] + ins[at + n + 1][m] for n in range(0, len(arrays), 2)]
                sums.append(jnp.concatenate(parts, axis=0) if len(parts) > 1 else parts[0])
            at += len(arrays)
        for n in range(count // 2):
            outs[0][n] = jnp.where(even, sums[2 * n], sums[2 * n + 1])
            outs[1][n] = jnp.where(even, sums[2 * n + 1], sums[2 * n])

    return call(body, "fold", cost(0, 8 * count * pairs[0][0][0].size))


def take_in(chain, arrays):
    return Call(chain).passes(*arrays)(lambda ins, outs, scratch: None, "take_in", cost(0, 0))


def fold_two(shape, chain, table, upper, lower):
    half = shaped((upper[0].shape[0] // 2, *upper[0].shape[1:]))
    call = Call(chain).scalars(table).reads(*upper, *lower)
    for _ in range(4):
        call.writes(half)

    def body(ins, outs, scratch):
        bit_at = shape.bits_at + shape.vec_bits
        for n, level in enumerate((1, 0)):
            even = ins[0][bit_at + level] == 0
            keep, got = ins[1 + 2 * n], ins[2 + 2 * n]
            for m in range(half.shape[0]):
                one, two = keep[2 * m] + got[2 * m], keep[2 * m + 1] + got[2 * m + 1]
                outs[2 * n][m] = jnp.where(even, one, two)
                outs[2 * n + 1][m] = jnp.where(even, two, one)

    return call(body, "fold_two", cost(0, 0))


def add_blocks(chain, table, keep, got, tiles):
    rows, columns = keep.shape[1:]
    size = rows // tiles
    call = Call(chain).scalars(table).reads(keep, got).writes(shaped((rows, columns)))
    for _ in range(tiles):
        call.writes(shaped((size, columns)))

    def body(ins, outs, scratch):
        outs[0][...] = ins[1][0] + ins[2][0]
        for n in range(tiles):
            number = lax.rem(ins[0][ins[0].shape[0] - 1] + n, tiles)
            outs[1 + n][...] = outs[0][pl.ds(pl.multiple_of(number * size, size), size), :]

    return call(body, "add_blocks", cost(0, 0))


def assemble(chain, table, share, turned, scale):
    tiles = len(turned)
    rows, columns = share.shape
    size = rows // tiles
    call = Call(chain).scalars(table).reads(share, *turned).writes(shaped((rows, columns)))

    def body(ins, outs, scratch):
        number = ins[0][ins[0].shape[0] - 1]
        flipped = [ins[2 + n][...].T for n in range(tiles)]
        for t in range(tiles):
            which = lax.rem(number - t + tiles, tiles)
            tile = flipped[0]
            for n in range(1, tiles):
                tile = jnp.where(which == n, flipped[n], tile)
            at = slice(t * size, (t + 1) * size)
            outs[0][at] = (ins[1][at] + tile) * scale

    return call(body, "assemble", cost(0, 0))[0]


def on_device(hamiltonian, columns, vectors, coefficients):
    block_rows, per_row = columns.shape
    peers = lax.axis_size("rows")
    groups = lax.axis_size("vecs")
    total_blocks = block_rows * peers
    width = vectors.shape[1]
    shape = Shape(block_rows, per_row, width, groups)
    chunks = shape.chunks
    rows_at, vecs_at = lax.axis_index("rows"), lax.axis_index("vecs")
    up = [(i, (i + 1) % peers) for i in range(peers)]
    down = [(j, i) for i, j in up]

    def exchange(first, last):
        return lax.ppermute(last, "rows", up), lax.ppermute(first, "rows", down)

    chain = Chain()
    halo = [exchange(vectors[:SIZE, :LANES], vectors[-SIZE:, :LANES])]

    local = jnp.arange(block_rows, dtype=jnp.int32)
    offsets = (columns - (rows_at * block_rows + local)[:, None] + REACH) % total_blocks
    slots = (offsets + (local % REACH)[:, None]).reshape(-1)
    per_group = peers // groups
    piece = width // per_group
    wanted = rows_at ^ (vecs_at * per_group)
    levels = (peers - 1).bit_length()
    bits = [(vecs_at >> b) & 1 for b in range(shape.vec_bits)] + [(wanted >> b) & 1 for b in range(levels)]
    bits.append(rows_at % per_group)
    table = jnp.concatenate([slots, jnp.stack(bits).astype(jnp.int32)])

    parts_h, vectors, parts, sends = prepare(shape, chain, table, hamiltonian, vectors)
    halo += [exchange(*strips) for strips in sends]
    common = (table, coefficients, parts_h, vectors)

    terms, older, inner, core_sends = ([None] * chunks for _ in range(4))
    core = rims = ends = near = None
    wide, before = None, [None] * chunks

    def swapped(x, distance):
        return lax.ppermute(x, "vecs", [(i, i ^ distance) for i in range(groups)])

    def received(sends):
        return {d: swapped(sends[d.bit_length() - 2], d) for d in range(2, groups, 2)}

    def forwarded(got):
        out = {}
        for d, rows in got.items():
            out[d], out[d + 1] = rows, swapped(rows, 1)
        return out

    def inside(step, c):
        nonlocal core, rims, near
        q = older[c] and older[c][1]
        if step < ORDER - 1:
            inner[c] = interior(step, c, shape, chain, common, parts[c], q)
        elif step == ORDER - 1:
            inner[c], core, core_sends[c] = core_rows(ORDER, c, shape, chain, common, parts[c], q, terms[c][1], core)
        else:
            near, rims = ring(step, c, shape, chain, common, parts[c], q, core[1] if near is None else near, rims)

    for step in range(1, ORDER):
        for c in range(chunks):
            inside(step, c)
            q = older[c] and (older[c][0], older[c][2])
            late = step == ORDER - 1
            spare = (chunks - 1 - c) * EARLY
            low, high, following = border(
                step, c, shape, chain, common, halo[c], q, parts[c], inner[c][1], (wide, spare) if late else ()
            )
            if late:
                wide, before[c] = low, lax.ppermute(high, "rows", up)
            else:
                halo[c] = exchange(low, high)
            older[c], terms[c], parts[c] = terms[c], (low, inner[c][0], high), following
    after = lax.ppermute(wide, "rows", down)
    got_core = [received(sends) for sends in core_sends]
    for c in range(chunks):
        inside(ORDER, c)
    got_rims = received(rims[1:])
    diagonal = gram_sums(shape, chain, table, (0,), [core[0], rims[0]], {}, None, 0)
    for c in range(chunks):
        q = (older[c][0], older[c][2])
        got = [[rows[d] for rows in got_core] for d in range(2, groups, 2)] if c == 0 else []
        ends, joined = last_border(ORDER, c, shape, chain, common, (before[c], after), q, parts[c], ends, got)
        if c == 0:
            all_core = {2 * n + 2: rows for n, rows in enumerate(joined)}
    near, *rows = take_in(chain, [near, *got_rims.values()])
    got_core = forwarded(all_core)
    got_rims = forwarded(dict(zip(got_rims, rows)))
    got_ends = received(ends[2:])

    kinds, far = tuple(range(min(2, groups))), tuple(range(2, groups))
    swaps = [[(i, i ^ (1 << level)) for i in range(peers)] for level in range(levels)]
    near, near_ends = swapped(near, 1), swapped(ends[1], 1)
    last = block_rows * BLOCK - SIZE
    result = [(core[0], 0, core[0].shape[0], 2 * SIZE), (rims[0], 0, SIZE, SIZE), (rims[0], SIZE, SIZE, last - SIZE)]
    result += [(ends[0], 0, SIZE, 0), (ends[0], SIZE, SIZE, last)]
    arrived = {1: [([near], 0), ([near], core[0].shape[0] // 2), ([near_ends], 0)]}
    whole = [] if far else result
    keep, send, *rest = gram_sums(shape, chain, table, kinds, [core[0], rims[0], ends[0]], arrived, diagonal, piece, whole, done=2)
    shares = [(keep, lax.ppermute(send, "rows", swaps[0]))]
    if far:
        arrived = {d: [([got_core[d]], 0), ([got_rims[d]], 0)] for d in far}
        sums, *rest = gram_sums(shape, chain, table, far, [core[0], rims[0]], arrived, None, 0, result)
        keep, send, *rows = fold(shape, chain, table, 1, shares, got_ends.values())
        shares = [(keep, lax.ppermute(send, "rows", swaps[1]))]
        got_ends = forwarded(dict(zip(got_ends, rows)))
        arrived = {d: [([got_ends[d]], 0)] for d in far}
        both = per_group == 2 and levels > 2
        made = gram_sums(shape, chain, table, far, [ends[0]], arrived, sums, piece, (), both)
        if both:
            upper = (made[0], lax.ppermute(made[1], "rows", swaps[0]))
            lower = (made[2], lax.ppermute(made[3], "rows", swaps[1]))
            made = fold_two(shape, chain, table, upper, lower)
            shares.append(
                (made[0], lax.ppermute(made[1], "rows", swaps[1]), made[2], lax.ppermute(made[3], "rows", swaps[0]))
            )
        else:
            shares.append((made[0], lax.ppermute(made[1], "rows", swaps[0])))
    filtered = rest[0]

    for level in range(1, levels - 1):
        ahead = [pair for n, pair in enumerate(shares) if level == 1 and len(shares) > 1 and (n == 0 or len(pair) > 2)]
        if len(ahead) == len(shares):
            continue
        joined = [shares] if shares[0][0].shape[0] == 1 and not ahead else [[pair] for pair in shares[len(ahead) :]]
        folded = [fold(shape, chain, table, level, pairs) for pairs in joined]
        shares = ahead + [(keep, lax.ppermute(send, "rows", swaps[level])) for keep, send in folded]

    keep, send = fold(shape, chain, table, levels - 1, shares)
    share, *tiles = add_blocks(chain, table, keep, lax.ppermute(send, "rows", swaps[-1]), per_group)
    turned = []
    for n in range(per_group):
        pairs = []
        for i in range(peers):
            for g in range(groups):
                to = (g * per_group + (i + n) % per_group) * groups + i // per_group
                pairs.append((i * groups + g, to))
        turned.append(lax.ppermute(tiles[n], ("rows", "vecs"), pairs))
    gram = assemble(chain, table, share, turned, 1.0 / (total_blocks * BLOCK))
    return filtered, gram


def solution(mesh):
    return jax.shard_map(
        on_device,
        mesh=mesh,
        in_specs=(P("rows", None, None, None), P("rows", None), P("rows", "vecs"), P()),
        out_specs=(P("rows", "vecs"), P("vecs", "rows")),
        check_vma=False,
    )
```
